32 devices in a mesh: tile: 16 (over z, y, core), layer: 2 (over x).
Axes of the slice: x: 2, y: 2, z: 4, core: 2. Of those that a mesh axis runs over, the one named last changes fastest.
Arguments:
- ensemble: float32 [64, 8, 8192], P(None, 'layer', 'tile'), may hold values from -6 to 6
- diff_x: float32 [8, 8192], P('layer', 'tile'), may hold values from 0.04 to 0.2
- diff_z: float32 [8, 8192], P('layer', 'tile'), may hold values from 0.04 to 0.2
- cour_x: float32 [8, 8192], P('layer', 'tile'), may hold values from -0.4 to 0.4
- cour_z: float32 [8, 8192], P('layer', 'tile'), may hold values from -0.4 to 0.4
- obs_cell: int32 [4, 512], replicated, may hold values from 0 to 65535
- obs_radius: int32 [4, 512], replicated, may hold values from 2048 to 8192
- obs_value: float32 [4, 512], replicated, may hold values from -6 to 6
- obs_var: float32 [4, 512], replicated, may hold values from 0.1 to 1
Outputs:
- posterior: float32 [64, 8, 8192], P(None, 'layer', 'tile')
The draws below stay inside these ranges and needn't reach their ends.
Inputs may be any that keep to these rules, and one draw needn't show every extreme that they name: `obs_cell`: cells are drawn independently over the whole grid; two observations may share a cell.
All inputs are finite; a program needn't handle non-finite values.
Results may differ from the reference program's by a relative error of at most 0.00019.
Values sent between devices are 32-bit elements; how exact they have to be, the bound alone decides.
A program may use at most 64 MiB of HBM per device.

```python
import math
import jax
import jax.numpy as jnp
from jax import lax

MEMBERS = 64
NB = 4
NOBS = 512
NL = 8
NH = 8192


def place_ends(values, rng, low, high):
    longest = values.shape.index(max(values.shape))
    spots = []
    for shift in (0, 1):
        where = [jax.random.randint(jax.random.fold_in(rng, axis), (), 0, length) for axis, length in enumerate(values.shape)]
        where[longest] = (where[longest] + shift) % values.shape[longest]
        spots.append(tuple(where))
    return values.at[spots[0]].set(low).at[spots[1]].set(high)


def level_of(key, extent, pieces, smallest, top_value):
    def one(position, blocks):
        heights = jax.random.uniform(jax.random.fold_in(jax.random.fold_in(key, 6), position), (blocks,), jnp.float32, smallest / len(pieces), top_value / len(pieces))
        return jnp.repeat(jnp.exp(heights), extent[position] // blocks).reshape((-1,) + (1,) * (len(extent) - position - 1))

    loudness = one(*pieces[0])
    for cut in pieces[1:]:
        loudness = loudness * one(*cut)
    return loudness


def normal_values(rng, dims, width, bound, shards=(), kind=jnp.bfloat16):
    entries = jax.random.normal(rng, dims, jnp.float32) * width
    if len(shards) > 0:
        entries = level_of(rng, dims, shards, -0.22, 0.18) * entries
    return jnp.clip(entries, min=-bound, max=bound).astype(kind)


def setup_inputs(seed: int = 0) -> dict:
    keys = jax.random.split(jax.random.key(seed), 10)
    ensemble = normal_values(keys[0], (MEMBERS, NL, NH), 1.0, 6.0, ((1, 2), (2, 16)), jnp.float32)
    diff_x = jnp.clip(jnp.exp(math.log(0.2) - 1.609438 * jax.random.uniform(keys[1], (NL, NH), jnp.float32) ** level_of(keys[1], (NL, NH), ((0, 2), (1, 16)), -0.2, 0.2)), 0.04, 0.2)
    diff_z = jnp.clip(jnp.exp(math.log(0.2) - 1.609438 * jax.random.uniform(keys[2], (NL, NH), jnp.float32) ** level_of(keys[2], (NL, NH), ((0, 2), (1, 16)), -0.2, 0.2)), 0.04, 0.2)
    cour_x = jnp.clip(jax.random.uniform(keys[3], (NL, NH), jnp.float32, -0.4, 0.4) * level_of(keys[3], (NL, NH), ((0, 2), (1, 16)), -0.4, 0.0), -0.4, 0.4)
    cour_z = jnp.clip(jax.random.uniform(keys[4], (NL, NH), jnp.float32, -0.4, 0.4) * level_of(keys[4], (NL, NH), ((0, 2), (1, 16)), -0.4, 0.0), -0.4, 0.4)
    obs_cell = place_ends(jax.random.randint(keys[5], (NB, NOBS), 0, NL * NH), jax.random.fold_in(keys[5], 1), 0, (NL * NH) - 1).astype(jnp.int32)
    obs_radius = place_ends(jax.random.randint(keys[6], (NB, NOBS), NH // 4, NH + 1), jax.random.fold_in(keys[6], 1), NH // 4, NH).astype(jnp.int32)
    obs_value = normal_values(keys[7], (NB, NOBS), 1.0, 6.0, (), jnp.float32)
    obs_var = jnp.clip(jnp.exp(jax.random.uniform(keys[8], (NB, NOBS), jnp.float32, math.log(0.1), math.log(1.0))), 0.1, 1.0)
    return dict(ensemble=ensemble, diff_x=diff_x, diff_z=diff_z, cour_x=cour_x, cour_z=cour_z, obs_cell=obs_cell, obs_radius=obs_radius, obs_value=obs_value, obs_var=obs_var)


def advect(ensemble, diff_x, diff_z, cour_x, cour_z):
    padded = jnp.pad(ensemble, ((0, 0), (1, 1), (1, 1)))
    centre = padded[:, 1:-1, 1:-1]
    upper = padded[:, :-2, 1:-1]
    lower = padded[:, 2:, 1:-1]
    west = padded[:, 1:-1, :-2]
    east = padded[:, 1:-1, 2:]
    return centre + diff_z * (upper - 2.0 * centre + lower) + diff_x * (west - 2.0 * centre + east) - 0.5 * cour_z * (lower - upper) - 0.5 * cour_x * (east - west)

def increments(prior, value, variance):
    members = prior.shape[1]
    ymean = lax.optimization_barrier(jnp.mean(prior, axis=1))
    anomaly = prior - ymean[:, None]
    spread = lax.optimization_barrier(jnp.sum(anomaly * anomaly, axis=1)) / (members - 1) + 1e-06
    shrink = variance / (spread + variance)
    postmean = spread * shrink * (ymean / spread + value / variance)
    delta = (postmean - ymean)[:, None] + (jnp.sqrt(shrink) - 1.0)[:, None] * anomaly
    factor = 1.0 / ((members - 1) * spread)
    return (anomaly, delta, factor)

def taper(positions, centres, radius):
    dist = jnp.abs(positions[None, :] - centres[:, None]).astype(jnp.float32)
    frac = jnp.maximum(1.0 - dist / radius[:, None].astype(jnp.float32), 0.0)
    return frac * frac

def reference(ensemble, diff_x, diff_z, cour_x, cour_z, obs_cell, obs_radius, obs_value, obs_var):
    state = advect(ensemble, diff_x, diff_z, cour_x, cour_z)
    positions = jnp.arange(NH, dtype=jnp.int32)
    for batch in range(NB):
        cells = obs_cell[batch]
        flat = state.reshape(MEMBERS, NL * NH)
        prior = jnp.take(flat, cells, axis=1).T
        anomaly, delta, factor = increments(prior, obs_value[batch], obs_var[batch])
        weight = taper(positions, cells % NH, obs_radius[batch]) * factor[:, None]
        xmean = lax.optimization_barrier(jnp.mean(state, axis=0))
        layered = jnp.transpose(state - xmean[None], (1, 0, 2))

        def one_layer(level):
            cov = jnp.dot(anomaly, level, precision=lax.Precision.HIGHEST)
            return jnp.dot(delta.T, cov * weight, precision=lax.Precision.HIGHEST)
        change = lax.map(one_layer, layered)
        state = state + jnp.transpose(change, (1, 0, 2))
    return state
```

```python
import functools

import jax
import jax.numpy as jnp
from jax import lax
from jax.experimental import pallas as pl
from jax.experimental.pallas import tpu as pltpu
from jax.sharding import PartitionSpec as P

MESH = pl.DeviceIdType.MESH
LANES = 128


def split_cell(cells, total):
    if total & (total - 1) == 0:
        return cells >> (total.bit_length() - 1), cells & (total - 1)
    return cells // total, cells % total


def halves(value):
    high = value.astype(jnp.bfloat16)
    return high, (value - high.astype(jnp.float32)).astype(jnp.bfloat16)


def gather_kernel(
    tiles, layers, ens_in, dx_in, dz_in, cx_in, cz_in, cell_in, state_out, prior,
    state, state_sem, ens, diff_x, diff_z, cour_x, cour_z, obs_cell, load_sem,
    cells, edge_w, edge_e, halo_w, halo_e, halo_u, halo_d, coef_up, coef_down, coef_u, coef_d,
    part, in_core, in_plane, in_line, halo_send, halo_recv, core_sem, plane_send, plane_recv, line_send, line_recv,
):
    loads = []
    for i, (src, dst) in enumerate(
        ((ens_in, ens), (dz_in, diff_z), (cz_in, cour_z), (dx_in, diff_x), (cx_in, cour_x), (cell_in, obs_cell))
    ):
        copy = pltpu.make_async_copy(src, dst, load_sem.at[i])
        copy.start()
        loads.append(copy)
    members, depth, width = ens.shape
    batches, count = obs_cell.shape
    tile, layer = lax.axis_index("tile"), lax.axis_index("layer")
    core, row, line = tile % 2, (tile // 2) % 2, tile // 4
    plane_n, line_n = layers * 2, tiles // 4
    spot = layer * 2 + row
    pair = (tile + 1 - 2 * core, layer)

    def plane_at(index):
        return (line * 4 + (index % 2) * 2 + core, index // 2)

    def line_at(index):
        return (index * 4 + row * 2 + core, layer)

    greeted = [pair, ((tile + 1) % tiles, layer), ((tile + tiles - 1) % tiles, layer)]
    greeted += [(tile, (layer + 1) % layers), (tile, (layer + layers - 1) % layers)]
    greeted += [plane_at((spot + j) % plane_n) for j in range(1, plane_n)]
    greeted += [line_at((line + j) % line_n) for j in range(1, line_n)]
    barrier = pltpu.get_barrier_semaphore()
    for device in greeted:
        pl.semaphore_signal(barrier, inc=1, device_id=device, device_id_type=MESH)

    for copy in loads:
        copy.wait()
    lane = lax.broadcasted_iota(jnp.int32, (members, LANES), 1)
    west = jnp.zeros((members, LANES), jnp.float32)
    east = jnp.zeros((members, LANES), jnp.float32)
    for l in range(depth):
        x = ens[:, l, :]
        cells[l] = x
        west = jnp.where(lane == l, x[:, 0:1], west)
        east = jnp.where(lane == l, x[:, width - 1 : width], east)
    edge_w[...] = west
    edge_e[...] = east
    tall = coef_up.shape
    coef_up[...] = jnp.broadcast_to(diff_z[0:1, :] + 0.5 * cour_z[0:1, :], tall)
    coef_down[...] = jnp.broadcast_to(diff_z[depth - 1 : depth, :] - 0.5 * cour_z[depth - 1 : depth, :], tall)
    pl.semaphore_wait(barrier, len(greeted))

    def remote(src, dst, send, recv, device):
        return pltpu.make_async_remote_copy(
            src_ref=src, dst_ref=dst, send_sem=send, recv_sem=recv, device_id=device, device_id_type=MESH
        )

    up, down = layer > 0, layer < layers - 1
    before, after = tile > 0, tile < tiles - 1
    above, below = (tile, lax.rem(layer + layers - 1, layers)), (tile, lax.rem(layer + 1, layers))
    ahead, behind = (lax.rem(tile + 1, tiles), layer), (lax.rem(tile + tiles - 1, tiles), layer)

    def move(i, sends, receives, src, dst, device):
        return sends, receives, remote(src, dst, halo_send.at[i], halo_recv.at[i], device), dst

    small = (
        move(0, after, before, edge_e, halo_w, ahead),
        move(1, before, after, edge_w, halo_e, behind),
        move(2, down, up, coef_down, coef_u, below),
        move(3, up, down, coef_up, coef_d, above),
    )
    large = (
        move(4, down, up, cells.at[depth - 1], halo_u, below),
        move(5, up, down, cells.at[0], halo_d, above),
    )
    for sends, receives, copy, place in small:
        pl.when(sends)(copy.start)
    for sends, receives, copy, place in small + large:

        @pl.when(jnp.logical_not(receives))
        def _(place=place):
            place[...] = jnp.zeros_like(place)

    for sends, receives, copy, place in small:
        pl.when(receives)(copy.wait_recv)

    column = lax.broadcasted_iota(jnp.int32, (members, width), 1)
    levels = list(range(depth)) + [-1, depth]
    parts = []
    for l in range(depth):
        x = cells[l]
        left = jnp.where(column == 0, halo_w[:, l : l + 1], pltpu.roll(x, 1, 1))
        right = jnp.where(column == width - 1, halo_e[:, l : l + 1], pltpu.roll(x, width - 1, 1))
        dx, dz = diff_x[l : l + 1, :], diff_z[l : l + 1, :]
        cx, cz = 0.5 * cour_x[l : l + 1, :], 0.5 * cour_z[l : l + 1, :]
        new = x * (1.0 - 2.0 * dz - 2.0 * dx) + left * (dx + cx) + right * (dx - cx)
        if l > 0:
            new = new + cells[l - 1] * (dz + cz)
        if l < depth - 1:
            new = new + cells[l + 1] * (dz - cz)
        state[l] = new
        parts.extend(halves(new))
    parts.extend(halves(cells[0] * coef_u[0:1, :]))
    parts.extend(halves(cells[depth - 1] * coef_d[0:1, :]))
    stacked = jnp.concatenate(parts, axis=0)

    blocks = count // LANES
    extent = blocks * members
    half = extent // 2
    size = half // plane_n
    scatter = size % (8 * line_n) == 0
    piece = size // line_n if scatter else size
    place = lax.broadcasted_iota(jnp.int32, (width, count), 0)

    def start_of(b, *steps):
        total = b * extent
        for index, length in steps:
            total = total + index * length
        return pl.multiple_of(total, 8)

    every = range(batches)
    core_out, plane_out, line_out, line_back, plane_back, core_back = ([[] for _ in every] for _ in range(6))
    for b in every:
        rows, cols = split_cell(obs_cell[b : b + 1, :], tiles * width)
        rows, cols = rows - layer * depth, cols - tile * width
        hot = jnp.where(place == cols, 1.0, 0.0).astype(jnp.bfloat16)
        picked = jnp.dot(stacked, hot, preferred_element_type=jnp.float32)
        total = jnp.zeros((members, count), jnp.float32)
        for i, l in enumerate(levels):
            both = picked[2 * i * members : (2 * i + 1) * members] + picked[(2 * i + 1) * members : (2 * i + 2) * members]
            total = jnp.where(rows == l, both, total)
        for k in range(blocks):
            part[pl.ds((b * blocks + k) * members, members), :] = total[:, k * LANES : (k + 1) * LANES]
        copy = remote(part.at[pl.ds(start_of(b, (1 - core, half)), half)], in_core.at[b], core_sem.at[b, 0], core_sem.at[b, 1], pair)
        copy.start()
        core_out[b].append(copy)

    for b in every:
        core_out[b][0].wait_recv()
        part[pl.ds(start_of(b, (core, half)), half), :] += in_core[b]
        for j in range(1, plane_n):
            to = (spot + j) % plane_n
            copy = remote(
                part.at[pl.ds(start_of(b, (core, half), (to, size)), size)], in_plane.at[b, j - 1],
                plane_send.at[b, j - 1], plane_recv.at[b, j - 1], plane_at(to),
            )
            copy.start()
            plane_out[b].append(copy)
    for b in every:
        base = start_of(b, (core, half), (spot, size))
        total = part[pl.ds(base, size), :]
        for j in range(1, plane_n):
            plane_out[b][j - 1].wait_recv()
            total = total + in_plane[b, j - 1]
        part[pl.ds(base, size), :] = total
        for j in range(1, line_n):
            to = (line + j) % line_n
            start = start_of(b, (core, half), (spot, size), (to, piece)) if scatter else base
            copy = remote(part.at[pl.ds(start, piece)], in_line.at[b, j - 1], line_send.at[b, j - 1], line_recv.at[b, j - 1], line_at(to))
            copy.start()
            line_out[b].append(copy)
    for sends, receives, copy, _ in large:
        pl.when(sends)(copy.start)

    def spread_plane(b):
        view = prior.at[pl.ds(start_of(b, (core, half), (spot, size)), size)]
        for j in range(1, plane_n):
            k = plane_n - 1 + j - 1
            copy = remote(view, view, plane_send.at[b, k], plane_recv.at[b, k], plane_at((spot + j) % plane_n))
            copy.start()
            plane_back[b].append(copy)

    for b in every:
        own = start_of(b, (core, half), (spot, size), (line, piece)) if scatter else start_of(b, (core, half), (spot, size))
        total = part[pl.ds(own, piece), :]
        for j in range(1, line_n):
            line_out[b][j - 1].wait_recv()
            total = total + in_line[b, j - 1]
        prior[pl.ds(own, piece), :] = total
        if scatter:
            view = prior.at[pl.ds(own, piece)]
            for j in range(1, line_n):
                k = line_n - 1 + j - 1
                copy = remote(view, view, line_send.at[b, k], line_recv.at[b, k], line_at((line + j) % line_n))
                copy.start()
                line_back[b].append(copy)
        else:
            spread_plane(b)
    if scatter:
        for b in every:
            for copy in line_back[b]:
                copy.wait_recv()
            spread_plane(b)

    for sends, receives, copy, _ in large:
        pl.when(receives)(copy.wait_recv)
    state[0] += halo_u[...] * (diff_z[0:1, :] + 0.5 * cour_z[0:1, :])
    state[depth - 1] += halo_d[...] * (diff_z[depth - 1 : depth, :] - 0.5 * cour_z[depth - 1 : depth, :])
    keep = pltpu.make_async_copy(state, state_out, state_sem)
    keep.start()

    for b in every:
        for copy in plane_back[b]:
            copy.wait_recv()
        view = prior.at[pl.ds(start_of(b, (core, half)), half)]
        copy = remote(view, view, core_sem.at[b, 2], core_sem.at[b, 3], pair)
        copy.start()
        core_back[b].append(copy)
    for b in every:
        core_back[b][0].wait_recv()
    for group in (core_out, plane_out, line_out, line_back, plane_back, core_back):
        for copies in group:
            for copy in copies:
                copy.wait_send()
    for sends, receives, copy, _ in small + large:
        pl.when(sends)(copy.wait_send)
    keep.wait()


def update_kernel(
    total_cols, width, state_in, prior_in, cell_in, radius_in, value_in, var_in, out,
    layers_ref, later_ref, prior, obs_cell, obs_radius, obs_value, obs_var, load_sem,
):
    loads = []
    for i, (src, dst) in enumerate(
        (
            (cell_in, obs_cell), (radius_in, obs_radius), (value_in, obs_value), (var_in, obs_var),
            (prior_in, prior), (state_in, layers_ref),
        )
    ):
        copy = pltpu.make_async_copy(src, dst, load_sem.at[i])
        copy.start()
        loads.append(copy)
    depth, members, _ = layers_ref.shape
    batches, count = obs_cell.shape
    blocks = count // LANES
    first = lax.axis_index("tile") * width
    for copy in loads[:-1]:
        copy.wait()
    for b in range(batches):
        for k in range(blocks):
            later_ref[b, :, k * LANES : (k + 1) * LANES] = prior[pl.ds((b * blocks + k) * members, members), :]
    centre = split_cell(obs_cell[...], total_cols)[1].astype(jnp.float32)
    inverse = 1.0 / obs_radius[...].astype(jnp.float32)
    upright = jnp.concatenate([centre, inverse], axis=0).T
    grid = (first + lax.broadcasted_iota(jnp.int32, (1, width), 1)).astype(jnp.float32)

    for b in range(batches):
        y = later_ref[b]
        value, variance = obs_value[b : b + 1, :], obs_var[b : b + 1, :]
        ymean = jnp.sum(y, axis=0, keepdims=True) * (1.0 / members)
        anomaly = y - ymean
        spread = jnp.sum(anomaly * anomaly, axis=0, keepdims=True) / (members - 1) + 1e-06
        shrink = variance / (spread + variance)
        postmean = spread * shrink * (ymean / spread + value / variance)
        delta = (postmean - ymean) + (jnp.sqrt(shrink) - 1.0) * anomaly
        delta = delta * (1.0 / ((members - 1) * spread))
        d_high, d_low = halves(delta)
        d_both = jnp.concatenate([d_high, d_low], axis=0)
        y_high = anomaly.astype(jnp.bfloat16).astype(jnp.float32)
        y_low = anomaly - y_high
        lhs = jnp.concatenate([y_high, y_high, y_low, y_low], axis=0).T.astype(jnp.bfloat16)
        here, scale = upright[:, b : b + 1], upright[:, batches + b : batches + b + 1]

        def taper(positions):
            frac = jnp.maximum(1.0 - jnp.abs(positions - here) * scale, 0.0)
            return frac * frac

        def change(x, weight):
            x_high, x_low = halves(x - jnp.sum(x, axis=0, keepdims=True) * (1.0 / members))
            rhs = jnp.concatenate([x_high, x_low, x_high, x_low], axis=0)
            gain = jnp.dot(lhs, rhs, preferred_element_type=jnp.float32) * weight
            g_high, g_low = halves(gain)
            one = jnp.dot(d_both, g_high, preferred_element_type=jnp.float32)
            two = jnp.dot(d_high, g_low, preferred_element_type=jnp.float32)
            return one[:members] + one[members:] + two

        for c in range(b + 1, batches):
            later_ref[c] += change(later_ref[c], taper(centre[c : c + 1, :]))
        weight = taper(grid)
        if b == 0:
            loads[-1].wait()
        for l in range(depth):
            x = layers_ref[l]
            x = x + change(x, weight)
            if b == batches - 1:
                out[:, l, :] = x
            else:
                layers_ref[l] = x


def divide(values, size):
    return values >> (size.bit_length() - 1) if size & (size - 1) == 0 else values // size


def dot_rows(a, b):
    return lax.dot_general(a, b, (((1,), (1,)), ((), ())), preferred_element_type=jnp.float32)


def remote(src, dst, send, recv, device):
    return pltpu.make_async_remote_copy(
        src_ref=src, dst_ref=dst, send_sem=send, recv_sem=recv, device_id=device, device_id_type=MESH
    )


def collect_kernel(
    tiles, layers, cap, ens_in, dx_in, dz_in, cx_in, cz_in, cell_in, radius_in, value_in, var_in,
    state_out, gathered, meta, table, flag,
    state, state_sem, ens, diff_x, diff_z, cour_x, cour_z, obs_cell, obs_radius, obs_value, obs_var, load_sem,
    cells, edge_w, edge_e, halo_w, halo_e, near_u, near_d, part_u, part_d, halo_u, halo_d,
    hop_send, hop_recv, line_send, line_recv, plane_send, plane_recv, core_send, core_recv,
):
    loads = []
    for i, (src, dst) in enumerate(
        (
            (cell_in, obs_cell), (ens_in, ens), (dz_in, diff_z), (cz_in, cour_z), (dx_in, diff_x), (cx_in, cour_x),
            (radius_in, obs_radius), (value_in, obs_value), (var_in, obs_var),
        )
    ):
        copy = pltpu.make_async_copy(src, dst, load_sem.at[i])
        copy.start()
        loads.append(copy)
    members, depth, width = ens.shape
    batches, count = obs_cell.shape
    chunks, devices, piece, _ = gathered.shape
    f32, bf16 = jnp.float32, jnp.bfloat16
    tile, layer = lax.axis_index("tile"), lax.axis_index("layer")
    core, row, line = tile % 2, (tile // 2) % 2, tile // 4
    plane_n, line_n = layers * 2, tiles // 4
    spot = layer * 2 + row
    pair = (tile + 1 - 2 * core, layer)

    def plane_at(index):
        return (line * 4 + (index % 2) * 2 + core, index // 2)

    def line_at(index):
        return (index * 4 + row * 2 + core, layer)

    above, below = (tile, lax.rem(layer + layers - 1, layers)), (tile, lax.rem(layer + 1, layers))
    ahead, behind = (lax.rem(tile + 1, tiles), layer), (lax.rem(tile + tiles - 1, tiles), layer)
    greeted = [pair, ahead, behind, below, above]
    greeted += [plane_at((spot + j) % plane_n) for j in range(1, plane_n)]
    greeted += [line_at((line + j) % line_n) for j in range(1, line_n)]
    barrier = pltpu.get_barrier_semaphore()
    for device in greeted:
        pl.semaphore_signal(barrier, inc=1, device_id=device, device_id_type=MESH)

    loads[0].wait()
    cell_row, cell_col = split_cell(obs_cell[...], tiles * width)
    cell_tile, cell_layer = divide(cell_col, width), divide(cell_row, depth)
    local_col, local_row = cell_col - cell_tile * width, cell_row - cell_layer * depth
    here = cell_tile == tile
    groups = [
        jnp.where(jnp.logical_and(here, cell_layer == layer + step), 1.0, 0.0) for step in (0, -1, 1)
    ]
    masks = jnp.concatenate(groups + [jnp.zeros_like(groups[0])], axis=0).astype(bf16)
    first = lax.broadcasted_iota(jnp.int32, (count, count), 0)
    second = lax.broadcasted_iota(jnp.int32, (count, count), 1)
    running = jnp.dot(masks, jnp.where(first <= second, 1.0, 0.0).astype(bf16), preferred_element_type=f32)
    code = (local_row * width + local_col + 1).astype(f32)
    slot = lax.broadcasted_iota(jnp.int32, (cap, count), 0).astype(f32)
    lane_w = lax.broadcasted_iota(jnp.int32, (cap, width), 1)
    found = []
    for k, edge in enumerate((None, depth - 1, 0)):
        before_ = jnp.zeros((1, 1), f32)
        total = jnp.zeros((cap, count), f32)
        for b in range(batches):
            i = k * batches + b
            wanted = groups[k][b : b + 1, :] > 0.5
            if edge is not None:
                wanted = jnp.logical_and(wanted, local_row[b : b + 1, :] == edge)
            rank = jnp.where(wanted, running[i : i + 1, :] + (before_ - 1.0), -1.0)
            total = total + jnp.where(rank == slot, code[b : b + 1, :], 0.0)
            before_ = before_ + running[i : i + 1, count - 1 : count]
        cell = jnp.sum(total, axis=1, keepdims=True).astype(jnp.int32) - 1
        at_row = divide(cell, width)
        at_col = jnp.where(cell >= 0, cell - at_row * width, -1)
        found.append((at_row, at_col, jnp.where(lane_w == at_col, 1.0, 0.0)))

    low = lax.broadcasted_iota(jnp.int32, (piece, LANES), 1) < members

    def packed(values):
        out = []
        for k in range(chunks):
            base = 2 * piece * k
            out.append(jnp.where(low, values[base : base + piece], values[base + piece : base + 2 * piece]))
        return out

    def doubled(values):
        return values + pltpu.roll(values, members, 1)

    for copy in loads[1:6]:
        copy.wait()
    lane = lax.broadcasted_iota(jnp.int32, (members, LANES), 1)
    west = jnp.zeros((members, LANES), f32)
    east = jnp.zeros((members, LANES), f32)
    for l in range(depth):
        x = ens[:, l, :]
        cells[l] = x
        west = jnp.where(lane == l, x[:, 0:1], west)
        east = jnp.where(lane == l, x[:, width - 1 : width], east)
    edge_w[...] = jnp.concatenate([west, west], axis=0).T[:8]
    edge_e[...] = jnp.concatenate([east, east], axis=0).T[:8]
    for ref, k, l in ((part_u, 1, 0), (part_d, 2, depth - 1)):
        raw = jnp.concatenate(halves(cells[l]), axis=0)
        for i, rows in enumerate(packed(doubled(dot_rows(found[k][2].astype(bf16), raw)))):
            ref[i * piece : (i + 1) * piece, :] = rows
    pl.semaphore_wait(barrier, len(greeted))

    up, down = layer > 0, layer < layers - 1
    before, after = tile > 0, tile < tiles - 1

    def move(i, sends, receives, src, dst, device):
        return sends, receives, remote(src, dst, hop_send.at[i], hop_recv.at[i], device), dst

    small = (
        move(0, down, up, part_d, near_u, below),
        move(1, up, down, part_u, near_d, above),
        move(2, after, before, edge_e, halo_w, ahead),
        move(3, before, after, edge_w, halo_e, behind),
    )
    large = (
        move(4, down, up, cells.at[depth - 1], halo_u, below),
        move(5, up, down, cells.at[0], halo_d, above),
    )
    for sends, receives, copy, place in small:
        pl.when(sends)(copy.start)
    for sends, receives, copy, place in small + large:

        @pl.when(jnp.logical_not(receives))
        def _(place=place):
            place[...] = jnp.zeros_like(place)

    at_row, at_col, hot = found[0]
    column = lax.broadcasted_iota(jnp.int32, (members, width), 1)
    total = jnp.zeros((cap, LANES), f32)
    for l in range(depth):
        x = cells[l]
        left = jnp.where(column == 0, 0.0, pltpu.roll(x, 1, 1))
        right = jnp.where(column == width - 1, 0.0, pltpu.roll(x, width - 1, 1))
        dx, dz = diff_x[l : l + 1, :], diff_z[l : l + 1, :]
        cx, cz = 0.5 * cour_x[l : l + 1, :], 0.5 * cour_z[l : l + 1, :]
        new = x * (1.0 - 2.0 * dz - 2.0 * dx) + left * (dx + cx) + right * (dx - cx)
        if l > 0:
            new = new + cells[l - 1] * (dz + cz)
        if l < depth - 1:
            new = new + cells[l + 1] * (dz - cz)
        state[l] = new
        picked = dot_rows(hot.astype(bf16), jnp.concatenate(halves(new), axis=0))
        total = total + jnp.where(at_row == l, picked, 0.0)
    mine = packed(doubled(total))
    coef_u = diff_z[0:1, :] + 0.5 * cour_z[0:1, :]
    coef_d = diff_z[depth - 1 : depth, :] - 0.5 * cour_z[depth - 1 : depth, :]
    take_u = jnp.where(at_row == 0, jnp.sum(hot * coef_u, axis=1, keepdims=True), 0.0)
    take_d = jnp.where(at_row == depth - 1, jnp.sum(hot * coef_d, axis=1, keepdims=True), 0.0)
    coef_w = diff_x[:, 0:1] + 0.5 * cour_x[:, 0:1]
    coef_e = diff_x[:, width - 1 : width] - 0.5 * cour_x[:, width - 1 : width]
    weights = [packed(jnp.broadcast_to(take, (cap, LANES))) for take in (take_u, take_d)]
    sides = []
    for at, coef in ((0, coef_w), (width - 1, coef_e)):
        for l in range(depth):
            take = jnp.where(jnp.logical_and(at_row == l, at_col == at), coef[l : l + 1, :], 0.0)
            sides.append(packed(jnp.broadcast_to(take, (cap, LANES))))

    for sends, receives, copy, place in small:
        pl.when(receives)(copy.wait_recv)
    me = (core * plane_n + spot) * line_n + line
    line_out, plane_out, core_out = ([[] for _ in range(chunks)] for _ in range(3))
    for k in range(chunks):
        rows = pl.ds(k * piece, piece)
        value = mine[k] + weights[0][k] * near_u[rows, :] + weights[1][k] * near_d[rows, :]
        for l in range(depth):
            value = value + sides[l][k] * halo_w[l : l + 1, :] + sides[depth + l][k] * halo_e[l : l + 1, :]
        gathered[k, me] = value
        view = gathered.at[k, me]
        for j in range(1, line_n):
            copy = remote(view, view, line_send.at[k, j - 1], line_recv.at[k, j - 1], line_at((line + j) % line_n))
            copy.start()
            line_out[k].append(copy)
    for sends, receives, copy, _ in large:
        pl.when(sends)(copy.start)

    for ref, coef, at in ((halo_w, coef_w, 0), (halo_e, coef_e, width - 1)):
        base = at // LANES * LANES
        block = lax.broadcasted_iota(jnp.int32, (members, LANES), 1)
        turned = jnp.concatenate([ref[...]] * (LANES // 8), axis=0).T[:members]
        for l in range(depth):
            term = turned[:, l : l + 1] * coef[l : l + 1, :]
            state[l, :, base : base + LANES] += jnp.where(block == at - base, term, 0.0)

    for copy in loads[6:]:
        copy.wait()
    core_of, row_of, line_of = cell_tile & 1, divide(cell_tile, 2) & 1, divide(cell_tile, 4)
    owner = (core_of * plane_n + cell_layer * 2 + row_of) * line_n + line_of
    key = (owner * count + lax.broadcasted_iota(jnp.int32, (batches, count), 1)).astype(f32)
    both = jnp.concatenate([key, owner.astype(f32)], axis=0)
    if 2 * batches % 8:
        both = jnp.concatenate([both, jnp.zeros((8 - 2 * batches % 8, count), f32)], axis=0)
    upright = both.T

    def pieces(values, n):
        out = []
        for _ in range(n):
            high = values.astype(bf16).astype(f32)
            out.append(high)
            values = values - high
        return out

    fields = (
        (cell_col.astype(f32), 2), (obs_radius[...].astype(f32), 2), (obs_value[...], 3), (obs_var[...], 3)
    )
    parts = []
    for values, n in fields:
        parts.extend(pieces(values, n))
    wide = table.shape[1]
    lane_d = lax.broadcasted_iota(jnp.int32, (count, wide), 1).astype(f32)
    used = jnp.zeros((1, wide), f32)
    if len(parts) * batches % 16:
        parts.append(jnp.zeros((16 - len(parts) * batches % 16, count), f32))
    parts = jnp.concatenate(parts, axis=0).astype(bf16)
    place = first.astype(f32)
    for b in range(batches):
        less = jnp.where(upright[:, b : b + 1] < key[b : b + 1, :], 1.0, 0.0)
        position = jnp.sum(less, axis=0, keepdims=True)
        order = jnp.where(place == position, 1.0, 0.0).astype(bf16)
        ordered = dot_rows(parts, order)
        i = 0
        for f, (_, n) in enumerate(fields):
            total = ordered[i * batches + b : i * batches + b + 1, :]
            for p in range(1, n):
                total = total + ordered[(i + p) * batches + b : (i + p) * batches + b + 1, :]
            meta[f * batches + b : f * batches + b + 1, :] = total
            i += n
        holder = upright[:, batches + b : batches + b + 1]
        length = jnp.sum(jnp.where(holder == lane_d, 1.0, 0.0), axis=0, keepdims=True)
        start = jnp.sum(jnp.where(holder < lane_d, 1.0, 0.0), axis=0, keepdims=True)
        table[b : b + 1, :] = length.astype(jnp.int32)
        table[batches + b : batches + b + 1, :] = start.astype(jnp.int32)
        table[2 * batches + b : 2 * batches + b + 1, :] = used.astype(jnp.int32)
        used = used + length
    flag[0] = (jnp.max(used) > cap).astype(jnp.int32)

    for k in range(chunks):
        for copy in line_out[k]:
            copy.wait_recv()
        view = gathered.at[k, pl.ds((core * plane_n + spot) * line_n, line_n)]
        for j in range(1, plane_n):
            copy = remote(view, view, plane_send.at[k, j - 1], plane_recv.at[k, j - 1], plane_at((spot + j) % plane_n))
            copy.start()
            plane_out[k].append(copy)

    for sends, receives, copy, _ in large:
        pl.when(receives)(copy.wait_recv)
    state[0] += halo_u[...] * coef_u
    state[depth - 1] += halo_d[...] * coef_d
    keep = pltpu.make_async_copy(state, state_out, state_sem)
    keep.start()

    for k in range(chunks):
        for copy in plane_out[k]:
            copy.wait_recv()
        view = gathered.at[k, pl.ds(core * plane_n * line_n, plane_n * line_n)]
        copy = remote(view, view, core_send.at[k], core_recv.at[k], pair)
        copy.start()
        core_out[k].append(copy)
    for k in range(chunks):
        core_out[k][0].wait_recv()
    for group in (line_out, plane_out, core_out):
        for copies in group:
            for copy in copies:
                copy.wait_send()
    for sends, receives, copy, _ in small + large:
        pl.when(sends)(copy.wait_send)
    keep.wait()


def apply_kernel(
    cap, width, table, state_in, gathered, meta, out, layers_ref, later_ref, flat, ordered, load_sem,
):
    load = pltpu.make_async_copy(state_in, layers_ref, load_sem)
    load.start()
    depth, members, _ = layers_ref.shape
    batches, _, count = later_ref.shape
    chunks, devices, piece, _ = gathered.shape
    first = lax.axis_index("tile") * width
    for k in range(chunks):
        for g in range(devices):
            rows = gathered[k, g]
            at = g * cap + 2 * piece * k
            flat[at : at + piece, :] = rows
            flat[at + piece : at + 2 * piece, :] = pltpu.roll(rows, members, 1)

    run = min(cap, (count // devices + 7) // 8 * 8 + 8)

    def spread(g, carry):
        for b in range(batches):
            dst, src = table[batches + b, g], g * cap + table[2 * batches + b, g]
            for i in range(0, run, 8):
                ordered[b, pl.ds(dst + i, 8), :] = flat[pl.ds(src + i, 8), :]

            @pl.when(table[b, g] > run)
            def _(b=b, dst=dst, src=src):
                for i in range(run, cap, 8):
                    ordered[b, pl.ds(dst + i, 8), :] = flat[pl.ds(src + i, 8), :]

        return carry

    lax.fori_loop(0, devices, spread, 0)
    for b in range(batches):
        later_ref[b] = ordered[b, :count, :].T[:members]
    centre = meta[0:batches, :]
    inverse = 1.0 / meta[batches : 2 * batches, :]
    upright = jnp.concatenate([centre, inverse], axis=0).T
    grid = (first + lax.broadcasted_iota(jnp.int32, (1, width), 1)).astype(jnp.float32)

    for b in range(batches):
        y = later_ref[b]
        value, variance = meta[2 * batches + b : 2 * batches + b + 1, :], meta[3 * batches + b : 3 * batches + b + 1, :]
        ymean = jnp.sum(y, axis=0, keepdims=True) * (1.0 / members)
        anomaly = y - ymean
        spread = jnp.sum(anomaly * anomaly, axis=0, keepdims=True) / (members - 1) + 1e-06
        shrink = variance / (spread + variance)
        postmean = spread * shrink * (ymean / spread + value / variance)
        delta = (postmean - ymean) + (jnp.sqrt(shrink) - 1.0) * anomaly
        delta = delta * (1.0 / ((members - 1) * spread))
        d_high, d_low = halves(delta)
        d_both = jnp.concatenate([d_high, d_low], axis=0)
        y_high = anomaly.astype(jnp.bfloat16).astype(jnp.float32)
        y_low = anomaly - y_high
        lhs = jnp.concatenate([y_high, y_high, y_low, y_low], axis=0).T.astype(jnp.bfloat16)
        here, scale = upright[:, b : b + 1], upright[:, batches + b : batches + b + 1]

        def taper(positions):
            frac = jnp.maximum(1.0 - jnp.abs(positions - here) * scale, 0.0)
            return frac * frac

        def change(x, weight):
            x_high, x_low = halves(x - jnp.sum(x, axis=0, keepdims=True) * (1.0 / members))
            rhs = jnp.concatenate([x_high, x_low, x_high, x_low], axis=0)
            gain = jnp.dot(lhs, rhs, preferred_element_type=jnp.float32) * weight
            g_high, g_low = halves(gain)
            one = jnp.dot(d_both, g_high, preferred_element_type=jnp.float32)
            two = jnp.dot(d_high, g_low, preferred_element_type=jnp.float32)
            return one[:members] + one[members:] + two

        for c in range(b + 1, batches):
            later_ref[c] += change(later_ref[c], taper(centre[c : c + 1, :]))
        weight = taper(grid)
        if b == 0:
            load.wait()
        for l in range(depth):
            x = layers_ref[l]
            x = x + change(x, weight)
            if b == batches - 1:
                out[:, l, :] = x
            else:
                layers_ref[l] = x


def slow_shards(ensemble, diff_x, diff_z, cour_x, cour_z, obs_cell, obs_radius, obs_value, obs_var):
    members, depth, width = ensemble.shape
    batches, count = obs_cell.shape
    tiles, layers = lax.axis_size("tile"), lax.axis_size("layer")
    rows = batches * count * members // LANES
    plane_n, line_n = layers * 2, tiles // 4
    half = rows // batches // 2
    size = half // plane_n
    piece = size // line_n if size % (8 * line_n) == 0 else size
    vmem = pl.BlockSpec(memory_space=pltpu.VMEM)
    hbm = pl.BlockSpec(memory_space=pltpu.HBM)
    f32 = jnp.float32
    dma = pltpu.SemaphoreType.DMA
    state, prior = pl.pallas_call(
        functools.partial(gather_kernel, tiles, layers),
        out_shape=(jax.ShapeDtypeStruct((depth, members, width), f32), jax.ShapeDtypeStruct((rows, LANES), f32)),
        in_specs=[hbm] * 6,
        out_specs=(hbm, vmem),
        scratch_shapes=[
            pltpu.VMEM((depth, members, width), f32),
            dma,
            pltpu.VMEM((members, depth, width), f32),
            *[pltpu.VMEM((depth, width), f32)] * 4,
            pltpu.VMEM((batches, count), jnp.int32),
            dma((6,)),
            pltpu.VMEM((depth, members, width), f32),
            *[pltpu.VMEM((members, LANES), f32)] * 4,
            *[pltpu.VMEM((members, width), f32)] * 2,
            *[pltpu.VMEM((8, width), f32)] * 4,
            pltpu.VMEM((rows, LANES), f32),
            pltpu.VMEM((batches, half, LANES), f32),
            pltpu.VMEM((batches, plane_n - 1, size, LANES), f32),
            pltpu.VMEM((batches, line_n - 1, piece, LANES), f32),
            dma((6,)),
            dma((6,)),
            dma((batches, 4)),
            dma((batches, 2 * plane_n - 2)),
            dma((batches, 2 * plane_n - 2)),
            dma((batches, 2 * line_n - 2)),
            dma((batches, 2 * line_n - 2)),
        ],
        compiler_params=pltpu.CompilerParams(collective_id=0, has_side_effects=True, vmem_limit_bytes=63 * 2**20),
        name="gather_prior",
    )(ensemble, diff_x, diff_z, cour_x, cour_z, obs_cell)
    return pl.pallas_call(
        functools.partial(update_kernel, tiles * width, width),
        out_shape=jax.ShapeDtypeStruct((members, depth, width), f32),
        in_specs=[hbm] * 6,
        out_specs=vmem,
        scratch_shapes=[
            pltpu.VMEM((depth, members, width), f32),
            pltpu.VMEM((batches, members, count), f32),
            pltpu.VMEM((rows, LANES), f32),
            *[pltpu.VMEM((batches, count), jnp.int32)] * 2,
            *[pltpu.VMEM((batches, count), f32)] * 2,
            dma((6,)),
        ],
        compiler_params=pltpu.CompilerParams(vmem_limit_bytes=63 * 2**20),
        name="update",
    )(state, prior, obs_cell, obs_radius, obs_value, obs_var)


def shards(ensemble, diff_x, diff_z, cour_x, cour_z, obs_cell, obs_radius, obs_value, obs_var):
    members, depth, width = ensemble.shape
    batches, count = obs_cell.shape
    tiles, layers = lax.axis_size("tile"), lax.axis_size("layer")
    devices = tiles * layers
    plane_n, line_n = layers * 2, tiles // 4
    mean = batches * count / devices
    cap = -int(-(mean + 4.0 * mean**0.5) // 16) * 16
    piece = 16 if cap % 32 == 0 else 8
    chunks = cap // (2 * piece)
    wide = -(-devices // LANES) * LANES
    vmem = pl.BlockSpec(memory_space=pltpu.VMEM)
    smem = pl.BlockSpec(memory_space=pltpu.SMEM)
    hbm = pl.BlockSpec(memory_space=pltpu.HBM)
    f32 = jnp.float32
    dma = pltpu.SemaphoreType.DMA
    state, gathered, meta, table, flag = pl.pallas_call(
        functools.partial(collect_kernel, tiles, layers, cap),
        out_shape=(
            jax.ShapeDtypeStruct((depth, members, width), f32),
            jax.ShapeDtypeStruct((chunks, devices, piece, LANES), f32),
            jax.ShapeDtypeStruct((4 * batches, count), f32),
            jax.ShapeDtypeStruct((3 * batches, wide), jnp.int32),
            jax.ShapeDtypeStruct((1,), jnp.int32),
        ),
        in_specs=[hbm] * 9,
        out_specs=(hbm, vmem, vmem, vmem, smem),
        scratch_shapes=[
            pltpu.VMEM((depth, members, width), f32),
            dma,
            pltpu.VMEM((members, depth, width), f32),
            *[pltpu.VMEM((depth, width), f32)] * 4,
            *[pltpu.VMEM((batches, count), jnp.int32)] * 2,
            *[pltpu.VMEM((batches, count), f32)] * 2,
            dma((9,)),
            pltpu.VMEM((depth, members, width), f32),
            *[pltpu.VMEM((8, LANES), f32)] * 4,
            *[pltpu.VMEM((cap // 2, LANES), f32)] * 4,
            *[pltpu.VMEM((members, width), f32)] * 2,
            dma((6,)),
            dma((6,)),
            *[dma((chunks, max(line_n - 1, 1)))] * 2,
            *[dma((chunks, plane_n - 1))] * 2,
            *[dma((chunks,))] * 2,
        ],
        compiler_params=pltpu.CompilerParams(collective_id=1, has_side_effects=True, vmem_limit_bytes=48 * 2**20),
        name="collect",
    )(ensemble, diff_x, diff_z, cour_x, cour_z, obs_cell, obs_radius, obs_value, obs_var)

    def fast():
        return pl.pallas_call(
            functools.partial(apply_kernel, cap, width),
            out_shape=jax.ShapeDtypeStruct((members, depth, width), f32),
            in_specs=[smem, hbm, vmem, vmem],
            out_specs=vmem,
            scratch_shapes=[
                pltpu.VMEM((depth, members, width), f32),
                pltpu.VMEM((batches, members, count), f32),
                pltpu.VMEM((devices * cap + cap, LANES), f32),
                pltpu.VMEM((batches, count + cap, LANES), f32),
                dma,
            ],
            compiler_params=pltpu.CompilerParams(vmem_limit_bytes=48 * 2**20),
            name="apply",
        )(table, state, gathered, meta)

    def slow():
        return slow_shards(ensemble, diff_x, diff_z, cour_x, cour_z, obs_cell, obs_radius, obs_value, obs_var)

    return lax.cond(flag[0] > 0, slow, fast)


def solution(mesh):
    in_specs = (
        P(None, "layer", "tile"),
        P("layer", "tile"),
        P("layer", "tile"),
        P("layer", "tile"),
        P("layer", "tile"),
        P(),
        P(),
        P(),
        P(),
    )
    out_specs = P(None, "layer", "tile")
    return jax.shard_map(shards, mesh=mesh, in_specs=in_specs, out_specs=out_specs, check_vma=False)
```

```python
import functools

import jax
import jax.numpy as jnp
from jax import lax
from jax.experimental import pallas as pl
from jax.experimental.pallas import tpu as pltpu
from jax.sharding import PartitionSpec as P

MESH = pl.DeviceIdType.MESH
LANES = 128


def split_cell(cells, total):
    if total & (total - 1) == 0:
        return cells >> (total.bit_length() - 1), cells & (total - 1)
    return cells // total, cells % total


def halves(value):
    high = value.astype(jnp.bfloat16)
    return high, (value - high.astype(jnp.float32)).astype(jnp.bfloat16)


def gather_kernel(
    tiles, layers, ens_in, dx_in, dz_in, cx_in, cz_in, cell_in, state_out, prior,
    state, state_sem, ens, diff_x, diff_z, cour_x, cour_z, obs_cell, load_sem,
    cells, edge_w, edge_e, halo_w, halo_e, halo_u, halo_d, coef_up, coef_down, coef_u, coef_d,
    part, in_core, in_plane, in_line, halo_send, halo_recv, core_sem, plane_send, plane_recv, line_send, line_recv,
):
    loads = []
    for i, (src, dst) in enumerate(
        ((ens_in, ens), (dz_in, diff_z), (cz_in, cour_z), (dx_in, diff_x), (cx_in, cour_x), (cell_in, obs_cell))
    ):
        copy = pltpu.make_async_copy(src, dst, load_sem.at[i])
        copy.start()
        loads.append(copy)
    members, depth, width = ens.shape
    batches, count = obs_cell.shape
    tile, layer = lax.axis_index("tile"), lax.axis_index("layer")
    core, row, line = tile % 2, (tile // 2) % 2, tile // 4
    plane_n, line_n = layers * 2, tiles // 4
    spot = layer * 2 + row
    pair = (tile + 1 - 2 * core, layer)

    def plane_at(index):
        return (line * 4 + (index % 2) * 2 + core, index // 2)

    def line_at(index):
        return (index * 4 + row * 2 + core, layer)

    greeted = [pair, ((tile + 1) % tiles, layer), ((tile + tiles - 1) % tiles, layer)]
    greeted += [(tile, (layer + 1) % layers), (tile, (layer + layers - 1) % layers)]
    greeted += [plane_at((spot + j) % plane_n) for j in range(1, plane_n)]
    greeted += [line_at((line + j) % line_n) for j in range(1, line_n)]
    barrier = pltpu.get_barrier_semaphore()
    for device in greeted:
        pl.semaphore_signal(barrier, inc=1, device_id=device, device_id_type=MESH)

    for copy in loads:
        copy.wait()
    lane = lax.broadcasted_iota(jnp.int32, (members, LANES), 1)
    west = jnp.zeros((members, LANES), jnp.float32)
    east = jnp.zeros((members, LANES), jnp.float32)
    for l in range(depth):
        x = ens[:, l, :]
        cells[l] = x
        west = jnp.where(lane == l, x[:, 0:1], west)
        east = jnp.where(lane == l, x[:, width - 1 : width], east)
    edge_w[...] = west
    edge_e[...] = east
    tall = coef_up.shape
    coef_up[...] = jnp.broadcast_to(diff_z[0:1, :] + 0.5 * cour_z[0:1, :], tall)
    coef_down[...] = jnp.broadcast_to(diff_z[depth - 1 : depth, :] - 0.5 * cour_z[depth - 1 : depth, :], tall)
    pl.semaphore_wait(barrier, len(greeted))

    def remote(src, dst, send, recv, device):
        return pltpu.make_async_remote_copy(
            src_ref=src, dst_ref=dst, send_sem=send, recv_sem=recv, device_id=device, device_id_type=MESH
        )

    up, down = layer > 0, layer < layers - 1
    before, after = tile > 0, tile < tiles - 1
    above, below = (tile, lax.rem(layer + layers - 1, layers)), (tile, lax.rem(layer + 1, layers))
    ahead, behind = (lax.rem(tile + 1, tiles), layer), (lax.rem(tile + tiles - 1, tiles), layer)

    def move(i, sends, receives, src, dst, device):
        return sends, receives, remote(src, dst, halo_send.at[i], halo_recv.at[i], device), dst

    small = (
        move(0, after, before, edge_e, halo_w, ahead),
        move(1, before, after, edge_w, halo_e, behind),
        move(2, down, up, coef_down, coef_u, below),
        move(3, up, down, coef_up, coef_d, above),
    )
    large = (
        move(4, down, up, cells.at[depth - 1], halo_u, below),
        move(5, up, down, cells.at[0], halo_d, above),
    )
    for sends, receives, copy, place in small:
        pl.when(sends)(copy.start)
    for sends, receives, copy, place in small + large:

        @pl.when(jnp.logical_not(receives))
        def _(place=place):
            place[...] = jnp.zeros_like(place)

    for sends, receives, copy, place in small:
        pl.when(receives)(copy.wait_recv)

    column = lax.broadcasted_iota(jnp.int32, (members, width), 1)
    levels = list(range(depth)) + [-1, depth]
    parts = []
    for l in range(depth):
        x = cells[l]
        left = jnp.where(column == 0, halo_w[:, l : l + 1], pltpu.roll(x, 1, 1))
        right = jnp.where(column == width - 1, halo_e[:, l : l + 1], pltpu.roll(x, width - 1, 1))
        dx, dz = diff_x[l : l + 1, :], diff_z[l : l + 1, :]
        cx, cz = 0.5 * cour_x[l : l + 1, :], 0.5 * cour_z[l : l + 1, :]
        new = x * (1.0 - 2.0 * dz - 2.0 * dx) + left * (dx + cx) + right * (dx - cx)
        if l > 0:
            new = new + cells[l - 1] * (dz + cz)
        if l < depth - 1:
            new = new + cells[l + 1] * (dz - cz)
        state[l] = new
        parts.extend(halves(new))
    parts.extend(halves(cells[0] * coef_u[0:1, :]))
    parts.extend(halves(cells[depth - 1] * coef_d[0:1, :]))
    stacked = jnp.concatenate(parts, axis=0)

    blocks = count // LANES
    extent = blocks * members
    half = extent // 2
    size = half // plane_n
    scatter = size % (8 * line_n) == 0
    piece = size // line_n if scatter else size
    place = lax.broadcasted_iota(jnp.int32, (width, count), 0)

    def start_of(b, *steps):
        total = b * extent
        for index, length in steps:
            total = total + index * length
        return pl.multiple_of(total, 8)

    every = range(batches)
    core_out, plane_out, line_out, line_back, plane_back, core_back = ([[] for _ in every] for _ in range(6))
    for b in every:
        rows, cols = split_cell(obs_cell[b : b + 1, :], tiles * width)
        rows, cols = rows - layer * depth, cols - tile * width
        hot = jnp.where(place == cols, 1.0, 0.0).astype(jnp.bfloat16)
        picked = jnp.dot(stacked, hot, preferred_element_type=jnp.float32)
        total = jnp.zeros((members, count), jnp.float32)
        for i, l in enumerate(levels):
            both = picked[2 * i * members : (2 * i + 1) * members] + picked[(2 * i + 1) * members : (2 * i + 2) * members]
            total = jnp.where(rows == l, both, total)
        for k in range(blocks):
            part[pl.ds((b * blocks + k) * members, members), :] = total[:, k * LANES : (k + 1) * LANES]
        copy = remote(part.at[pl.ds(start_of(b, (1 - core, half)), half)], in_core.at[b], core_sem.at[b, 0], core_sem.at[b, 1], pair)
        copy.start()
        core_out[b].append(copy)

    for b in every:
        core_out[b][0].wait_recv()
        part[pl.ds(start_of(b, (core, half)), half), :] += in_core[b]
        for j in range(1, plane_n):
            to = (spot + j) % plane_n
            copy = remote(
                part.at[pl.ds(start_of(b, (core, half), (to, size)), size)], in_plane.at[b, j - 1],
                plane_send.at[b, j - 1], plane_recv.at[b, j - 1], plane_at(to),
            )
            copy.start()
            plane_out[b].append(copy)
    for b in every:
        base = start_of(b, (core, half), (spot, size))
        total = part[pl.ds(base, size), :]
        for j in range(1, plane_n):
            plane_out[b][j - 1].wait_recv()
            total = total + in_plane[b, j - 1]
        part[pl.ds(base, size), :] = total
        for j in range(1, line_n):
            to = (line + j) % line_n
            start = start_of(b, (core, half), (spot, size), (to, piece)) if scatter else base
            copy = remote(part.at[pl.ds(start, piece)], in_line.at[b, j - 1], line_send.at[b, j - 1], line_recv.at[b, j - 1], line_at(to))
            copy.start()
            line_out[b].append(copy)
    for sends, receives, copy, _ in large:
        pl.when(sends)(copy.start)

    def spread_plane(b):
        view = prior.at[pl.ds(start_of(b, (core, half), (spot, size)), size)]
        for j in range(1, plane_n):
            k = plane_n - 1 + j - 1
            copy = remote(view, view, plane_send.at[b, k], plane_recv.at[b, k], plane_at((spot + j) % plane_n))
            copy.start()
            plane_back[b].append(copy)

    for b in every:
        own = start_of(b, (core, half), (spot, size), (line, piece)) if scatter else start_of(b, (core, half), (spot, size))
        total = part[pl.ds(own, piece), :]
        for j in range(1, line_n):
            line_out[b][j - 1].wait_recv()
            total = total + in_line[b, j - 1]
        prior[pl.ds(own, piece), :] = total
        if scatter:
            view = prior.at[pl.ds(own, piece)]
            for j in range(1, line_n):
                k = line_n - 1 + j - 1
                copy = remote(view, view, line_send.at[b, k], line_recv.at[b, k], line_at((line + j) % line_n))
                copy.start()
                line_back[b].append(copy)
        else:
            spread_plane(b)
    if scatter:
        for b in every:
            for copy in line_back[b]:
                copy.wait_recv()
            spread_plane(b)

    for sends, receives, copy, _ in large:
        pl.when(receives)(copy.wait_recv)
    state[0] += halo_u[...] * (diff_z[0:1, :] + 0.5 * cour_z[0:1, :])
    state[depth - 1] += halo_d[...] * (diff_z[depth - 1 : depth, :] - 0.5 * cour_z[depth - 1 : depth, :])
    keep = pltpu.make_async_copy(state, state_out, state_sem)
    keep.start()

    for b in every:
        for copy in plane_back[b]:
            copy.wait_recv()
        view = prior.at[pl.ds(start_of(b, (core, half)), half)]
        copy = remote(view, view, core_sem.at[b, 2], core_sem.at[b, 3], pair)
        copy.start()
        core_back[b].append(copy)
    for b in every:
        core_back[b][0].wait_recv()
    for group in (core_out, plane_out, line_out, line_back, plane_back, core_back):
        for copies in group:
            for copy in copies:
                copy.wait_send()
    for sends, receives, copy, _ in small + large:
        pl.when(sends)(copy.wait_send)
    keep.wait()


def update_kernel(
    total_cols, width, state_in, prior_in, cell_in, radius_in, value_in, var_in, out,
    layers_ref, later_ref, prior, obs_cell, obs_radius, obs_value, obs_var, load_sem,
):
    loads = []
    for i, (src, dst) in enumerate(
        (
            (cell_in, obs_cell), (radius_in, obs_radius), (value_in, obs_value), (var_in, obs_var),
            (prior_in, prior), (state_in, layers_ref),
        )
    ):
        copy = pltpu.make_async_copy(src, dst, load_sem.at[i])
        copy.start()
        loads.append(copy)
    depth, members, _ = layers_ref.shape
    batches, count = obs_cell.shape
    blocks = count // LANES
    first = lax.axis_index("tile") * width
    for copy in loads[:-1]:
        copy.wait()
    for b in range(batches):
        for k in range(blocks):
            later_ref[b, :, k * LANES : (k + 1) * LANES] = prior[pl.ds((b * blocks + k) * members, members), :]
    centre = split_cell(obs_cell[...], total_cols)[1].astype(jnp.float32)
    inverse = 1.0 / obs_radius[...].astype(jnp.float32)
    upright = jnp.concatenate([centre, inverse], axis=0).T
    grid = (first + lax.broadcasted_iota(jnp.int32, (1, width), 1)).astype(jnp.float32)

    for b in range(batches):
        y = later_ref[b]
        value, variance = obs_value[b : b + 1, :], obs_var[b : b + 1, :]
        ymean = jnp.sum(y, axis=0, keepdims=True) * (1.0 / members)
        anomaly = y - ymean
        spread = jnp.sum(anomaly * anomaly, axis=0, keepdims=True) / (members - 1) + 1e-06
        shrink = variance / (spread + variance)
        postmean = spread * shrink * (ymean / spread + value / variance)
        delta = (postmean - ymean) + (jnp.sqrt(shrink) - 1.0) * anomaly
        delta = delta * (1.0 / ((members - 1) * spread))
        d_high, d_low = halves(delta)
        d_both = jnp.concatenate([d_high, d_low], axis=0)
        y_high = anomaly.astype(jnp.bfloat16).astype(jnp.float32)
        y_low = anomaly - y_high
        lhs = jnp.concatenate([y_high, y_high, y_low, y_low], axis=0).T.astype(jnp.bfloat16)
        here, scale = upright[:, b : b + 1], upright[:, batches + b : batches + b + 1]

        def taper(positions):
            frac = jnp.maximum(1.0 - jnp.abs(positions - here) * scale, 0.0)
            return frac * frac

        def change(x, weight):
            x_high, x_low = halves(x - jnp.sum(x, axis=0, keepdims=True) * (1.0 / members))
            rhs = jnp.concatenate([x_high, x_low, x_high, x_low], axis=0)
            gain = jnp.dot(lhs, rhs, preferred_element_type=jnp.float32) * weight
            g_high, g_low = halves(gain)
            one = jnp.dot(d_both, g_high, preferred_element_type=jnp.float32)
            two = jnp.dot(d_high, g_low, preferred_element_type=jnp.float32)
            return one[:members] + one[members:] + two

        for c in range(b + 1, batches):
            later_ref[c] += change(later_ref[c], taper(centre[c : c + 1, :]))
        weight = taper(grid)
        if b == 0:
            loads[-1].wait()
        for l in range(depth):
            x = layers_ref[l]
            x = x + change(x, weight)
            if b == batches - 1:
                out[:, l, :] = x
            else:
                layers_ref[l] = x


def divide(values, size):
    return values >> (size.bit_length() - 1) if size & (size - 1) == 0 else values // size


def dot_rows(a, b):
    return lax.dot_general(a, b, (((1,), (1,)), ((), ())), preferred_element_type=jnp.float32)


def remote(src, dst, send, recv, device):
    return pltpu.make_async_remote_copy(
        src_ref=src, dst_ref=dst, send_sem=send, recv_sem=recv, device_id=device, device_id_type=MESH
    )


def collect_kernel(
    tiles, layers, cap, ens_in, dx_in, dz_in, cx_in, cz_in, cell_in, radius_in, value_in, var_in,
    state_out, gathered, meta, taper_in, kinks, table, flag,
    state, state_sem, ens, diff_x, diff_z, cour_x, cour_z, obs_cell, obs_radius, obs_value, obs_var, load_sem,
    cells, edge_w, edge_e, halo_w, halo_e, near_u, near_d, part_u, part_d, halo_u, halo_d,
    hop_send, hop_recv, line_send, line_recv, plane_send, plane_recv, core_send, core_recv,
):
    loads = []
    for i, (src, dst) in enumerate(
        (
            (cell_in, obs_cell), (ens_in, ens), (dz_in, diff_z), (cz_in, cour_z), (dx_in, diff_x), (cx_in, cour_x),
            (radius_in, obs_radius), (value_in, obs_value), (var_in, obs_var),
        )
    ):
        copy = pltpu.make_async_copy(src, dst, load_sem.at[i])
        copy.start()
        loads.append(copy)
    members, depth, width = ens.shape
    batches, count = obs_cell.shape
    chunks, devices, piece, _ = gathered.shape
    f32, bf16 = jnp.float32, jnp.bfloat16
    tile, layer = lax.axis_index("tile"), lax.axis_index("layer")
    core, row, line = tile % 2, (tile // 2) % 2, tile // 4
    plane_n, line_n = layers * 2, tiles // 4
    spot = layer * 2 + row
    pair = (tile + 1 - 2 * core, layer)

    def plane_at(index):
        return (line * 4 + (index % 2) * 2 + core, index // 2)

    def line_at(index):
        return (index * 4 + row * 2 + core, layer)

    above, below = (tile, lax.rem(layer + layers - 1, layers)), (tile, lax.rem(layer + 1, layers))
    ahead, behind = (lax.rem(tile + 1, tiles), layer), (lax.rem(tile + tiles - 1, tiles), layer)
    greeted = [pair, ahead, behind, below, above]
    greeted += [plane_at((spot + j) % plane_n) for j in range(1, plane_n)]
    greeted += [line_at((line + j) % line_n) for j in range(1, line_n)]
    barrier = pltpu.get_barrier_semaphore()
    for device in greeted:
        pl.semaphore_signal(barrier, inc=1, device_id=device, device_id_type=MESH)

    loads[0].wait()
    cell_row, cell_col = split_cell(obs_cell[...], tiles * width)
    cell_tile, cell_layer = divide(cell_col, width), divide(cell_row, depth)
    local_col, local_row = cell_col - cell_tile * width, cell_row - cell_layer * depth
    here = cell_tile == tile
    groups = [
        jnp.where(jnp.logical_and(here, cell_layer == layer + step), 1.0, 0.0) for step in (0, -1, 1)
    ]
    masks = jnp.concatenate(groups + [jnp.zeros_like(groups[0])], axis=0).astype(bf16)
    first = lax.broadcasted_iota(jnp.int32, (count, count), 0)
    second = lax.broadcasted_iota(jnp.int32, (count, count), 1)
    running = jnp.dot(masks, jnp.where(first <= second, 1.0, 0.0).astype(bf16), preferred_element_type=f32)
    code = (local_row * width + local_col + 1).astype(f32)
    slot = lax.broadcasted_iota(jnp.int32, (cap, count), 0).astype(f32)
    lane_w = lax.broadcasted_iota(jnp.int32, (cap, width), 1)
    found = []
    for k, edge in enumerate((None, depth - 1, 0)):
        before_ = jnp.zeros((1, 1), f32)
        total = jnp.zeros((cap, count), f32)
        for b in range(batches):
            i = k * batches + b
            wanted = groups[k][b : b + 1, :] > 0.5
            if edge is not None:
                wanted = jnp.logical_and(wanted, local_row[b : b + 1, :] == edge)
            rank = jnp.where(wanted, running[i : i + 1, :] + (before_ - 1.0), -1.0)
            total = total + jnp.where(rank == slot, code[b : b + 1, :], 0.0)
            before_ = before_ + running[i : i + 1, count - 1 : count]
        cell = jnp.sum(total, axis=1, keepdims=True).astype(jnp.int32) - 1
        at_row = divide(cell, width)
        at_col = jnp.where(cell >= 0, cell - at_row * width, -1)
        found.append((at_row, at_col, jnp.where(lane_w == at_col, 1.0, 0.0)))

    low = lax.broadcasted_iota(jnp.int32, (piece, LANES), 1) < members

    def packed(values):
        out = []
        for k in range(chunks):
            base = 2 * piece * k
            out.append(jnp.where(low, values[base : base + piece], values[base + piece : base + 2 * piece]))
        return out

    def doubled(values):
        return values + pltpu.roll(values, members, 1)

    for copy in loads[1:6]:
        copy.wait()
    lane = lax.broadcasted_iota(jnp.int32, (members, LANES), 1)
    west = jnp.zeros((members, LANES), f32)
    east = jnp.zeros((members, LANES), f32)
    for l in range(depth):
        x = ens[:, l, :]
        cells[l] = x
        west = jnp.where(lane == l, x[:, 0:1], west)
        east = jnp.where(lane == l, x[:, width - 1 : width], east)
    edge_w[...] = jnp.concatenate([west, west], axis=0).T[:8]
    edge_e[...] = jnp.concatenate([east, east], axis=0).T[:8]
    for ref, k, l in ((part_u, 1, 0), (part_d, 2, depth - 1)):
        raw = jnp.concatenate(halves(cells[l]), axis=0)
        for i, rows in enumerate(packed(doubled(dot_rows(found[k][2].astype(bf16), raw)))):
            ref[i * piece : (i + 1) * piece, :] = rows
    pl.semaphore_wait(barrier, len(greeted))

    up, down = layer > 0, layer < layers - 1
    before, after = tile > 0, tile < tiles - 1

    def move(i, sends, receives, src, dst, device):
        return sends, receives, remote(src, dst, hop_send.at[i], hop_recv.at[i], device), dst

    small = (
        move(0, down, up, part_d, near_u, below),
        move(1, up, down, part_u, near_d, above),
        move(2, after, before, edge_e, halo_w, ahead),
        move(3, before, after, edge_w, halo_e, behind),
    )
    large = (
        move(4, down, up, cells.at[depth - 1], halo_u, below),
        move(5, up, down, cells.at[0], halo_d, above),
    )
    for sends, receives, copy, place in small:
        pl.when(sends)(copy.start)
    for sends, receives, copy, place in small + large:

        @pl.when(jnp.logical_not(receives))
        def _(place=place):
            place[...] = jnp.zeros_like(place)

    at_row, at_col, hot = found[0]
    column = lax.broadcasted_iota(jnp.int32, (members, width), 1)
    total = jnp.zeros((cap, LANES), f32)
    for l in range(depth):
        x = cells[l]
        left = jnp.where(column == 0, 0.0, pltpu.roll(x, 1, 1))
        right = jnp.where(column == width - 1, 0.0, pltpu.roll(x, width - 1, 1))
        dx, dz = diff_x[l : l + 1, :], diff_z[l : l + 1, :]
        cx, cz = 0.5 * cour_x[l : l + 1, :], 0.5 * cour_z[l : l + 1, :]
        new = x * (1.0 - 2.0 * dz - 2.0 * dx) + left * (dx + cx) + right * (dx - cx)
        if l > 0:
            new = new + cells[l - 1] * (dz + cz)
        if l < depth - 1:
            new = new + cells[l + 1] * (dz - cz)
        state[l] = new
        picked = dot_rows(hot.astype(bf16), jnp.concatenate(halves(new), axis=0))
        total = total + jnp.where(at_row == l, picked, 0.0)
    mine = packed(doubled(total))
    coef_u = diff_z[0:1, :] + 0.5 * cour_z[0:1, :]
    coef_d = diff_z[depth - 1 : depth, :] - 0.5 * cour_z[depth - 1 : depth, :]
    take_u = jnp.where(at_row == 0, jnp.sum(hot * coef_u, axis=1, keepdims=True), 0.0)
    take_d = jnp.where(at_row == depth - 1, jnp.sum(hot * coef_d, axis=1, keepdims=True), 0.0)
    coef_w = diff_x[:, 0:1] + 0.5 * cour_x[:, 0:1]
    coef_e = diff_x[:, width - 1 : width] - 0.5 * cour_x[:, width - 1 : width]
    weights = [packed(jnp.broadcast_to(take, (cap, LANES))) for take in (take_u, take_d)]
    sides = []
    for at, coef in ((0, coef_w), (width - 1, coef_e)):
        for l in range(depth):
            take = jnp.where(jnp.logical_and(at_row == l, at_col == at), coef[l : l + 1, :], 0.0)
            sides.append(packed(jnp.broadcast_to(take, (cap, LANES))))

    for sends, receives, copy, place in small:
        pl.when(receives)(copy.wait_recv)
    me = (core * plane_n + spot) * line_n + line
    line_out, plane_out, core_out = ([[] for _ in range(chunks)] for _ in range(3))
    for k in range(chunks):
        rows = pl.ds(k * piece, piece)
        value = mine[k] + weights[0][k] * near_u[rows, :] + weights[1][k] * near_d[rows, :]
        for l in range(depth):
            value = value + sides[l][k] * halo_w[l : l + 1, :] + sides[depth + l][k] * halo_e[l : l + 1, :]
        gathered[k, me] = value
        view = gathered.at[k, me]
        for j in range(1, line_n):
            copy = remote(view, view, line_send.at[k, j - 1], line_recv.at[k, j - 1], line_at((line + j) % line_n))
            copy.start()
            line_out[k].append(copy)
    for sends, receives, copy, _ in large:
        pl.when(sends)(copy.start)

    for ref, coef, at in ((halo_w, coef_w, 0), (halo_e, coef_e, width - 1)):
        base = at // LANES * LANES
        block = lax.broadcasted_iota(jnp.int32, (members, LANES), 1)
        turned = jnp.concatenate([ref[...]] * (LANES // 8), axis=0).T[:members]
        for l in range(depth):
            term = turned[:, l : l + 1] * coef[l : l + 1, :]
            state[l, :, base : base + LANES] += jnp.where(block == at - base, term, 0.0)

    for copy in loads[6:]:
        copy.wait()
    core_of, row_of, line_of = cell_tile & 1, divide(cell_tile, 2) & 1, divide(cell_tile, 4)
    owner = (core_of * plane_n + cell_layer * 2 + row_of) * line_n + line_of
    key = (owner * count + lax.broadcasted_iota(jnp.int32, (batches, count), 1)).astype(f32)
    upright = jnp.concatenate([key, jnp.zeros_like(key)], axis=0).T

    def pieces(values, n):
        out = []
        for _ in range(n):
            high = values.astype(bf16).astype(f32)
            out.append(high)
            values = values - high
        return out

    fields = (
        (cell_col.astype(f32), 2), (obs_radius[...].astype(f32), 2), (obs_value[...], 3), (obs_var[...], 3)
    )
    parts = []
    for values, n in fields:
        parts.extend(pieces(values, n))
    devices_at = lax.broadcasted_iota(jnp.int32, (devices, count), 0)
    tiles_at = lax.broadcasted_iota(jnp.int32, (tiles, count), 0)
    ends = [divide(cell_col + obs_radius[...] * step, width) for step in (-1, 0, 1)]
    used = jnp.zeros((devices, 1), f32)
    worst = jnp.zeros((tiles, 1), f32)
    if len(parts) * batches % 16:
        parts.append(jnp.zeros((16 - len(parts) * batches % 16, count), f32))
    parts = jnp.concatenate(parts, axis=0).astype(bf16)
    place = first.astype(f32)
    for b in range(batches):
        less = jnp.where(upright[:, b : b + 1] < key[b : b + 1, :], 1.0, 0.0)
        position = jnp.sum(less, axis=0, keepdims=True)
        order = jnp.where(place == position, 1.0, 0.0).astype(bf16)
        ordered = dot_rows(parts, order)
        i = 0
        for f, (_, n) in enumerate(fields):
            total = ordered[i * batches + b : i * batches + b + 1, :]
            for p in range(1, n):
                total = total + ordered[(i + p) * batches + b : (i + p) * batches + b + 1, :]
            meta[f * batches + b : f * batches + b + 1, :] = total
            i += n
        holder = owner[b : b + 1, :]
        length = jnp.sum(jnp.where(holder == devices_at, 1.0, 0.0), axis=1, keepdims=True)
        start = jnp.sum(jnp.where(holder < devices_at, 1.0, 0.0), axis=1, keepdims=True)
        table[:, b : b + 1] = length.astype(jnp.int32)
        table[:, batches + b : batches + b + 1] = start.astype(jnp.int32)
        table[:, 2 * batches + b : 2 * batches + b + 1] = used.astype(jnp.int32)
        used = used + length
        bent = jnp.zeros((tiles, count), f32)
        for end in ends:
            bent = bent + jnp.where(end[b : b + 1, :] == tiles_at, 1.0, 0.0)
        worst = jnp.maximum(worst, jnp.sum(bent, axis=1, keepdims=True))
    over = jnp.logical_or(jnp.max(used) > cap, jnp.max(worst) > LANES)
    flag[0] = over.astype(jnp.int32)

    for k in range(chunks):
        for copy in line_out[k]:
            copy.wait_recv()
        view = gathered.at[k, pl.ds((core * plane_n + spot) * line_n, line_n)]
        for j in range(1, plane_n):
            copy = remote(view, view, plane_send.at[k, j - 1], plane_recv.at[k, j - 1], plane_at((spot + j) % plane_n))
            copy.start()
            plane_out[k].append(copy)

    middle = (width - 1) / 2
    lowest = (tile * width).astype(f32)
    highest = lowest + (width - 1)
    centre, radius = meta[0:batches, :], meta[batches : 2 * batches, :]
    inverse = 1.0 / radius
    right_of, left_of = centre <= lowest, centre >= highest
    near, far = centre - radius, centre + radius
    smooth = jnp.logical_or(
        jnp.logical_and(right_of, far >= highest), jnp.logical_and(left_of, near <= lowest)
    )
    away = jnp.logical_or(jnp.logical_and(right_of, far <= lowest), jnp.logical_and(left_of, near >= highest))
    kink = jnp.where(jnp.logical_or(smooth, away), 0.0, 1.0)
    value = jnp.where(smooth, 1.0 - jnp.abs(lowest + middle - centre) * inverse, 0.0)
    slope = jnp.where(smooth, jnp.where(right_of, -middle, middle) * inverse, 0.0)
    padded = jnp.concatenate([kink] + [jnp.zeros_like(kink)] * (16 // batches - 1), axis=0).astype(bf16)
    counted = jnp.dot(padded, jnp.where(first <= second, 1.0, 0.0).astype(bf16), preferred_element_type=f32)
    rank = jnp.where(kink > 0.5, counted[:batches] - 1.0, -1.0)
    for i, rows in enumerate((value * value, 2.0 * value * slope, slope * slope, rank)):
        taper_in[i * batches : (i + 1) * batches, :] = rows
    parts = pieces(centre, 2) + pieces(inverse, 3)
    parts = jnp.concatenate(parts + [jnp.zeros_like(centre)] * (-len(parts) % (16 // batches)), axis=0).astype(bf16)
    kink_row = lax.broadcasted_iota(jnp.int32, (LANES, count), 0).astype(f32)
    kink_lane = lax.broadcasted_iota(jnp.int32, (LANES, LANES), 1)
    columns = jnp.zeros((LANES, LANES), f32)
    for b in range(batches):
        ordered = dot_rows(jnp.where(kink_row == rank[b : b + 1, :], 1.0, 0.0).astype(bf16), parts)
        at = [ordered[:, p * batches + b : p * batches + b + 1] for p in range(5)]
        columns = jnp.where(kink_lane == b, at[0] + at[1], columns)
        columns = jnp.where(kink_lane == batches + b, at[2] + at[3] + at[4], columns)
    kinks[...] = columns

    for sends, receives, copy, _ in large:
        pl.when(receives)(copy.wait_recv)
    state[0] += halo_u[...] * coef_u
    state[depth - 1] += halo_d[...] * coef_d
    keep = pltpu.make_async_copy(state, state_out, state_sem)
    keep.start()

    for k in range(chunks):
        for copy in plane_out[k]:
            copy.wait_recv()
        view = gathered.at[k, pl.ds(core * plane_n * line_n, plane_n * line_n)]
        copy = remote(view, view, core_send.at[k], core_recv.at[k], pair)
        copy.start()
        core_out[k].append(copy)
    for k in range(chunks):
        core_out[k][0].wait_recv()
    for group in (line_out, plane_out, core_out):
        for copies in group:
            for copy in copies:
                copy.wait_send()
    for sends, receives, copy, _ in small + large:
        pl.when(sends)(copy.wait_send)
    keep.wait()


def apply_kernel(
    cap, width, table, state_in, gathered, meta, taper_in, kinks, out, layers_ref, later_ref, flat, ordered, load_sem,
):
    load = pltpu.make_async_copy(state_in, layers_ref, load_sem)
    load.start()
    depth, members, _ = layers_ref.shape
    batches, _, count = later_ref.shape
    chunks, devices, piece, _ = gathered.shape
    first = lax.axis_index("tile") * width
    for k in range(chunks):
        for g in range(devices):
            rows = gathered[k, g]
            at = g * cap + 2 * piece * k
            flat[at : at + piece, :] = rows
            flat[at + piece : at + 2 * piece, :] = pltpu.roll(rows, members, 1)

    run = min(cap, (count // devices + 7) // 8 * 8 + 8)

    def spread(g, carry):
        for b in range(batches):
            dst, src = table[g, batches + b], g * cap + table[g, 2 * batches + b]
            for i in range(0, run, 8):
                ordered[b, pl.ds(dst + i, 8), :] = flat[pl.ds(src + i, 8), :]

            @pl.when(table[g, b] > run)
            def _(b=b, dst=dst, src=src):
                for i in range(run, cap, 8):
                    ordered[b, pl.ds(dst + i, 8), :] = flat[pl.ds(src + i, 8), :]

        return carry

    lax.fori_loop(0, devices, spread, 0)
    for b in range(batches):
        later_ref[b] = ordered[b, :count, :].T[:members]
    centre = meta[0:batches, :]
    inverse = 1.0 / meta[batches : 2 * batches, :]
    upright = jnp.concatenate([centre, inverse], axis=0).T
    grid = (first + lax.broadcasted_iota(jnp.int32, (1, width), 1)).astype(jnp.float32)

    middle = (width - 1) / 2
    offset = lax.broadcasted_iota(jnp.int32, (1, width), 1).astype(jnp.float32)
    ratio = (offset - middle) * (1.0 / middle)
    low = lax.broadcasted_iota(jnp.int32, (LANES, LANES), 1) < members
    kink_row = lax.broadcasted_iota(jnp.int32, (LANES, count), 0).astype(jnp.float32)
    third = 3 * members

    def bump(positions, here, scale):
        frac = jnp.maximum(1.0 - jnp.abs(positions - here) * scale, 0.0)
        return frac * frac

    for b in range(batches):
        y = later_ref[b]
        value, variance = meta[2 * batches + b : 2 * batches + b + 1, :], meta[3 * batches + b : 3 * batches + b + 1, :]
        ymean = jnp.sum(y, axis=0, keepdims=True) * (1.0 / members)
        anomaly = y - ymean
        spread = jnp.sum(anomaly * anomaly, axis=0, keepdims=True) / (members - 1) + 1e-06
        shrink = variance / (spread + variance)
        postmean = spread * shrink * (ymean / spread + value / variance)
        delta = (postmean - ymean) + (jnp.sqrt(shrink) - 1.0) * anomaly
        delta = delta * (1.0 / ((members - 1) * spread))
        d_high, d_low = halves(delta)
        d_both = jnp.concatenate([d_high, d_low], axis=0)
        y_high = anomaly.astype(jnp.bfloat16).astype(jnp.float32)
        y_low = anomaly - y_high
        y_both = jnp.concatenate([y_high, y_low], axis=0).astype(jnp.bfloat16)
        here, scale = upright[:, b : b + 1], upright[:, batches + b : batches + b + 1]

        def stack(x):
            x_high, x_low = halves(x - jnp.sum(x, axis=0, keepdims=True) * (1.0 / members))
            return jnp.concatenate([x_high, x_low, x_high, x_low], axis=0)

        if b < batches - 1:
            lhs = jnp.concatenate([y_high, y_high, y_low, y_low], axis=0).T.astype(jnp.bfloat16)
        for c in range(b + 1, batches):
            x = later_ref[c]
            gain = jnp.dot(lhs, stack(x), preferred_element_type=jnp.float32) * bump(centre[c : c + 1, :], here, scale)
            g_high, g_low = halves(gain)
            one = jnp.dot(d_both, g_high, preferred_element_type=jnp.float32)
            two = jnp.dot(d_high, g_low, preferred_element_type=jnp.float32)
            later_ref[c] = x + (one[:members] + one[members:] + two)

        scaled = [delta * taper_in[i * batches + b : i * batches + b + 1, :] for i in range(3)]
        scaled = halves(jnp.concatenate(scaled, axis=0))
        moment = dot_rows(jnp.concatenate(scaled, axis=0), y_both)
        moment = moment[:third] + moment[third:]
        moment = halves(moment + pltpu.roll(moment, members, 1))
        choose = jnp.where(kink_row == taper_in[3 * batches + b : 3 * batches + b + 1, :], 1.0, 0.0).astype(jnp.bfloat16)
        y_kink = dot_rows(choose, y_both)
        turned = pltpu.roll(y_kink, members, 1)
        y_kink = (jnp.where(low, y_kink, turned).astype(jnp.bfloat16), jnp.where(low, turned, y_kink).astype(jnp.bfloat16))
        left = jnp.concatenate([jnp.concatenate(moment, axis=1), jnp.concatenate(y_kink, axis=1)], axis=0)
        d_kink = dot_rows(d_both, choose)
        d_kink = jnp.concatenate([d_kink, jnp.where(kink_row[:, :LANES] < members, d_kink, 0.0)], axis=1).astype(jnp.bfloat16)
        weight = bump(grid, kinks[:, b : b + 1], kinks[:, batches + b : batches + b + 1])
        if b == 0:
            load.wait()
        for l in range(depth):
            x = layers_ref[l]
            both = jnp.dot(left, stack(x), preferred_element_type=jnp.float32)
            gain = jnp.concatenate(halves(both[third:] * weight), axis=0)
            more = jnp.dot(d_kink, gain, preferred_element_type=jnp.float32)
            x = x + (both[:members] + ratio * (both[members : 2 * members] + ratio * both[2 * members : third]))
            x = x + (more[:members] + more[members:])
            if b == batches - 1:
                out[:, l, :] = x
            else:
                layers_ref[l] = x


def slow_shards(ensemble, diff_x, diff_z, cour_x, cour_z, obs_cell, obs_radius, obs_value, obs_var):
    members, depth, width = ensemble.shape
    batches, count = obs_cell.shape
    tiles, layers = lax.axis_size("tile"), lax.axis_size("layer")
    rows = batches * count * members // LANES
    plane_n, line_n = layers * 2, tiles // 4
    half = rows // batches // 2
    size = half // plane_n
    piece = size // line_n if size % (8 * line_n) == 0 else size
    vmem = pl.BlockSpec(memory_space=pltpu.VMEM)
    hbm = pl.BlockSpec(memory_space=pltpu.HBM)
    f32 = jnp.float32
    dma = pltpu.SemaphoreType.DMA
    state, prior = pl.pallas_call(
        functools.partial(gather_kernel, tiles, layers),
        out_shape=(jax.ShapeDtypeStruct((depth, members, width), f32), jax.ShapeDtypeStruct((rows, LANES), f32)),
        in_specs=[hbm] * 6,
        out_specs=(hbm, vmem),
        scratch_shapes=[
            pltpu.VMEM((depth, members, width), f32),
            dma,
            pltpu.VMEM((members, depth, width), f32),
            *[pltpu.VMEM((depth, width), f32)] * 4,
            pltpu.VMEM((batches, count), jnp.int32),
            dma((6,)),
            pltpu.VMEM((depth, members, width), f32),
            *[pltpu.VMEM((members, LANES), f32)] * 4,
            *[pltpu.VMEM((members, width), f32)] * 2,
            *[pltpu.VMEM((8, width), f32)] * 4,
            pltpu.VMEM((rows, LANES), f32),
            pltpu.VMEM((batches, half, LANES), f32),
            pltpu.VMEM((batches, plane_n - 1, size, LANES), f32),
            pltpu.VMEM((batches, line_n - 1, piece, LANES), f32),
            dma((6,)),
            dma((6,)),
            dma((batches, 4)),
            dma((batches, 2 * plane_n - 2)),
            dma((batches, 2 * plane_n - 2)),
            dma((batches, 2 * line_n - 2)),
            dma((batches, 2 * line_n - 2)),
        ],
        compiler_params=pltpu.CompilerParams(collective_id=0, has_side_effects=True, vmem_limit_bytes=63 * 2**20),
        name="gather_prior",
    )(ensemble, diff_x, diff_z, cour_x, cour_z, obs_cell)
    return pl.pallas_call(
        functools.partial(update_kernel, tiles * width, width),
        out_shape=jax.ShapeDtypeStruct((members, depth, width), f32),
        in_specs=[hbm] * 6,
        out_specs=vmem,
        scratch_shapes=[
            pltpu.VMEM((depth, members, width), f32),
            pltpu.VMEM((batches, members, count), f32),
            pltpu.VMEM((rows, LANES), f32),
            *[pltpu.VMEM((batches, count), jnp.int32)] * 2,
            *[pltpu.VMEM((batches, count), f32)] * 2,
            dma((6,)),
        ],
        compiler_params=pltpu.CompilerParams(vmem_limit_bytes=63 * 2**20),
        name="update",
    )(state, prior, obs_cell, obs_radius, obs_value, obs_var)


def shards(ensemble, diff_x, diff_z, cour_x, cour_z, obs_cell, obs_radius, obs_value, obs_var):
    members, depth, width = ensemble.shape
    batches, count = obs_cell.shape
    tiles, layers = lax.axis_size("tile"), lax.axis_size("layer")
    devices = tiles * layers
    plane_n, line_n = layers * 2, tiles // 4
    mean = batches * count / devices
    cap = -int(-(mean + 4.0 * mean**0.5) // 16) * 16
    piece = 16 if cap % 32 == 0 else 8
    chunks = cap // (2 * piece)
    vmem = pl.BlockSpec(memory_space=pltpu.VMEM)
    smem = pl.BlockSpec(memory_space=pltpu.SMEM)
    hbm = pl.BlockSpec(memory_space=pltpu.HBM)
    f32 = jnp.float32
    dma = pltpu.SemaphoreType.DMA
    state, gathered, meta, taper_in, kinks, table, flag = pl.pallas_call(
        functools.partial(collect_kernel, tiles, layers, cap),
        out_shape=(
            jax.ShapeDtypeStruct((depth, members, width), f32),
            jax.ShapeDtypeStruct((chunks, devices, piece, LANES), f32),
            jax.ShapeDtypeStruct((4 * batches, count), f32),
            jax.ShapeDtypeStruct((4 * batches, count), f32),
            jax.ShapeDtypeStruct((LANES, LANES), f32),
            jax.ShapeDtypeStruct((devices, 3 * batches), jnp.int32),
            jax.ShapeDtypeStruct((1,), jnp.int32),
        ),
        in_specs=[hbm] * 9,
        out_specs=(hbm, vmem, vmem, vmem, vmem, vmem, smem),
        scratch_shapes=[
            pltpu.VMEM((depth, members, width), f32),
            dma,
            pltpu.VMEM((members, depth, width), f32),
            *[pltpu.VMEM((depth, width), f32)] * 4,
            *[pltpu.VMEM((batches, count), jnp.int32)] * 2,
            *[pltpu.VMEM((batches, count), f32)] * 2,
            dma((9,)),
            pltpu.VMEM((depth, members, width), f32),
            *[pltpu.VMEM((8, LANES), f32)] * 4,
            *[pltpu.VMEM((cap // 2, LANES), f32)] * 4,
            *[pltpu.VMEM((members, width), f32)] * 2,
            dma((6,)),
            dma((6,)),
            *[dma((chunks, max(line_n - 1, 1)))] * 2,
            *[dma((chunks, plane_n - 1))] * 2,
            *[dma((chunks,))] * 2,
        ],
        compiler_params=pltpu.CompilerParams(collective_id=1, has_side_effects=True, vmem_limit_bytes=48 * 2**20),
        name="collect",
    )(ensemble, diff_x, diff_z, cour_x, cour_z, obs_cell, obs_radius, obs_value, obs_var)

    def fast():
        return pl.pallas_call(
            functools.partial(apply_kernel, cap, width),
            out_shape=jax.ShapeDtypeStruct((members, depth, width), f32),
            in_specs=[smem, hbm, vmem, vmem, vmem, vmem],
            out_specs=vmem,
            scratch_shapes=[
                pltpu.VMEM((depth, members, width), f32),
                pltpu.VMEM((batches, members, count), f32),
                pltpu.VMEM((devices * cap + cap, LANES), f32),
                pltpu.VMEM((batches, count + cap, LANES), f32),
                dma,
            ],
            compiler_params=pltpu.CompilerParams(vmem_limit_bytes=48 * 2**20),
            name="apply",
        )(table, state, gathered, meta, taper_in, kinks)

    def slow():
        return slow_shards(ensemble, diff_x, diff_z, cour_x, cour_z, obs_cell, obs_radius, obs_value, obs_var)

    return lax.cond(flag[0] > 0, slow, fast)


def solution(mesh):
    in_specs = (
        P(None, "layer", "tile"),
        P("layer", "tile"),
        P("layer", "tile"),
        P("layer", "tile"),
        P("layer", "tile"),
        P(),
        P(),
        P(),
        P(),
    )
    out_specs = P(None, "layer", "tile")
    return jax.shard_map(shards, mesh=mesh, in_specs=in_specs, out_specs=out_specs, check_vma=False)
```

```python
import functools

import jax
import jax.numpy as jnp
from jax import lax
from jax.experimental import pallas as pl
from jax.experimental.pallas import tpu as pltpu
from jax.sharding import PartitionSpec as P

MESH = pl.DeviceIdType.MESH
LANES = 128


def split_cell(cells, total):
    if total & (total - 1) == 0:
        return cells >> (total.bit_length() - 1), cells & (total - 1)
    return cells // total, cells % total


def halves(value):
    high = value.astype(jnp.bfloat16)
    return high, (value - high.astype(jnp.float32)).astype(jnp.bfloat16)


def gather_kernel(
    tiles, layers, ens_in, dx_in, dz_in, cx_in, cz_in, cell_in, state_out, prior,
    state, state_sem, ens, diff_x, diff_z, cour_x, cour_z, obs_cell, load_sem,
    cells, edge_w, edge_e, halo_w, halo_e, halo_u, halo_d, coef_up, coef_down, coef_u, coef_d,
    part, in_core, in_plane, in_line, halo_send, halo_recv, core_sem, plane_send, plane_recv, line_send, line_recv,
):
    loads = []
    for i, (src, dst) in enumerate(
        ((ens_in, ens), (dz_in, diff_z), (cz_in, cour_z), (dx_in, diff_x), (cx_in, cour_x), (cell_in, obs_cell))
    ):
        copy = pltpu.make_async_copy(src, dst, load_sem.at[i])
        copy.start()
        loads.append(copy)
    members, depth, width = ens.shape
    batches, count = obs_cell.shape
    tile, layer = lax.axis_index("tile"), lax.axis_index("layer")
    core, row, line = tile % 2, (tile // 2) % 2, tile // 4
    plane_n, line_n = layers * 2, tiles // 4
    spot = layer * 2 + row
    pair = (tile + 1 - 2 * core, layer)

    def plane_at(index):
        return (line * 4 + (index % 2) * 2 + core, index // 2)

    def line_at(index):
        return (index * 4 + row * 2 + core, layer)

    greeted = [pair, ((tile + 1) % tiles, layer), ((tile + tiles - 1) % tiles, layer)]
    greeted += [(tile, (layer + 1) % layers), (tile, (layer + layers - 1) % layers)]
    greeted += [plane_at((spot + j) % plane_n) for j in range(1, plane_n)]
    greeted += [line_at((line + j) % line_n) for j in range(1, line_n)]
    barrier = pltpu.get_barrier_semaphore()
    for device in greeted:
        pl.semaphore_signal(barrier, inc=1, device_id=device, device_id_type=MESH)

    for copy in loads:
        copy.wait()
    lane = lax.broadcasted_iota(jnp.int32, (members, LANES), 1)
    west = jnp.zeros((members, LANES), jnp.float32)
    east = jnp.zeros((members, LANES), jnp.float32)
    for l in range(depth):
        x = ens[:, l, :]
        cells[l] = x
        west = jnp.where(lane == l, x[:, 0:1], west)
        east = jnp.where(lane == l, x[:, width - 1 : width], east)
    edge_w[...] = west
    edge_e[...] = east
    tall = coef_up.shape
    coef_up[...] = jnp.broadcast_to(diff_z[0:1, :] + 0.5 * cour_z[0:1, :], tall)
    coef_down[...] = jnp.broadcast_to(diff_z[depth - 1 : depth, :] - 0.5 * cour_z[depth - 1 : depth, :], tall)
    pl.semaphore_wait(barrier, len(greeted))

    def remote(src, dst, send, recv, device):
        return pltpu.make_async_remote_copy(
            src_ref=src, dst_ref=dst, send_sem=send, recv_sem=recv, device_id=device, device_id_type=MESH
        )

    up, down = layer > 0, layer < layers - 1
    before, after = tile > 0, tile < tiles - 1
    above, below = (tile, lax.rem(layer + layers - 1, layers)), (tile, lax.rem(layer + 1, layers))
    ahead, behind = (lax.rem(tile + 1, tiles), layer), (lax.rem(tile + tiles - 1, tiles), layer)

    def move(i, sends, receives, src, dst, device):
        return sends, receives, remote(src, dst, halo_send.at[i], halo_recv.at[i], device), dst

    small = (
        move(0, after, before, edge_e, halo_w, ahead),
        move(1, before, after, edge_w, halo_e, behind),
        move(2, down, up, coef_down, coef_u, below),
        move(3, up, down, coef_up, coef_d, above),
    )
    large = (
        move(4, down, up, cells.at[depth - 1], halo_u, below),
        move(5, up, down, cells.at[0], halo_d, above),
    )
    for sends, receives, copy, place in small:
        pl.when(sends)(copy.start)
    for sends, receives, copy, place in small + large:

        @pl.when(jnp.logical_not(receives))
        def _(place=place):
            place[...] = jnp.zeros_like(place)

    for sends, receives, copy, place in small:
        pl.when(receives)(copy.wait_recv)

    column = lax.broadcasted_iota(jnp.int32, (members, width), 1)
    levels = list(range(depth)) + [-1, depth]
    parts = []
    for l in range(depth):
        x = cells[l]
        left = jnp.where(column == 0, halo_w[:, l : l + 1], pltpu.roll(x, 1, 1))
        right = jnp.where(column == width - 1, halo_e[:, l : l + 1], pltpu.roll(x, width - 1, 1))
        dx, dz = diff_x[l : l + 1, :], diff_z[l : l + 1, :]
        cx, cz = 0.5 * cour_x[l : l + 1, :], 0.5 * cour_z[l : l + 1, :]
        new = x * (1.0 - 2.0 * dz - 2.0 * dx) + left * (dx + cx) + right * (dx - cx)
        if l > 0:
            new = new + cells[l - 1] * (dz + cz)
        if l < depth - 1:
            new = new + cells[l + 1] * (dz - cz)
        state[l] = new
        parts.extend(halves(new))
    parts.extend(halves(cells[0] * coef_u[0:1, :]))
    parts.extend(halves(cells[depth - 1] * coef_d[0:1, :]))
    stacked = jnp.concatenate(parts, axis=0)

    blocks = count // LANES
    extent = blocks * members
    half = extent // 2
    size = half // plane_n
    scatter = size % (8 * line_n) == 0
    piece = size // line_n if scatter else size
    place = lax.broadcasted_iota(jnp.int32, (width, count), 0)

    def start_of(b, *steps):
        total = b * extent
        for index, length in steps:
            total = total + index * length
        return pl.multiple_of(total, 8)

    every = range(batches)
    core_out, plane_out, line_out, line_back, plane_back, core_back = ([[] for _ in every] for _ in range(6))
    for b in every:
        rows, cols = split_cell(obs_cell[b : b + 1, :], tiles * width)
        rows, cols = rows - layer * depth, cols - tile * width
        hot = jnp.where(place == cols, 1.0, 0.0).astype(jnp.bfloat16)
        picked = jnp.dot(stacked, hot, preferred_element_type=jnp.float32)
        total = jnp.zeros((members, count), jnp.float32)
        for i, l in enumerate(levels):
            both = picked[2 * i * members : (2 * i + 1) * members] + picked[(2 * i + 1) * members : (2 * i + 2) * members]
            total = jnp.where(rows == l, both, total)
        for k in range(blocks):
            part[pl.ds((b * blocks + k) * members, members), :] = total[:, k * LANES : (k + 1) * LANES]
        copy = remote(part.at[pl.ds(start_of(b, (1 - core, half)), half)], in_core.at[b], core_sem.at[b, 0], core_sem.at[b, 1], pair)
        copy.start()
        core_out[b].append(copy)

    for b in every:
        core_out[b][0].wait_recv()
        part[pl.ds(start_of(b, (core, half)), half), :] += in_core[b]
        for j in range(1, plane_n):
            to = (spot + j) % plane_n
            copy = remote(
                part.at[pl.ds(start_of(b, (core, half), (to, size)), size)], in_plane.at[b, j - 1],
                plane_send.at[b, j - 1], plane_recv.at[b, j - 1], plane_at(to),
            )
            copy.start()
            plane_out[b].append(copy)
    for b in every:
        base = start_of(b, (core, half), (spot, size))
        total = part[pl.ds(base, size), :]
        for j in range(1, plane_n):
            plane_out[b][j - 1].wait_recv()
            total = total + in_plane[b, j - 1]
        part[pl.ds(base, size), :] = total
        for j in range(1, line_n):
            to = (line + j) % line_n
            start = start_of(b, (core, half), (spot, size), (to, piece)) if scatter else base
            copy = remote(part.at[pl.ds(start, piece)], in_line.at[b, j - 1], line_send.at[b, j - 1], line_recv.at[b, j - 1], line_at(to))
            copy.start()
            line_out[b].append(copy)
    for sends, receives, copy, _ in large:
        pl.when(sends)(copy.start)

    def spread_plane(b):
        view = prior.at[pl.ds(start_of(b, (core, half), (spot, size)), size)]
        for j in range(1, plane_n):
            k = plane_n - 1 + j - 1
            copy = remote(view, view, plane_send.at[b, k], plane_recv.at[b, k], plane_at((spot + j) % plane_n))
            copy.start()
            plane_back[b].append(copy)

    for b in every:
        own = start_of(b, (core, half), (spot, size), (line, piece)) if scatter else start_of(b, (core, half), (spot, size))
        total = part[pl.ds(own, piece), :]
        for j in range(1, line_n):
            line_out[b][j - 1].wait_recv()
            total = total + in_line[b, j - 1]
        prior[pl.ds(own, piece), :] = total
        if scatter:
            view = prior.at[pl.ds(own, piece)]
            for j in range(1, line_n):
                k = line_n - 1 + j - 1
                copy = remote(view, view, line_send.at[b, k], line_recv.at[b, k], line_at((line + j) % line_n))
                copy.start()
                line_back[b].append(copy)
        else:
            spread_plane(b)
    if scatter:
        for b in every:
            for copy in line_back[b]:
                copy.wait_recv()
            spread_plane(b)

    for sends, receives, copy, _ in large:
        pl.when(receives)(copy.wait_recv)
    state[0] += halo_u[...] * (diff_z[0:1, :] + 0.5 * cour_z[0:1, :])
    state[depth - 1] += halo_d[...] * (diff_z[depth - 1 : depth, :] - 0.5 * cour_z[depth - 1 : depth, :])
    keep = pltpu.make_async_copy(state, state_out, state_sem)
    keep.start()

    for b in every:
        for copy in plane_back[b]:
            copy.wait_recv()
        view = prior.at[pl.ds(start_of(b, (core, half)), half)]
        copy = remote(view, view, core_sem.at[b, 2], core_sem.at[b, 3], pair)
        copy.start()
        core_back[b].append(copy)
    for b in every:
        core_back[b][0].wait_recv()
    for group in (core_out, plane_out, line_out, line_back, plane_back, core_back):
        for copies in group:
            for copy in copies:
                copy.wait_send()
    for sends, receives, copy, _ in small + large:
        pl.when(sends)(copy.wait_send)
    keep.wait()


def update_kernel(
    total_cols, width, state_in, prior_in, cell_in, radius_in, value_in, var_in, out,
    layers_ref, later_ref, prior, obs_cell, obs_radius, obs_value, obs_var, load_sem,
):
    loads = []
    for i, (src, dst) in enumerate(
        (
            (cell_in, obs_cell), (radius_in, obs_radius), (value_in, obs_value), (var_in, obs_var),
            (prior_in, prior), (state_in, layers_ref),
        )
    ):
        copy = pltpu.make_async_copy(src, dst, load_sem.at[i])
        copy.start()
        loads.append(copy)
    depth, members, _ = layers_ref.shape
    batches, count = obs_cell.shape
    blocks = count // LANES
    first = lax.axis_index("tile") * width
    for copy in loads[:-1]:
        copy.wait()
    for b in range(batches):
        for k in range(blocks):
            later_ref[b, :, k * LANES : (k + 1) * LANES] = prior[pl.ds((b * blocks + k) * members, members), :]
    centre = split_cell(obs_cell[...], total_cols)[1].astype(jnp.float32)
    inverse = 1.0 / obs_radius[...].astype(jnp.float32)
    upright = jnp.concatenate([centre, inverse], axis=0).T
    grid = (first + lax.broadcasted_iota(jnp.int32, (1, width), 1)).astype(jnp.float32)

    for b in range(batches):
        y = later_ref[b]
        value, variance = obs_value[b : b + 1, :], obs_var[b : b + 1, :]
        ymean = jnp.sum(y, axis=0, keepdims=True) * (1.0 / members)
        anomaly = y - ymean
        spread = jnp.sum(anomaly * anomaly, axis=0, keepdims=True) / (members - 1) + 1e-06
        shrink = variance / (spread + variance)
        postmean = spread * shrink * (ymean / spread + value / variance)
        delta = (postmean - ymean) + (jnp.sqrt(shrink) - 1.0) * anomaly
        delta = delta * (1.0 / ((members - 1) * spread))
        d_high, d_low = halves(delta)
        d_both = jnp.concatenate([d_high, d_low], axis=0)
        y_high = anomaly.astype(jnp.bfloat16).astype(jnp.float32)
        y_low = anomaly - y_high
        lhs = jnp.concatenate([y_high, y_high, y_low, y_low], axis=0).T.astype(jnp.bfloat16)
        here, scale = upright[:, b : b + 1], upright[:, batches + b : batches + b + 1]

        def taper(positions):
            frac = jnp.maximum(1.0 - jnp.abs(positions - here) * scale, 0.0)
            return frac * frac

        def change(x, weight):
            x_high, x_low = halves(x - jnp.sum(x, axis=0, keepdims=True) * (1.0 / members))
            rhs = jnp.concatenate([x_high, x_low, x_high, x_low], axis=0)
            gain = jnp.dot(lhs, rhs, preferred_element_type=jnp.float32) * weight
            g_high, g_low = halves(gain)
            one = jnp.dot(d_both, g_high, preferred_element_type=jnp.float32)
            two = jnp.dot(d_high, g_low, preferred_element_type=jnp.float32)
            return one[:members] + one[members:] + two

        for c in range(b + 1, batches):
            later_ref[c] += change(later_ref[c], taper(centre[c : c + 1, :]))
        weight = taper(grid)
        if b == 0:
            loads[-1].wait()
        for l in range(depth):
            x = layers_ref[l]
            x = x + change(x, weight)
            if b == batches - 1:
                out[:, l, :] = x
            else:
                layers_ref[l] = x


def divide(values, size):
    return values >> (size.bit_length() - 1) if size & (size - 1) == 0 else values // size


def dot_rows(a, b):
    return lax.dot_general(a, b, (((1,), (1,)), ((), ())), preferred_element_type=jnp.float32)


def remote(src, dst, send, recv, device):
    return pltpu.make_async_remote_copy(
        src_ref=src, dst_ref=dst, send_sem=send, recv_sem=recv, device_id=device, device_id_type=MESH
    )


def collect_kernel(
    tiles, layers, cap, cuts, bends, ens_in, dx_in, dz_in, cx_in, cz_in, cell_in, radius_in, value_in, var_in,
    state_out, flat, meta, taper_in, kinks, tapers, table, flag,
    state, state_sem, ens, diff_x, diff_z, cour_x, cour_z, obs_cell, obs_radius, obs_value, obs_var, load_sem,
    cells, edge_w, edge_e, halo_w, halo_e, near_u, near_d, part_u, part_d, halo_u, halo_d,
    gathered, hop_send, hop_recv, line_send, line_recv, plane_send, plane_recv, core_send, core_recv,
):
    loads = []
    for i, (src, dst) in enumerate(
        (
            (cell_in, obs_cell), (ens_in, ens), (dz_in, diff_z), (cz_in, cour_z), (dx_in, diff_x), (cx_in, cour_x),
            (radius_in, obs_radius), (value_in, obs_value), (var_in, obs_var),
        )
    ):
        copy = pltpu.make_async_copy(src, dst, load_sem.at[i])
        copy.start()
        loads.append(copy)
    members, depth, width = ens.shape
    batches, count = obs_cell.shape
    chunks, devices, piece, _ = gathered.shape
    f32, bf16 = jnp.float32, jnp.bfloat16
    tile, layer = lax.axis_index("tile"), lax.axis_index("layer")
    core, row, line = tile % 2, (tile // 2) % 2, tile // 4
    plane_n, line_n = layers * 2, tiles // 4
    spot = layer * 2 + row
    pair = (tile + 1 - 2 * core, layer)

    def plane_at(index):
        return (line * 4 + (index % 2) * 2 + core, index // 2)

    def line_at(index):
        return (index * 4 + row * 2 + core, layer)

    above, below = (tile, lax.rem(layer + layers - 1, layers)), (tile, lax.rem(layer + 1, layers))
    ahead, behind = (lax.rem(tile + 1, tiles), layer), (lax.rem(tile + tiles - 1, tiles), layer)
    greeted = [pair, ahead, behind, below, above]
    greeted += [plane_at((spot + j) % plane_n) for j in range(1, plane_n)]
    greeted += [line_at((line + j) % line_n) for j in range(1, line_n)]
    barrier = pltpu.get_barrier_semaphore()
    for device in greeted:
        pl.semaphore_signal(barrier, inc=1, device_id=device, device_id_type=MESH)

    loads[0].wait()
    cell_row, cell_col = split_cell(obs_cell[...], tiles * width)
    cell_tile, cell_layer = divide(cell_col, width), divide(cell_row, depth)
    local_col, local_row = cell_col - cell_tile * width, cell_row - cell_layer * depth
    here = cell_tile == tile
    groups = [
        jnp.where(jnp.logical_and(here, cell_layer == layer + step), 1.0, 0.0) for step in (0, -1, 1)
    ]
    masks = jnp.concatenate(groups + [jnp.zeros_like(groups[0])], axis=0).astype(bf16)
    first = lax.broadcasted_iota(jnp.int32, (count, count), 0)
    second = lax.broadcasted_iota(jnp.int32, (count, count), 1)
    running = jnp.dot(masks, jnp.where(first <= second, 1.0, 0.0).astype(bf16), preferred_element_type=f32)
    code = (local_row * width + local_col + 1).astype(f32)
    slot = lax.broadcasted_iota(jnp.int32, (cap, count), 0).astype(f32)
    lane_w = lax.broadcasted_iota(jnp.int32, (cap, width), 1)
    found = []
    for k, edge in enumerate((None, depth - 1, 0)):
        before_ = jnp.zeros((1, 1), f32)
        total = jnp.zeros((cap, count), f32)
        for b in range(batches):
            i = k * batches + b
            wanted = groups[k][b : b + 1, :] > 0.5
            if edge is not None:
                wanted = jnp.logical_and(wanted, local_row[b : b + 1, :] == edge)
            rank = jnp.where(wanted, running[i : i + 1, :] + (before_ - 1.0), -1.0)
            total = total + jnp.where(rank == slot, code[b : b + 1, :], 0.0)
            before_ = before_ + running[i : i + 1, count - 1 : count]
        cell = jnp.sum(total, axis=1, keepdims=True).astype(jnp.int32) - 1
        at_row = divide(cell, width)
        at_col = jnp.where(cell >= 0, cell - at_row * width, -1)
        found.append((at_row, at_col, jnp.where(lane_w == at_col, 1.0, 0.0)))

    low = lax.broadcasted_iota(jnp.int32, (piece, LANES), 1) < members

    def packed(values):
        out = []
        for k in range(chunks):
            base = 2 * piece * k
            out.append(jnp.where(low, values[base : base + piece], values[base + piece : base + 2 * piece]))
        return out

    def doubled(values):
        return values + pltpu.roll(values, members, 1)

    for copy in loads[1:6]:
        copy.wait()
    lane = lax.broadcasted_iota(jnp.int32, (members, LANES), 1)
    west = jnp.zeros((members, LANES), f32)
    east = jnp.zeros((members, LANES), f32)
    for l in range(depth):
        x = ens[:, l, :]
        cells[l] = x
        west = jnp.where(lane == l, x[:, 0:1], west)
        east = jnp.where(lane == l, x[:, width - 1 : width], east)
    edge_w[...] = jnp.concatenate([west, west], axis=0).T[:8]
    edge_e[...] = jnp.concatenate([east, east], axis=0).T[:8]
    for ref, k, l in ((part_u, 1, 0), (part_d, 2, depth - 1)):
        raw = jnp.concatenate(halves(cells[l]), axis=0)
        for i, rows in enumerate(packed(doubled(dot_rows(found[k][2].astype(bf16), raw)))):
            ref[i * piece : (i + 1) * piece, :] = rows
    pl.semaphore_wait(barrier, len(greeted))

    up, down = layer > 0, layer < layers - 1
    before, after = tile > 0, tile < tiles - 1

    def move(i, sends, receives, src, dst, device):
        return sends, receives, remote(src, dst, hop_send.at[i], hop_recv.at[i], device), dst

    small = (
        move(0, down, up, part_d, near_u, below),
        move(1, up, down, part_u, near_d, above),
        move(2, after, before, edge_e, halo_w, ahead),
        move(3, before, after, edge_w, halo_e, behind),
    )
    large = (
        move(4, down, up, cells.at[depth - 1], halo_u, below),
        move(5, up, down, cells.at[0], halo_d, above),
    )
    for sends, receives, copy, place in small:
        pl.when(sends)(copy.start)
    for sends, receives, copy, place in small + large:

        @pl.when(jnp.logical_not(receives))
        def _(place=place):
            place[...] = jnp.zeros_like(place)

    at_row, at_col, hot = found[0]
    column = lax.broadcasted_iota(jnp.int32, (members, width), 1)
    total = jnp.zeros((cap, LANES), f32)
    for l in range(depth):
        x = cells[l]
        left = jnp.where(column == 0, 0.0, pltpu.roll(x, 1, 1))
        right = jnp.where(column == width - 1, 0.0, pltpu.roll(x, width - 1, 1))
        dx, dz = diff_x[l : l + 1, :], diff_z[l : l + 1, :]
        cx, cz = 0.5 * cour_x[l : l + 1, :], 0.5 * cour_z[l : l + 1, :]
        new = x * (1.0 - 2.0 * dz - 2.0 * dx) + left * (dx + cx) + right * (dx - cx)
        if l > 0:
            new = new + cells[l - 1] * (dz + cz)
        if l < depth - 1:
            new = new + cells[l + 1] * (dz - cz)
        state[l] = new
        picked = dot_rows(hot.astype(bf16), jnp.concatenate(halves(new), axis=0))
        total = total + jnp.where(at_row == l, picked, 0.0)
    mine = packed(doubled(total))
    coef_u = diff_z[0:1, :] + 0.5 * cour_z[0:1, :]
    coef_d = diff_z[depth - 1 : depth, :] - 0.5 * cour_z[depth - 1 : depth, :]
    take_u = jnp.where(at_row == 0, jnp.sum(hot * coef_u, axis=1, keepdims=True), 0.0)
    take_d = jnp.where(at_row == depth - 1, jnp.sum(hot * coef_d, axis=1, keepdims=True), 0.0)
    coef_w = diff_x[:, 0:1] + 0.5 * cour_x[:, 0:1]
    coef_e = diff_x[:, width - 1 : width] - 0.5 * cour_x[:, width - 1 : width]
    weights = [packed(jnp.broadcast_to(take, (cap, LANES))) for take in (take_u, take_d)]
    sides = []
    for at, coef in ((0, coef_w), (width - 1, coef_e)):
        for l in range(depth):
            take = jnp.where(jnp.logical_and(at_row == l, at_col == at), coef[l : l + 1, :], 0.0)
            sides.append(packed(jnp.broadcast_to(take, (cap, LANES))))

    for sends, receives, copy, place in small:
        pl.when(receives)(copy.wait_recv)
    me = (core * plane_n + spot) * line_n + line
    line_out, plane_out, core_out = ([[] for _ in range(chunks)] for _ in range(3))
    for k in range(chunks):
        rows = pl.ds(k * piece, piece)
        value = mine[k] + weights[0][k] * near_u[rows, :] + weights[1][k] * near_d[rows, :]
        for l in range(depth):
            value = value + sides[l][k] * halo_w[l : l + 1, :] + sides[depth + l][k] * halo_e[l : l + 1, :]
        gathered[k, me] = value
        view = gathered.at[k, me]
        for j in range(1, line_n):
            copy = remote(view, view, line_send.at[k, j - 1], line_recv.at[k, j - 1], line_at((line + j) % line_n))
            copy.start()
            line_out[k].append(copy)
    for sends, receives, copy, _ in large:
        pl.when(sends)(copy.start)

    for ref, coef, at in ((halo_w, coef_w, 0), (halo_e, coef_e, width - 1)):
        base = at // LANES * LANES
        block = lax.broadcasted_iota(jnp.int32, (members, LANES), 1)
        turned = jnp.concatenate([ref[...]] * (LANES // 8), axis=0).T[:members]
        for l in range(depth):
            term = turned[:, l : l + 1] * coef[l : l + 1, :]
            state[l, :, base : base + LANES] += jnp.where(block == at - base, term, 0.0)

    for copy in loads[6:]:
        copy.wait()
    core_of, row_of, line_of = cell_tile & 1, divide(cell_tile, 2) & 1, divide(cell_tile, 4)
    owner = (core_of * plane_n + cell_layer * 2 + row_of) * line_n + line_of
    key = (owner * count + lax.broadcasted_iota(jnp.int32, (batches, count), 1)).astype(f32)
    upright = jnp.concatenate([key, jnp.zeros_like(key)], axis=0).T

    def pieces(values, n):
        out = []
        for _ in range(n):
            high = values.astype(bf16).astype(f32)
            out.append(high)
            values = values - high
        return out

    fields = (
        (cell_col.astype(f32), 2), (obs_radius[...].astype(f32), 2), (obs_value[...], 3), (obs_var[...], 3)
    )
    parts = []
    for values, n in fields:
        parts.extend(pieces(values, n))
    devices_at = lax.broadcasted_iota(jnp.int32, (devices, count), 0)
    cuts_at = lax.broadcasted_iota(jnp.int32, (tiles * cuts, count), 0)
    ends = [divide(cell_col + obs_radius[...] * step, width // cuts) for step in (-1, 0, 1)]
    used = jnp.zeros((devices, 1), f32)
    worst = jnp.zeros((tiles * cuts, 1), f32)
    longest = jnp.zeros((devices, 1), f32)
    if len(parts) * batches % 16:
        parts.append(jnp.zeros((16 - len(parts) * batches % 16, count), f32))
    parts = jnp.concatenate(parts, axis=0).astype(bf16)
    place = first.astype(f32)
    for b in range(batches):
        less = jnp.where(upright[:, b : b + 1] < key[b : b + 1, :], 1.0, 0.0)
        position = jnp.sum(less, axis=0, keepdims=True)
        order = jnp.where(place == position, 1.0, 0.0).astype(bf16)
        ordered = dot_rows(parts, order)
        i = 0
        for f, (_, n) in enumerate(fields):
            total = ordered[i * batches + b : i * batches + b + 1, :]
            for p in range(1, n):
                total = total + ordered[(i + p) * batches + b : (i + p) * batches + b + 1, :]
            meta[f * batches + b : f * batches + b + 1, :] = total
            i += n
        holder = owner[b : b + 1, :]
        length = jnp.sum(jnp.where(holder == devices_at, 1.0, 0.0), axis=1, keepdims=True)
        start = jnp.sum(jnp.where(holder < devices_at, 1.0, 0.0), axis=1, keepdims=True)
        table[:, b : b + 1] = length.astype(jnp.int32)
        table[:, batches + b : batches + b + 1] = start.astype(jnp.int32)
        table[:, 2 * batches + b : 2 * batches + b + 1] = used.astype(jnp.int32)
        used = used + length
        longest = jnp.maximum(longest, length)
        bent = jnp.zeros((tiles * cuts, count), f32)
        for end in ends:
            bent = bent + jnp.where(end[b : b + 1, :] == cuts_at, 1.0, 0.0)
        worst = jnp.maximum(worst, jnp.sum(bent, axis=1, keepdims=True))
    longest = jnp.max(longest, axis=0, keepdims=True)
    table[:, 3 * batches : 3 * batches + 1] = jnp.broadcast_to(longest, (devices, 1)).astype(jnp.int32)
    over = jnp.logical_or(jnp.max(used) > cap, jnp.max(worst) > bends)
    flag[0] = over.astype(jnp.int32)

    for k in range(chunks):
        for copy in line_out[k]:
            copy.wait_recv()
        view = gathered.at[k, pl.ds((core * plane_n + spot) * line_n, line_n)]
        for j in range(1, plane_n):
            copy = remote(view, view, plane_send.at[k, j - 1], plane_recv.at[k, j - 1], plane_at((spot + j) % plane_n))
            copy.start()
            plane_out[k].append(copy)

    part_w = width // cuts
    middle = (part_w - 1) / 2
    centre, radius = meta[0:batches, :], meta[batches : 2 * batches, :]
    inverse = 1.0 / radius
    near, far = centre - radius, centre + radius
    bent = []
    for c in range(cuts):
        lowest = (tile * width + c * part_w).astype(f32)
        highest = lowest + (part_w - 1)
        right_of, left_of = centre <= lowest, centre >= highest
        smooth = jnp.logical_or(
            jnp.logical_and(right_of, far >= highest), jnp.logical_and(left_of, near <= lowest)
        )
        away = jnp.logical_or(jnp.logical_and(right_of, far <= lowest), jnp.logical_and(left_of, near >= highest))
        bent.append(jnp.where(jnp.logical_or(smooth, away), 0.0, 1.0))
        value = jnp.where(smooth, 1.0 - jnp.abs(lowest + middle - centre) * inverse, 0.0)
        slope = jnp.where(smooth, jnp.where(right_of, -middle, middle) * inverse, 0.0)
        for i, rows in enumerate((value * value, 2.0 * value * slope, slope * slope)):
            start = (c * 4 + i) * batches
            taper_in[start : start + batches, :] = rows
    padded = jnp.concatenate(bent + [jnp.zeros_like(centre)] * (-cuts % (16 // batches)), axis=0).astype(bf16)
    counted = jnp.dot(padded, jnp.where(first <= second, 1.0, 0.0).astype(bf16), preferred_element_type=f32)
    ranks = []
    for c in range(cuts):
        ranks.append(jnp.where(bent[c] > 0.5, counted[c * batches : (c + 1) * batches] - 1.0, -1.0))
        taper_in[(c * 4 + 3) * batches : (c * 4 + 4) * batches, :] = ranks[c]
    parts = pieces(centre, 2) + pieces(inverse, 3)
    parts = jnp.concatenate(parts + [jnp.zeros_like(centre)] * (-len(parts) % (16 // batches)), axis=0).astype(bf16)
    kink_row = lax.broadcasted_iota(jnp.int32, (bends, count), 0).astype(f32)
    grid = (tile * width + lax.broadcasted_iota(jnp.int32, (1, width), 1)).astype(f32)

    def bump(positions, here, scale):
        frac = jnp.maximum(1.0 - jnp.abs(positions - here) * scale, 0.0)
        return frac * frac

    for b in range(batches):
        choose = [jnp.where(kink_row == ranks[c][b : b + 1, :], 1.0, 0.0).astype(bf16) for c in range(cuts)]
        ordered = dot_rows(jnp.concatenate(choose, axis=0), parts)
        at = [ordered[:, p * batches + b : p * batches + b + 1] for p in range(5)]
        kink_c, kink_i = at[0] + at[1], at[2] + at[3] + at[4]
        for c in range(cuts):
            rows = slice(c * bends, (c + 1) * bends)
            kinks[b, c] = bump(grid[:, c * part_w : (c + 1) * part_w], kink_c[rows], kink_i[rows])
    upright = jnp.concatenate([centre, inverse], axis=0).T
    i = 0
    for b in range(batches):
        for c in range(b + 1, batches):
            tapers[i] = bump(centre[c : c + 1, :], upright[:, b : b + 1], upright[:, batches + b : batches + b + 1])
            i += 1

    for sends, receives, copy, _ in large:
        pl.when(receives)(copy.wait_recv)
    state[0] += halo_u[...] * coef_u
    state[depth - 1] += halo_d[...] * coef_d
    keep = pltpu.make_async_copy(state, state_out, state_sem)
    keep.start()

    def unpack(k, side):
        for i in range(devices // 2):
            g = side * (devices // 2) + i
            rows = gathered[k, g]
            at = pl.multiple_of(g * cap + 2 * piece * k, 8)
            flat[pl.ds(at, piece), :] = rows
            flat[pl.ds(at + piece, piece), :] = pltpu.roll(rows, members, 1)

    for k in range(chunks):
        for copy in plane_out[k]:
            copy.wait_recv()
        view = gathered.at[k, pl.ds(core * plane_n * line_n, plane_n * line_n)]
        copy = remote(view, view, core_send.at[k], core_recv.at[k], pair)
        copy.start()
        core_out[k].append(copy)
        unpack(k, core)
    for k in range(chunks):
        core_out[k][0].wait_recv()
        unpack(k, 1 - core)
    for group in (line_out, plane_out, core_out):
        for copies in group:
            for copy in copies:
                copy.wait_send()
    for sends, receives, copy, _ in small + large:
        pl.when(sends)(copy.wait_send)
    keep.wait()


def apply_kernel(
    cap, table, state_in, flat, meta, taper_in, kinks, tapers, out, layers_ref, later_ref, ordered, load_sem,
):
    load = pltpu.make_async_copy(state_in, layers_ref, load_sem)
    load.start()
    depth, members, _ = layers_ref.shape
    batches, _, count = later_ref.shape
    devices = table.shape[0]
    mean = count / devices
    run = min(cap, -int(-(mean + 4.0 * mean**0.5) // 8) * 8)

    def spread(size):
        def step(g, carry):
            for b in range(batches):
                dst, src = table[g, batches + b], g * cap + table[g, 2 * batches + b]
                for i in range(0, size, 8):
                    ordered[b, pl.ds(dst + i, 8), :] = flat[pl.ds(src + i, 8), :]
            return carry

        return step

    lax.fori_loop(0, devices, spread(run), 0, unroll=4)

    @pl.when(table[0, 3 * batches] > run)
    def _():
        lax.fori_loop(0, devices, spread(cap), 0)

    for b in range(batches):
        later_ref[b] = ordered[b, :count, :].T[:members]
    _, cuts, bends, part_w = kinks.shape
    middle = (part_w - 1) / 2
    offset = lax.broadcasted_iota(jnp.int32, (1, part_w), 1).astype(jnp.float32)
    ratio = (offset - middle) * (1.0 / middle)
    ratio = jnp.concatenate([ratio] * depth, axis=1)
    third = 3 * members
    both_low = lax.broadcasted_iota(jnp.int32, (third, LANES), 1) < members
    low = lax.broadcasted_iota(jnp.int32, (2 * members, LANES), 1) < members
    top = lax.broadcasted_iota(jnp.int32, (2 * members, LANES), 0) < members
    kink_row = lax.broadcasted_iota(jnp.int32, (bends, count), 0).astype(jnp.float32)
    pair = 0

    for b in range(batches):
        y = later_ref[b]
        value, variance = meta[2 * batches + b : 2 * batches + b + 1, :], meta[3 * batches + b : 3 * batches + b + 1, :]
        ymean = jnp.sum(y, axis=0, keepdims=True) * (1.0 / members)
        anomaly = y - ymean
        spread = jnp.sum(anomaly * anomaly, axis=0, keepdims=True) / (members - 1) + 1e-06
        shrink = variance / (spread + variance)
        postmean = spread * shrink * (ymean / spread + value / variance)
        delta = (postmean - ymean) + (jnp.sqrt(shrink) - 1.0) * anomaly
        delta = delta * (1.0 / ((members - 1) * spread))
        d_high, d_low = halves(delta)
        d_both = jnp.concatenate([d_high, d_low], axis=0)
        y_high = anomaly.astype(jnp.bfloat16).astype(jnp.float32)
        y_low = anomaly - y_high
        y_both = jnp.concatenate([y_high, y_low], axis=0).astype(jnp.bfloat16)

        def stack(x):
            x_high, x_low = halves(x - jnp.sum(x, axis=0, keepdims=True) * (1.0 / members))
            return jnp.concatenate([x_high, x_high, x_low, x_low], axis=0)

        def twice(x):
            return jnp.concatenate([x, x], axis=1).astype(jnp.bfloat16)

        if b < batches - 1:
            lhs = twice(jnp.concatenate([y_high, y_low], axis=0).T)
        rest = range(b + 1, batches)
        crosses = [jnp.dot(lhs, stack(later_ref[c]), preferred_element_type=jnp.float32) for c in rest]
        gains = [halves(cross * tapers[pair + i]) for i, cross in enumerate(crosses)]
        pair += len(rest)
        ones = [jnp.dot(d_both, high, preferred_element_type=jnp.float32) for high, _ in gains]
        twos = [jnp.dot(d_high, lower, preferred_element_type=jnp.float32) for _, lower in gains]
        for i, c in enumerate(rest):
            later_ref[c] += ones[i][:members] + ones[i][members:] + twos[i]

        scaled = []
        for c in range(cuts):
            for i in range(3):
                row = (c * 4 + i) * batches + b
                scaled.append(delta * taper_in[row : row + 1, :])
        moments = dot_rows(jnp.concatenate(halves(jnp.concatenate(scaled, axis=0)), axis=0), y_both)
        choose = []
        for c in range(cuts):
            row = (c * 4 + 3) * batches + b
            choose.append(jnp.where(kink_row == taper_in[row : row + 1, :], 1.0, 0.0).astype(jnp.bfloat16))
        choose = jnp.concatenate(choose, axis=0)
        y_kink = dot_rows(choose, y_both)
        d_kink = dot_rows(d_both, choose)
        turned = pltpu.roll(d_kink, members, 1)
        lefts, rights = [], []
        if b == 0:
            load.wait()
        for c in range(cuts):
            moment = moments[c * third : (c + 1) * third] + moments[(cuts + c) * third : (cuts + c + 1) * third]
            m_high, m_low = halves(moment + pltpu.roll(moment, members, 1))
            moment = jnp.where(both_low, m_high.astype(jnp.float32), m_low.astype(jnp.float32))
            left = twice(jnp.concatenate([moment, y_kink[c * bends : (c + 1) * bends]], axis=0))
            if cuts == 1:
                right = jnp.concatenate([d_kink, jnp.where(top, d_kink, 0.0)], axis=1)
            elif c == 0:
                right = jnp.where(low, d_kink, jnp.where(top, turned, 0.0))
            else:
                right = jnp.where(low, turned, jnp.where(top, d_kink, 0.0))
            right = right.astype(jnp.bfloat16)
            lefts.append(left)
            rights.append(right)
        olds, firsts, gains, seconds = [], [], [], []
        for c in range(cuts):
            columns = slice(c * part_w, (c + 1) * part_w)
            olds.append(jnp.concatenate([layers_ref[l, :, columns] for l in range(depth)], axis=1))
            firsts.append(jnp.dot(lefts[c], stack(olds[c]), preferred_element_type=jnp.float32))
        for c in range(cuts):
            weight = jnp.concatenate([kinks[b, c]] * depth, axis=1)
            gains.append(jnp.concatenate(halves(firsts[c][third:] * weight), axis=0))
        for c in range(cuts):
            seconds.append(jnp.dot(rights[c], gains[c], preferred_element_type=jnp.float32))
        for c in range(cuts):
            both, more = firsts[c], seconds[c]
            x = olds[c] + (both[:members] + ratio * (both[members : 2 * members] + ratio * both[2 * members : third]))
            x = x + (more[:members] + more[members:])
            columns = slice(c * part_w, (c + 1) * part_w)
            for l in range(depth):
                if b == batches - 1:
                    out[:, l, columns] = x[:, l * part_w : (l + 1) * part_w]
                else:
                    layers_ref[l, :, columns] = x[:, l * part_w : (l + 1) * part_w]


def slow_shards(ensemble, diff_x, diff_z, cour_x, cour_z, obs_cell, obs_radius, obs_value, obs_var):
    members, depth, width = ensemble.shape
    batches, count = obs_cell.shape
    tiles, layers = lax.axis_size("tile"), lax.axis_size("layer")
    rows = batches * count * members // LANES
    plane_n, line_n = layers * 2, tiles // 4
    half = rows // batches // 2
    size = half // plane_n
    piece = size // line_n if size % (8 * line_n) == 0 else size
    vmem = pl.BlockSpec(memory_space=pltpu.VMEM)
    hbm = pl.BlockSpec(memory_space=pltpu.HBM)
    f32 = jnp.float32
    dma = pltpu.SemaphoreType.DMA
    state, prior = pl.pallas_call(
        functools.partial(gather_kernel, tiles, layers),
        out_shape=(jax.ShapeDtypeStruct((depth, members, width), f32), jax.ShapeDtypeStruct((rows, LANES), f32)),
        in_specs=[hbm] * 6,
        out_specs=(hbm, vmem),
        scratch_shapes=[
            pltpu.VMEM((depth, members, width), f32),
            dma,
            pltpu.VMEM((members, depth, width), f32),
            *[pltpu.VMEM((depth, width), f32)] * 4,
            pltpu.VMEM((batches, count), jnp.int32),
            dma((6,)),
            pltpu.VMEM((depth, members, width), f32),
            *[pltpu.VMEM((members, LANES), f32)] * 4,
            *[pltpu.VMEM((members, width), f32)] * 2,
            *[pltpu.VMEM((8, width), f32)] * 4,
            pltpu.VMEM((rows, LANES), f32),
            pltpu.VMEM((batches, half, LANES), f32),
            pltpu.VMEM((batches, plane_n - 1, size, LANES), f32),
            pltpu.VMEM((batches, line_n - 1, piece, LANES), f32),
            dma((6,)),
            dma((6,)),
            dma((batches, 4)),
            dma((batches, 2 * plane_n - 2)),
            dma((batches, 2 * plane_n - 2)),
            dma((batches, 2 * line_n - 2)),
            dma((batches, 2 * line_n - 2)),
        ],
        compiler_params=pltpu.CompilerParams(collective_id=0, has_side_effects=True, vmem_limit_bytes=63 * 2**20),
        name="gather_prior",
    )(ensemble, diff_x, diff_z, cour_x, cour_z, obs_cell)
    return pl.pallas_call(
        functools.partial(update_kernel, tiles * width, width),
        out_shape=jax.ShapeDtypeStruct((members, depth, width), f32),
        in_specs=[hbm] * 6,
        out_specs=vmem,
        scratch_shapes=[
            pltpu.VMEM((depth, members, width), f32),
            pltpu.VMEM((batches, members, count), f32),
            pltpu.VMEM((rows, LANES), f32),
            *[pltpu.VMEM((batches, count), jnp.int32)] * 2,
            *[pltpu.VMEM((batches, count), f32)] * 2,
            dma((6,)),
        ],
        compiler_params=pltpu.CompilerParams(vmem_limit_bytes=63 * 2**20),
        name="update",
    )(state, prior, obs_cell, obs_radius, obs_value, obs_var)


def shards(ensemble, diff_x, diff_z, cour_x, cour_z, obs_cell, obs_radius, obs_value, obs_var):
    members, depth, width = ensemble.shape
    batches, count = obs_cell.shape
    tiles, layers = lax.axis_size("tile"), lax.axis_size("layer")
    devices = tiles * layers
    plane_n, line_n = layers * 2, tiles // 4
    mean = batches * count / devices
    cap = -int(-(mean + 4.0 * mean**0.5) // 16) * 16
    piece = 16 if cap % 32 == 0 else 8
    chunks = cap // (2 * piece)
    cuts, bends = (2, 64) if width % (2 * LANES) == 0 else (1, LANES)
    vmem = pl.BlockSpec(memory_space=pltpu.VMEM)
    smem = pl.BlockSpec(memory_space=pltpu.SMEM)
    hbm = pl.BlockSpec(memory_space=pltpu.HBM)
    f32 = jnp.float32
    dma = pltpu.SemaphoreType.DMA
    state, flat, meta, taper_in, kinks, tapers, table, flag = pl.pallas_call(
        functools.partial(collect_kernel, tiles, layers, cap, cuts, bends),
        out_shape=(
            jax.ShapeDtypeStruct((depth, members, width), f32),
            jax.ShapeDtypeStruct((devices * cap + cap, LANES), f32),
            jax.ShapeDtypeStruct((4 * batches, count), f32),
            jax.ShapeDtypeStruct((cuts * 4 * batches, count), f32),
            jax.ShapeDtypeStruct((batches, cuts, bends, width // cuts), f32),
            jax.ShapeDtypeStruct((batches * (batches - 1) // 2, count, count), f32),
            jax.ShapeDtypeStruct((devices, 3 * batches + 1), jnp.int32),
            jax.ShapeDtypeStruct((1,), jnp.int32),
        ),
        in_specs=[hbm] * 9,
        out_specs=(hbm, vmem, vmem, vmem, vmem, vmem, vmem, smem),
        scratch_shapes=[
            pltpu.VMEM((depth, members, width), f32),
            dma,
            pltpu.VMEM((members, depth, width), f32),
            *[pltpu.VMEM((depth, width), f32)] * 4,
            *[pltpu.VMEM((batches, count), jnp.int32)] * 2,
            *[pltpu.VMEM((batches, count), f32)] * 2,
            dma((9,)),
            pltpu.VMEM((depth, members, width), f32),
            *[pltpu.VMEM((8, LANES), f32)] * 4,
            *[pltpu.VMEM((cap // 2, LANES), f32)] * 4,
            *[pltpu.VMEM((members, width), f32)] * 2,
            pltpu.VMEM((chunks, devices, piece, LANES), f32),
            dma((6,)),
            dma((6,)),
            *[dma((chunks, max(line_n - 1, 1)))] * 2,
            *[dma((chunks, plane_n - 1))] * 2,
            *[dma((chunks,))] * 2,
        ],
        compiler_params=pltpu.CompilerParams(collective_id=1, has_side_effects=True, vmem_limit_bytes=48 * 2**20),
        name="collect",
    )(ensemble, diff_x, diff_z, cour_x, cour_z, obs_cell, obs_radius, obs_value, obs_var)

    def fast():
        return pl.pallas_call(
            functools.partial(apply_kernel, cap),
            out_shape=jax.ShapeDtypeStruct((members, depth, width), f32),
            in_specs=[smem, hbm, vmem, vmem, vmem, vmem, vmem],
            out_specs=vmem,
            scratch_shapes=[
                pltpu.VMEM((depth, members, width), f32),
                pltpu.VMEM((batches, members, count), f32),
                pltpu.VMEM((batches, count + cap, LANES), f32),
                dma,
            ],
            compiler_params=pltpu.CompilerParams(vmem_limit_bytes=48 * 2**20),
            name="apply",
        )(table, state, flat, meta, taper_in, kinks, tapers)

    def slow():
        return slow_shards(ensemble, diff_x, diff_z, cour_x, cour_z, obs_cell, obs_radius, obs_value, obs_var)

    return lax.cond(flag[0] > 0, slow, fast)


def solution(mesh):
    in_specs = (
        P(None, "layer", "tile"),
        P("layer", "tile"),
        P("layer", "tile"),
        P("layer", "tile"),
        P("layer", "tile"),
        P(),
        P(),
        P(),
        P(),
    )
    out_specs = P(None, "layer", "tile")
    return jax.shard_map(shards, mesh=mesh, in_specs=in_specs, out_specs=out_specs, check_vma=False)
```

```python
import functools

import jax
import jax.numpy as jnp
from jax import lax
from jax.experimental import pallas as pl
from jax.experimental.pallas import tpu as pltpu
from jax.sharding import PartitionSpec as P

MESH = pl.DeviceIdType.MESH
LANES = 128


def split_cell(cells, total):
    if total & (total - 1) == 0:
        return cells >> (total.bit_length() - 1), cells & (total - 1)
    return cells // total, cells % total


def halves(value):
    high = value.astype(jnp.bfloat16)
    return high, (value - high.astype(jnp.float32)).astype(jnp.bfloat16)


def gather_kernel(
    tiles, layers, ens_in, dx_in, dz_in, cx_in, cz_in, cell_in, state_out, prior,
    state, state_sem, ens, diff_x, diff_z, cour_x, cour_z, obs_cell, load_sem,
    cells, edge_w, edge_e, halo_w, halo_e, halo_u, halo_d, coef_up, coef_down, coef_u, coef_d,
    part, in_core, in_plane, in_line, halo_send, halo_recv, core_sem, plane_send, plane_recv, line_send, line_recv,
):
    loads = []
    for i, (src, dst) in enumerate(
        ((ens_in, ens), (dz_in, diff_z), (cz_in, cour_z), (dx_in, diff_x), (cx_in, cour_x), (cell_in, obs_cell))
    ):
        copy = pltpu.make_async_copy(src, dst, load_sem.at[i])
        copy.start()
        loads.append(copy)
    members, depth, width = ens.shape
    batches, count = obs_cell.shape
    tile, layer = lax.axis_index("tile"), lax.axis_index("layer")
    core, row, line = tile % 2, (tile // 2) % 2, tile // 4
    plane_n, line_n = layers * 2, tiles // 4
    spot = layer * 2 + row
    pair = (tile + 1 - 2 * core, layer)

    def plane_at(index):
        return (line * 4 + (index % 2) * 2 + core, index // 2)

    def line_at(index):
        return (index * 4 + row * 2 + core, layer)

    greeted = [pair, ((tile + 1) % tiles, layer), ((tile + tiles - 1) % tiles, layer)]
    greeted += [(tile, (layer + 1) % layers), (tile, (layer + layers - 1) % layers)]
    greeted += [plane_at((spot + j) % plane_n) for j in range(1, plane_n)]
    greeted += [line_at((line + j) % line_n) for j in range(1, line_n)]
    barrier = pltpu.get_barrier_semaphore()
    for device in greeted:
        pl.semaphore_signal(barrier, inc=1, device_id=device, device_id_type=MESH)

    for copy in loads:
        copy.wait()
    lane = lax.broadcasted_iota(jnp.int32, (members, LANES), 1)
    west = jnp.zeros((members, LANES), jnp.float32)
    east = jnp.zeros((members, LANES), jnp.float32)
    for l in range(depth):
        x = ens[:, l, :]
        cells[l] = x
        west = jnp.where(lane == l, x[:, 0:1], west)
        east = jnp.where(lane == l, x[:, width - 1 : width], east)
    edge_w[...] = west
    edge_e[...] = east
    tall = coef_up.shape
    coef_up[...] = jnp.broadcast_to(diff_z[0:1, :] + 0.5 * cour_z[0:1, :], tall)
    coef_down[...] = jnp.broadcast_to(diff_z[depth - 1 : depth, :] - 0.5 * cour_z[depth - 1 : depth, :], tall)
    pl.semaphore_wait(barrier, len(greeted))

    def remote(src, dst, send, recv, device):
        return pltpu.make_async_remote_copy(
            src_ref=src, dst_ref=dst, send_sem=send, recv_sem=recv, device_id=device, device_id_type=MESH
        )

    up, down = layer > 0, layer < layers - 1
    before, after = tile > 0, tile < tiles - 1
    above, below = (tile, lax.rem(layer + layers - 1, layers)), (tile, lax.rem(layer + 1, layers))
    ahead, behind = (lax.rem(tile + 1, tiles), layer), (lax.rem(tile + tiles - 1, tiles), layer)

    def move(i, sends, receives, src, dst, device):
        return sends, receives, remote(src, dst, halo_send.at[i], halo_recv.at[i], device), dst

    small = (
        move(0, after, before, edge_e, halo_w, ahead),
        move(1, before, after, edge_w, halo_e, behind),
        move(2, down, up, coef_down, coef_u, below),
        move(3, up, down, coef_up, coef_d, above),
    )
    large = (
        move(4, down, up, cells.at[depth - 1], halo_u, below),
        move(5, up, down, cells.at[0], halo_d, above),
    )
    for sends, receives, copy, place in small:
        pl.when(sends)(copy.start)
    for sends, receives, copy, place in small + large:

        @pl.when(jnp.logical_not(receives))
        def _(place=place):
            place[...] = jnp.zeros_like(place)

    for sends, receives, copy, place in small:
        pl.when(receives)(copy.wait_recv)

    column = lax.broadcasted_iota(jnp.int32, (members, width), 1)
    levels = list(range(depth)) + [-1, depth]
    parts = []
    for l in range(depth):
        x = cells[l]
        left = jnp.where(column == 0, halo_w[:, l : l + 1], pltpu.roll(x, 1, 1))
        right = jnp.where(column == width - 1, halo_e[:, l : l + 1], pltpu.roll(x, width - 1, 1))
        dx, dz = diff_x[l : l + 1, :], diff_z[l : l + 1, :]
        cx, cz = 0.5 * cour_x[l : l + 1, :], 0.5 * cour_z[l : l + 1, :]
        new = x * (1.0 - 2.0 * dz - 2.0 * dx) + left * (dx + cx) + right * (dx - cx)
        if l > 0:
            new = new + cells[l - 1] * (dz + cz)
        if l < depth - 1:
            new = new + cells[l + 1] * (dz - cz)
        state[l] = new
        parts.extend(halves(new))
    parts.extend(halves(cells[0] * coef_u[0:1, :]))
    parts.extend(halves(cells[depth - 1] * coef_d[0:1, :]))
    stacked = jnp.concatenate(parts, axis=0)

    blocks = count // LANES
    extent = blocks * members
    half = extent // 2
    size = half // plane_n
    scatter = size % (8 * line_n) == 0
    piece = size // line_n if scatter else size
    place = lax.broadcasted_iota(jnp.int32, (width, count), 0)

    def start_of(b, *steps):
        total = b * extent
        for index, length in steps:
            total = total + index * length
        return pl.multiple_of(total, 8)

    every = range(batches)
    core_out, plane_out, line_out, line_back, plane_back, core_back = ([[] for _ in every] for _ in range(6))
    for b in every:
        rows, cols = split_cell(obs_cell[b : b + 1, :], tiles * width)
        rows, cols = rows - layer * depth, cols - tile * width
        hot = jnp.where(place == cols, 1.0, 0.0).astype(jnp.bfloat16)
        picked = jnp.dot(stacked, hot, preferred_element_type=jnp.float32)
        total = jnp.zeros((members, count), jnp.float32)
        for i, l in enumerate(levels):
            both = picked[2 * i * members : (2 * i + 1) * members] + picked[(2 * i + 1) * members : (2 * i + 2) * members]
            total = jnp.where(rows == l, both, total)
        for k in range(blocks):
            part[pl.ds((b * blocks + k) * members, members), :] = total[:, k * LANES : (k + 1) * LANES]
        copy = remote(part.at[pl.ds(start_of(b, (1 - core, half)), half)], in_core.at[b], core_sem.at[b, 0], core_sem.at[b, 1], pair)
        copy.start()
        core_out[b].append(copy)

    for b in every:
        core_out[b][0].wait_recv()
        part[pl.ds(start_of(b, (core, half)), half), :] += in_core[b]
        for j in range(1, plane_n):
            to = (spot + j) % plane_n
            copy = remote(
                part.at[pl.ds(start_of(b, (core, half), (to, size)), size)], in_plane.at[b, j - 1],
                plane_send.at[b, j - 1], plane_recv.at[b, j - 1], plane_at(to),
            )
            copy.start()
            plane_out[b].append(copy)
    for b in every:
        base = start_of(b, (core, half), (spot, size))
        total = part[pl.ds(base, size), :]
        for j in range(1, plane_n):
            plane_out[b][j - 1].wait_recv()
            total = total + in_plane[b, j - 1]
        part[pl.ds(base, size), :] = total
        for j in range(1, line_n):
            to = (line + j) % line_n
            start = start_of(b, (core, half), (spot, size), (to, piece)) if scatter else base
            copy = remote(part.at[pl.ds(start, piece)], in_line.at[b, j - 1], line_send.at[b, j - 1], line_recv.at[b, j - 1], line_at(to))
            copy.start()
            line_out[b].append(copy)
    for sends, receives, copy, _ in large:
        pl.when(sends)(copy.start)

    def spread_plane(b):
        view = prior.at[pl.ds(start_of(b, (core, half), (spot, size)), size)]
        for j in range(1, plane_n):
            k = plane_n - 1 + j - 1
            copy = remote(view, view, plane_send.at[b, k], plane_recv.at[b, k], plane_at((spot + j) % plane_n))
            copy.start()
            plane_back[b].append(copy)

    for b in every:
        own = start_of(b, (core, half), (spot, size), (line, piece)) if scatter else start_of(b, (core, half), (spot, size))
        total = part[pl.ds(own, piece), :]
        for j in range(1, line_n):
            line_out[b][j - 1].wait_recv()
            total = total + in_line[b, j - 1]
        prior[pl.ds(own, piece), :] = total
        if scatter:
            view = prior.at[pl.ds(own, piece)]
            for j in range(1, line_n):
                k = line_n - 1 + j - 1
                copy = remote(view, view, line_send.at[b, k], line_recv.at[b, k], line_at((line + j) % line_n))
                copy.start()
                line_back[b].append(copy)
        else:
            spread_plane(b)
    if scatter:
        for b in every:
            for copy in line_back[b]:
                copy.wait_recv()
            spread_plane(b)

    for sends, receives, copy, _ in large:
        pl.when(receives)(copy.wait_recv)
    state[0] += halo_u[...] * (diff_z[0:1, :] + 0.5 * cour_z[0:1, :])
    state[depth - 1] += halo_d[...] * (diff_z[depth - 1 : depth, :] - 0.5 * cour_z[depth - 1 : depth, :])
    keep = pltpu.make_async_copy(state, state_out, state_sem)
    keep.start()

    for b in every:
        for copy in plane_back[b]:
            copy.wait_recv()
        view = prior.at[pl.ds(start_of(b, (core, half)), half)]
        copy = remote(view, view, core_sem.at[b, 2], core_sem.at[b, 3], pair)
        copy.start()
        core_back[b].append(copy)
    for b in every:
        core_back[b][0].wait_recv()
    for group in (core_out, plane_out, line_out, line_back, plane_back, core_back):
        for copies in group:
            for copy in copies:
                copy.wait_send()
    for sends, receives, copy, _ in small + large:
        pl.when(sends)(copy.wait_send)
    keep.wait()


def update_kernel(
    total_cols, width, state_in, prior_in, cell_in, radius_in, value_in, var_in, out,
    layers_ref, later_ref, prior, obs_cell, obs_radius, obs_value, obs_var, load_sem,
):
    loads = []
    for i, (src, dst) in enumerate(
        (
            (cell_in, obs_cell), (radius_in, obs_radius), (value_in, obs_value), (var_in, obs_var),
            (prior_in, prior), (state_in, layers_ref),
        )
    ):
        copy = pltpu.make_async_copy(src, dst, load_sem.at[i])
        copy.start()
        loads.append(copy)
    depth, members, _ = layers_ref.shape
    batches, count = obs_cell.shape
    blocks = count // LANES
    first = lax.axis_index("tile") * width
    for copy in loads[:-1]:
        copy.wait()
    for b in range(batches):
        for k in range(blocks):
            later_ref[b, :, k * LANES : (k + 1) * LANES] = prior[pl.ds((b * blocks + k) * members, members), :]
    centre = split_cell(obs_cell[...], total_cols)[1].astype(jnp.float32)
    inverse = 1.0 / obs_radius[...].astype(jnp.float32)
    upright = jnp.concatenate([centre, inverse], axis=0).T
    grid = (first + lax.broadcasted_iota(jnp.int32, (1, width), 1)).astype(jnp.float32)

    for b in range(batches):
        y = later_ref[b]
        value, variance = obs_value[b : b + 1, :], obs_var[b : b + 1, :]
        ymean = jnp.sum(y, axis=0, keepdims=True) * (1.0 / members)
        anomaly = y - ymean
        spread = jnp.sum(anomaly * anomaly, axis=0, keepdims=True) / (members - 1) + 1e-06
        shrink = variance / (spread + variance)
        postmean = spread * shrink * (ymean / spread + value / variance)
        delta = (postmean - ymean) + (jnp.sqrt(shrink) - 1.0) * anomaly
        delta = delta * (1.0 / ((members - 1) * spread))
        d_high, d_low = halves(delta)
        d_both = jnp.concatenate([d_high, d_low], axis=0)
        y_high = anomaly.astype(jnp.bfloat16).astype(jnp.float32)
        y_low = anomaly - y_high
        lhs = jnp.concatenate([y_high, y_high, y_low, y_low], axis=0).T.astype(jnp.bfloat16)
        here, scale = upright[:, b : b + 1], upright[:, batches + b : batches + b + 1]

        def taper(positions):
            frac = jnp.maximum(1.0 - jnp.abs(positions - here) * scale, 0.0)
            return frac * frac

        def change(x, weight):
            x_high, x_low = halves(x - jnp.sum(x, axis=0, keepdims=True) * (1.0 / members))
            rhs = jnp.concatenate([x_high, x_low, x_high, x_low], axis=0)
            gain = jnp.dot(lhs, rhs, preferred_element_type=jnp.float32) * weight
            g_high, g_low = halves(gain)
            one = jnp.dot(d_both, g_high, preferred_element_type=jnp.float32)
            two = jnp.dot(d_high, g_low, preferred_element_type=jnp.float32)
            return one[:members] + one[members:] + two

        for c in range(b + 1, batches):
            later_ref[c] += change(later_ref[c], taper(centre[c : c + 1, :]))
        weight = taper(grid)
        if b == 0:
            loads[-1].wait()
        for l in range(depth):
            x = layers_ref[l]
            x = x + change(x, weight)
            if b == batches - 1:
                out[:, l, :] = x
            else:
                layers_ref[l] = x


def divide(values, size):
    return values >> (size.bit_length() - 1) if size & (size - 1) == 0 else values // size


def dot_rows(a, b):
    return lax.dot_general(a, b, (((1,), (1,)), ((), ())), preferred_element_type=jnp.float32)


def remote(src, dst, send, recv, device):
    return pltpu.make_async_remote_copy(
        src_ref=src, dst_ref=dst, send_sem=send, recv_sem=recv, device_id=device, device_id_type=MESH
    )


def collect_kernel(
    tiles, layers, cap, cuts, bends, ens_in, dx_in, dz_in, cx_in, cz_in, cell_in, radius_in, value_in, var_in,
    state_out, flat, meta, taper_in, kinks, tapers, table, flag,
    state, state_sem, ens, diff_x, diff_z, cour_x, cour_z, obs_cell, obs_radius, obs_value, obs_var, load_sem,
    cells, edge_w, edge_e, halo_w, halo_e, near_u, near_d, part_u, part_d, halo_u, halo_d,
    gathered, hop_send, hop_recv, line_send, line_recv, plane_send, plane_recv, core_send, core_recv,
):
    loads = []
    for i, (src, dst) in enumerate(
        (
            (cell_in, obs_cell), (ens_in, ens), (dz_in, diff_z), (cz_in, cour_z), (dx_in, diff_x), (cx_in, cour_x),
            (radius_in, obs_radius), (value_in, obs_value), (var_in, obs_var),
        )
    ):
        copy = pltpu.make_async_copy(src, dst, load_sem.at[i])
        copy.start()
        loads.append(copy)
    members, depth, width = ens.shape
    batches, count = obs_cell.shape
    chunks, devices, piece, _ = gathered.shape
    f32, bf16 = jnp.float32, jnp.bfloat16
    tile, layer = lax.axis_index("tile"), lax.axis_index("layer")
    core, row, line = tile % 2, (tile // 2) % 2, tile // 4
    plane_n, line_n = layers * 2, tiles // 4
    spot = layer * 2 + row
    pair = (tile + 1 - 2 * core, layer)

    def plane_at(index):
        return (line * 4 + (index % 2) * 2 + core, index // 2)

    def line_at(index):
        return (index * 4 + row * 2 + core, layer)

    above, below = (tile, lax.rem(layer + layers - 1, layers)), (tile, lax.rem(layer + 1, layers))
    ahead, behind = (lax.rem(tile + 1, tiles), layer), (lax.rem(tile + tiles - 1, tiles), layer)
    greeted = [pair, ahead, behind, below, above]
    greeted += [plane_at((spot + j) % plane_n) for j in range(1, plane_n)]
    greeted += [line_at((line + j) % line_n) for j in range(1, line_n)]
    barrier = pltpu.get_barrier_semaphore()
    for device in greeted:
        pl.semaphore_signal(barrier, inc=1, device_id=device, device_id_type=MESH)

    loads[0].wait()
    cell_row, cell_col = split_cell(obs_cell[...], tiles * width)
    cell_tile, cell_layer = divide(cell_col, width), divide(cell_row, depth)
    local_col, local_row = cell_col - cell_tile * width, cell_row - cell_layer * depth
    here = cell_tile == tile
    up_rim = jnp.logical_and(local_row == 0, cell_layer > 0)
    down_rim = jnp.logical_and(local_row == depth - 1, cell_layer < layers - 1)
    side_rim = jnp.logical_or(local_col == 0, local_col == width - 1)
    rim = jnp.where(jnp.logical_or(side_rim, jnp.logical_or(up_rim, down_rim)), 1.0, 0.0)
    groups = [
        jnp.where(jnp.logical_and(here, cell_layer == layer + step), share, 0.0)
        for step, share in ((0, 1.0 - rim), (0, rim), (-1, rim), (1, rim))
    ]
    masks = jnp.concatenate(groups, axis=0).astype(bf16)
    first = lax.broadcasted_iota(jnp.int32, (count, count), 0)
    second = lax.broadcasted_iota(jnp.int32, (count, count), 1)
    running = jnp.dot(masks, jnp.where(first <= second, 1.0, 0.0).astype(bf16), preferred_element_type=f32)
    code = (local_row * width + local_col + 1).astype(f32)
    late = 2 * piece
    ranks, sums = [], []
    for k in range(4):
        total = jnp.zeros((1, 1), f32)
        rows = []
        for b in range(batches):
            i = k * batches + b
            rows.append(running[i : i + 1, :] + (total - 1.0))
            total = total + running[i : i + 1, count - 1 : count]
        ranks.append(rows)
        sums.append(total)

    def locate(size, slots_of):
        slot = lax.broadcasted_iota(jnp.int32, (size, count), 0).astype(f32)
        lanes = lax.broadcasted_iota(jnp.int32, (size, width), 1)
        total = jnp.zeros((size, count), f32)
        for b in range(batches):
            total = total + jnp.where(slots_of(b) == slot, code[b : b + 1, :], 0.0)
        cell = jnp.sum(total, axis=1, keepdims=True).astype(jnp.int32) - 1
        at_row = divide(cell, width)
        at_col = jnp.where(cell >= 0, cell - at_row * width, -1)
        return at_row, at_col, jnp.where(lanes == at_col, 1.0, 0.0)

    def facing(k, edge):
        def slots_of(b):
            wanted = jnp.logical_and(groups[k][b : b + 1, :] > 0.5, local_row[b : b + 1, :] == edge)
            return jnp.where(wanted, ranks[k][b] + (late - sums[k]), -1.0)

        return locate(late, slots_of)[2]

    def own(b):
        rim_slot = jnp.where(groups[1][b : b + 1, :] > 0.5, ranks[1][b] + (cap - sums[1]), -1.0)
        return jnp.where(groups[0][b : b + 1, :] > 0.5, ranks[0][b], rim_slot)

    low = lax.broadcasted_iota(jnp.int32, (piece, LANES), 1) < members

    def packed(values):
        out = []
        for k in range(values.shape[0] // late):
            base = 2 * piece * k
            out.append(jnp.where(low, values[base : base + piece], values[base + piece : base + 2 * piece]))
        return out

    def doubled(values):
        return values + pltpu.roll(values, members, 1)

    for copy in loads[1:6]:
        copy.wait()
    lane = lax.broadcasted_iota(jnp.int32, (members, LANES), 1)
    west = jnp.zeros((members, LANES), f32)
    east = jnp.zeros((members, LANES), f32)
    for l in range(depth):
        x = ens[:, l, :]
        cells[l] = x
        west = jnp.where(lane == l, x[:, 0:1], west)
        east = jnp.where(lane == l, x[:, width - 1 : width], east)
    edge_w[...] = jnp.concatenate([west, west], axis=0).T[:8]
    edge_e[...] = jnp.concatenate([east, east], axis=0).T[:8]
    for ref, k, edge, l in ((part_u, 2, depth - 1, 0), (part_d, 3, 0, depth - 1)):
        raw = jnp.concatenate(halves(cells[l]), axis=0)
        ref[...] = packed(doubled(dot_rows(facing(k, edge).astype(bf16), raw)))[0]
    pl.semaphore_wait(barrier, len(greeted))

    up, down = layer > 0, layer < layers - 1
    before, after = tile > 0, tile < tiles - 1

    def move(i, sends, receives, src, dst, device):
        return sends, receives, remote(src, dst, hop_send.at[i], hop_recv.at[i], device), dst

    small = (
        move(0, down, up, part_d, near_u, below),
        move(1, up, down, part_u, near_d, above),
        move(2, after, before, edge_e, halo_w, ahead),
        move(3, before, after, edge_w, halo_e, behind),
    )
    large = (
        move(4, down, up, cells.at[depth - 1], halo_u, below),
        move(5, up, down, cells.at[0], halo_d, above),
    )
    for sends, receives, copy, place in small:
        pl.when(sends)(copy.start)
    for sends, receives, copy, _ in large:
        pl.when(sends)(copy.start)
    for sends, receives, copy, place in small + large:

        @pl.when(jnp.logical_not(receives))
        def _(place=place):
            place[...] = jnp.zeros_like(place)

    at_row, at_col, hot = locate(cap, own)
    column = lax.broadcasted_iota(jnp.int32, (members, width), 1)
    total = jnp.zeros((cap, LANES), f32)
    for l in range(depth):
        x = cells[l]
        left = jnp.where(column == 0, 0.0, pltpu.roll(x, 1, 1))
        right = jnp.where(column == width - 1, 0.0, pltpu.roll(x, width - 1, 1))
        dx, dz = diff_x[l : l + 1, :], diff_z[l : l + 1, :]
        cx, cz = 0.5 * cour_x[l : l + 1, :], 0.5 * cour_z[l : l + 1, :]
        new = x * (1.0 - 2.0 * dz - 2.0 * dx) + left * (dx + cx) + right * (dx - cx)
        if l > 0:
            new = new + cells[l - 1] * (dz + cz)
        if l < depth - 1:
            new = new + cells[l + 1] * (dz - cz)
        state[l] = new
        picked = dot_rows(hot.astype(bf16), jnp.concatenate(halves(new), axis=0))
        total = total + jnp.where(at_row == l, picked, 0.0)
    mine = packed(doubled(total))
    me = (core * plane_n + spot) * line_n + line
    line_out, plane_out, core_out = ([[] for _ in range(chunks)] for _ in range(3))

    def send_line(k, value):
        gathered[k, me] = value
        view = gathered.at[k, me]
        for j in range(1, line_n):
            copy = remote(view, view, line_send.at[k, j - 1], line_recv.at[k, j - 1], line_at((line + j) % line_n))
            copy.start()
            line_out[k].append(copy)

    for k in range(chunks - 1):
        send_line(k, mine[k])
    coef_u = diff_z[0:1, :] + 0.5 * cour_z[0:1, :]
    coef_d = diff_z[depth - 1 : depth, :] - 0.5 * cour_z[depth - 1 : depth, :]
    coef_w = diff_x[:, 0:1] + 0.5 * cour_x[:, 0:1]
    coef_e = diff_x[:, width - 1 : width] - 0.5 * cour_x[:, width - 1 : width]
    at_row, at_col, hot = at_row[cap - late :], at_col[cap - late :], hot[cap - late :]
    take_u = jnp.where(at_row == 0, jnp.sum(hot * coef_u, axis=1, keepdims=True), 0.0)
    take_d = jnp.where(at_row == depth - 1, jnp.sum(hot * coef_d, axis=1, keepdims=True), 0.0)

    def spread_out(take):
        return packed(jnp.broadcast_to(take, (late, LANES)))[0]

    takes = [spread_out(take_u), spread_out(take_d)]
    sides = []
    for at, coef in ((0, coef_w), (width - 1, coef_e)):
        for l in range(depth):
            sides.append(spread_out(jnp.where(jnp.logical_and(at_row == l, at_col == at), coef[l : l + 1, :], 0.0)))

    for sends, receives, copy, place in small:
        pl.when(receives)(copy.wait_recv)
    value = mine[chunks - 1] + takes[0] * near_u[...] + takes[1] * near_d[...]
    for l in range(depth):
        value = value + sides[l] * halo_w[l : l + 1, :] + sides[depth + l] * halo_e[l : l + 1, :]
    send_line(chunks - 1, value)

    for ref, coef, at in ((halo_w, coef_w, 0), (halo_e, coef_e, width - 1)):
        base = at // LANES * LANES
        block = lax.broadcasted_iota(jnp.int32, (members, LANES), 1)
        turned = jnp.concatenate([ref[...]] * (LANES // 8), axis=0).T[:members]
        for l in range(depth):
            term = turned[:, l : l + 1] * coef[l : l + 1, :]
            state[l, :, base : base + LANES] += jnp.where(block == at - base, term, 0.0)

    for copy in loads[6:]:
        copy.wait()
    core_of, row_of, line_of = cell_tile & 1, divide(cell_tile, 2) & 1, divide(cell_tile, 4)
    owner = (core_of * plane_n + cell_layer * 2 + row_of) * line_n + line_of
    owner = owner * 2 + rim.astype(jnp.int32)
    key = (owner * count + lax.broadcasted_iota(jnp.int32, (batches, count), 1)).astype(f32)
    upright = jnp.concatenate([key, jnp.zeros_like(key)], axis=0).T

    def pieces(values, n):
        out = []
        for _ in range(n):
            high = values.astype(bf16).astype(f32)
            out.append(high)
            values = values - high
        return out

    fields = (
        (cell_col.astype(f32), 2), (obs_radius[...].astype(f32), 2), (obs_value[...], 3), (obs_var[...], 3)
    )
    parts = []
    for values, n in fields:
        parts.extend(pieces(values, n))
    holders = 2 * devices
    devices_at = lax.broadcasted_iota(jnp.int32, (holders, count), 0)
    cuts_at = lax.broadcasted_iota(jnp.int32, (tiles * cuts, count), 0)
    ends = [divide(cell_col + obs_radius[...] * step, width // cuts) for step in (-1, 0, 1)]
    used = jnp.zeros((holders, 1), f32)
    begins = []
    worst = jnp.zeros((tiles * cuts, 1), f32)
    longest = jnp.zeros((holders, 1), f32)
    if len(parts) * batches % 16:
        parts.append(jnp.zeros((16 - len(parts) * batches % 16, count), f32))
    parts = jnp.concatenate(parts, axis=0).astype(bf16)
    place = first.astype(f32)
    for b in range(batches):
        less = jnp.where(upright[:, b : b + 1] < key[b : b + 1, :], 1.0, 0.0)
        position = jnp.sum(less, axis=0, keepdims=True)
        order = jnp.where(place == position, 1.0, 0.0).astype(bf16)
        ordered = dot_rows(parts, order)
        i = 0
        for f, (_, n) in enumerate(fields):
            total = ordered[i * batches + b : i * batches + b + 1, :]
            for p in range(1, n):
                total = total + ordered[(i + p) * batches + b : (i + p) * batches + b + 1, :]
            meta[f * batches + b : f * batches + b + 1, :] = total
            i += n
        holder = owner[b : b + 1, :]
        length = jnp.sum(jnp.where(holder == devices_at, 1.0, 0.0), axis=1, keepdims=True)
        start = jnp.sum(jnp.where(holder < devices_at, 1.0, 0.0), axis=1, keepdims=True)
        table[:, b : b + 1] = length.astype(jnp.int32)
        table[:, batches + b : batches + b + 1] = start.astype(jnp.int32)
        begins.append(used)
        used = used + length
        longest = jnp.maximum(longest, length)
        bent = jnp.zeros((tiles * cuts, count), f32)
        for end in ends:
            bent = bent + jnp.where(end[b : b + 1, :] == cuts_at, 1.0, 0.0)
        worst = jnp.maximum(worst, jnp.sum(bent, axis=1, keepdims=True))
    odd = lax.broadcasted_iota(jnp.int32, (holders, 1), 0) % 2
    end = jnp.where(odd == 1, cap - used, 0.0)
    for b in range(batches):
        table[:, 2 * batches + b : 2 * batches + b + 1] = (begins[b] + end).astype(jnp.int32)
    for i in range(2):
        most = jnp.max(jnp.where(odd == i, longest, 0.0), axis=0, keepdims=True)
        table[:, 3 * batches + i : 3 * batches + i + 1] = jnp.broadcast_to(most, (holders, 1)).astype(jnp.int32)
    inner = jnp.broadcast_to(jnp.where(odd == 0, used, 0.0), (holders, LANES))
    pair_of = jnp.broadcast_to(used, (holders, LANES))
    room = jnp.where(odd == 1, pltpu.roll(inner, 1, 0) + pair_of, 0.0)
    rim_most = jnp.max(jnp.where(odd == 1, used, 0.0))
    over = jnp.logical_or(jnp.max(room) > cap, jnp.logical_or(rim_most > late, jnp.max(worst) > bends))
    flag[0] = over.astype(jnp.int32)

    def send_plane(k):
        for copy in line_out[k]:
            copy.wait_recv()
        view = gathered.at[k, pl.ds((core * plane_n + spot) * line_n, line_n)]
        for j in range(1, plane_n):
            copy = remote(view, view, plane_send.at[k, j - 1], plane_recv.at[k, j - 1], plane_at((spot + j) % plane_n))
            copy.start()
            plane_out[k].append(copy)

    for k in range(chunks - 1):
        send_plane(k)

    part_w = width // cuts
    middle = (part_w - 1) / 2
    centre, radius = meta[0:batches, :], meta[batches : 2 * batches, :]
    inverse = 1.0 / radius
    near, far = centre - radius, centre + radius
    bent = []
    for c in range(cuts):
        lowest = (tile * width + c * part_w).astype(f32)
        highest = lowest + (part_w - 1)
        right_of, left_of = centre <= lowest, centre >= highest
        smooth = jnp.logical_or(
            jnp.logical_and(right_of, far >= highest), jnp.logical_and(left_of, near <= lowest)
        )
        away = jnp.logical_or(jnp.logical_and(right_of, far <= lowest), jnp.logical_and(left_of, near >= highest))
        bent.append(jnp.where(jnp.logical_or(smooth, away), 0.0, 1.0))
        value = jnp.where(smooth, 1.0 - jnp.abs(lowest + middle - centre) * inverse, 0.0)
        slope = jnp.where(smooth, jnp.where(right_of, -middle, middle) * inverse, 0.0)
        for i, rows in enumerate((value * value, 2.0 * value * slope, slope * slope)):
            start = (c * 4 + i) * batches
            taper_in[start : start + batches, :] = rows
    padded = jnp.concatenate(bent + [jnp.zeros_like(centre)] * (-cuts % (16 // batches)), axis=0).astype(bf16)
    counted = jnp.dot(padded, jnp.where(first <= second, 1.0, 0.0).astype(bf16), preferred_element_type=f32)
    ranks = []
    for c in range(cuts):
        ranks.append(jnp.where(bent[c] > 0.5, counted[c * batches : (c + 1) * batches] - 1.0, -1.0))
        taper_in[(c * 4 + 3) * batches : (c * 4 + 4) * batches, :] = ranks[c]
    parts = pieces(centre, 2) + pieces(inverse, 3)
    parts = jnp.concatenate(parts + [jnp.zeros_like(centre)] * (-len(parts) % (16 // batches)), axis=0).astype(bf16)
    kink_row = lax.broadcasted_iota(jnp.int32, (bends, count), 0).astype(f32)
    grid = (tile * width + lax.broadcasted_iota(jnp.int32, (1, width), 1)).astype(f32)

    def bump(positions, here, scale):
        frac = jnp.maximum(1.0 - jnp.abs(positions - here) * scale, 0.0)
        return frac * frac

    for b in range(batches):
        choose = [jnp.where(kink_row == ranks[c][b : b + 1, :], 1.0, 0.0).astype(bf16) for c in range(cuts)]
        ordered = dot_rows(jnp.concatenate(choose, axis=0), parts)
        at = [ordered[:, p * batches + b : p * batches + b + 1] for p in range(5)]
        kink_c, kink_i = at[0] + at[1], at[2] + at[3] + at[4]
        for c in range(cuts):
            rows = slice(c * bends, (c + 1) * bends)
            kinks[b, c] = bump(grid[:, c * part_w : (c + 1) * part_w], kink_c[rows], kink_i[rows])
    upright = jnp.concatenate([centre, inverse], axis=0).T
    i = 0
    for b in range(batches):
        for c in range(b + 1, batches):
            tapers[i] = bump(centre[c : c + 1, :], upright[:, b : b + 1], upright[:, batches + b : batches + b + 1])
            i += 1

    send_plane(chunks - 1)
    for sends, receives, copy, _ in large:
        pl.when(receives)(copy.wait_recv)
    state[0] += halo_u[...] * coef_u
    state[depth - 1] += halo_d[...] * coef_d
    keep = pltpu.make_async_copy(state, state_out, state_sem)
    keep.start()

    def unpack(k, side):
        for i in range(devices // 2):
            g = side * (devices // 2) + i
            rows = gathered[k, g]
            at = pl.multiple_of(g * cap + 2 * piece * k, 8)
            flat[pl.ds(at, piece), :] = rows
            flat[pl.ds(at + piece, piece), :] = pltpu.roll(rows, members, 1)

    for k in range(chunks):
        for copy in plane_out[k]:
            copy.wait_recv()
        view = gathered.at[k, pl.ds(core * plane_n * line_n, plane_n * line_n)]
        copy = remote(view, view, core_send.at[k], core_recv.at[k], pair)
        copy.start()
        core_out[k].append(copy)
        unpack(k, core)
    for k in range(chunks):
        core_out[k][0].wait_recv()
        unpack(k, 1 - core)
    for group in (line_out, plane_out, core_out):
        for copies in group:
            for copy in copies:
                copy.wait_send()
    for sends, receives, copy, _ in small + large:
        pl.when(sends)(copy.wait_send)
    keep.wait()


def apply_kernel(
    cap, table, state_in, flat, meta, taper_in, kinks, tapers, out, layers_ref, later_ref, ordered, load_sem,
):
    load = pltpu.make_async_copy(state_in, layers_ref, load_sem)
    load.start()
    depth, members, _ = layers_ref.shape
    batches, _, count = later_ref.shape
    devices = table.shape[0] // 2
    mean = count / devices
    run = min(cap, -int(-(mean + 4.0 * mean**0.5) // 8) * 8)
    short = max(8, run // 16 * 8)

    def spread(sizes):
        def step(g, carry):
            for b in range(batches):
                for i in range(2):
                    dst, src = table[2 * g + i, batches + b], g * cap + table[2 * g + i, 2 * batches + b]
                    for at in range(0, sizes[i], 8):
                        ordered[b, pl.ds(dst + at, 8), :] = flat[pl.ds(src + at, 8), :]
            return carry

        return step

    lax.fori_loop(0, devices, spread((run, short)), 0, unroll=4)

    @pl.when(jnp.logical_or(table[0, 3 * batches] > run, table[0, 3 * batches + 1] > short))
    def _():
        lax.fori_loop(0, devices, spread((cap, cap)), 0)

    for b in range(batches):
        later_ref[b] = ordered[b, :count, :].T[:members]
    _, cuts, bends, part_w = kinks.shape
    middle = (part_w - 1) / 2
    offset = lax.broadcasted_iota(jnp.int32, (1, part_w), 1).astype(jnp.float32)
    ratio = (offset - middle) * (1.0 / middle)
    ratio = jnp.concatenate([ratio] * depth, axis=1)
    third = 3 * members
    both_low = lax.broadcasted_iota(jnp.int32, (third, LANES), 1) < members
    low = lax.broadcasted_iota(jnp.int32, (2 * members, LANES), 1) < members
    top = lax.broadcasted_iota(jnp.int32, (2 * members, LANES), 0) < members
    kink_row = lax.broadcasted_iota(jnp.int32, (bends, count), 0).astype(jnp.float32)
    pair = 0

    for b in range(batches):
        y = later_ref[b]
        value, variance = meta[2 * batches + b : 2 * batches + b + 1, :], meta[3 * batches + b : 3 * batches + b + 1, :]
        ymean = jnp.sum(y, axis=0, keepdims=True) * (1.0 / members)
        anomaly = y - ymean
        spread = jnp.sum(anomaly * anomaly, axis=0, keepdims=True) / (members - 1) + 1e-06
        shrink = variance / (spread + variance)
        postmean = spread * shrink * (ymean / spread + value / variance)
        delta = (postmean - ymean) + (jnp.sqrt(shrink) - 1.0) * anomaly
        delta = delta * (1.0 / ((members - 1) * spread))
        d_high, d_low = halves(delta)
        d_both = jnp.concatenate([d_high, d_low], axis=0)
        y_high = anomaly.astype(jnp.bfloat16).astype(jnp.float32)
        y_low = anomaly - y_high
        y_both = jnp.concatenate([y_high, y_low], axis=0).astype(jnp.bfloat16)

        def stack(x):
            x_high, x_low = halves(x - jnp.sum(x, axis=0, keepdims=True) * (1.0 / members))
            return jnp.concatenate([x_high, x_high, x_low, x_low], axis=0)

        def twice(x):
            return jnp.concatenate([x, x], axis=1).astype(jnp.bfloat16)

        if b < batches - 1:
            lhs = twice(jnp.concatenate([y_high, y_low], axis=0).T)
        scaled = []
        for c in range(cuts):
            for i in range(3):
                row = (c * 4 + i) * batches + b
                scaled.append(delta * taper_in[row : row + 1, :])
        moments = dot_rows(jnp.concatenate(halves(jnp.concatenate(scaled, axis=0)), axis=0), y_both)
        choose = []
        for c in range(cuts):
            row = (c * 4 + 3) * batches + b
            choose.append(jnp.where(kink_row == taper_in[row : row + 1, :], 1.0, 0.0).astype(jnp.bfloat16))
        choose = jnp.concatenate(choose, axis=0)
        y_kink = dot_rows(choose, y_both)
        d_kink = dot_rows(d_both, choose)
        turned = pltpu.roll(d_kink, members, 1)
        lefts, rights = [], []
        if b == 0:
            load.wait()
        for c in range(cuts):
            moment = moments[c * third : (c + 1) * third] + moments[(cuts + c) * third : (cuts + c + 1) * third]
            m_high, m_low = halves(moment + pltpu.roll(moment, members, 1))
            moment = jnp.where(both_low, m_high.astype(jnp.float32), m_low.astype(jnp.float32))
            left = twice(jnp.concatenate([moment, y_kink[c * bends : (c + 1) * bends]], axis=0))
            if cuts == 1:
                right = jnp.concatenate([d_kink, jnp.where(top, d_kink, 0.0)], axis=1)
            elif c == 0:
                right = jnp.where(low, d_kink, jnp.where(top, turned, 0.0))
            else:
                right = jnp.where(low, turned, jnp.where(top, d_kink, 0.0))
            right = right.astype(jnp.bfloat16)
            lefts.append(left)
            rights.append(right)
        rest = range(b + 1, batches)
        crosses = [jnp.dot(lhs, stack(later_ref[c]), preferred_element_type=jnp.float32) for c in rest]
        splits = [halves(cross * tapers[pair + i]) for i, cross in enumerate(crosses)]
        pair += len(rest)
        ones = [jnp.dot(d_both, high, preferred_element_type=jnp.float32) for high, _ in splits]
        twos = [jnp.dot(d_high, lower, preferred_element_type=jnp.float32) for _, lower in splits]
        for i, c in enumerate(rest):
            later_ref[c] += ones[i][:members] + ones[i][members:] + twos[i]

        olds, firsts, gains, seconds = [], [], [], []
        for c in range(cuts):
            columns = slice(c * part_w, (c + 1) * part_w)
            olds.append(jnp.concatenate([layers_ref[l, :, columns] for l in range(depth)], axis=1))
            firsts.append(jnp.dot(lefts[c], stack(olds[c]), preferred_element_type=jnp.float32))
        for c in range(cuts):
            weight = jnp.concatenate([kinks[b, c]] * depth, axis=1)
            gains.append(jnp.concatenate(halves(firsts[c][third:] * weight), axis=0))
        for c in range(cuts):
            seconds.append(jnp.dot(rights[c], gains[c], preferred_element_type=jnp.float32))
        for c in range(cuts):
            both, more = firsts[c], seconds[c]
            x = olds[c] + (both[:members] + ratio * (both[members : 2 * members] + ratio * both[2 * members : third]))
            x = x + (more[:members] + more[members:])
            columns = slice(c * part_w, (c + 1) * part_w)
            for l in range(depth):
                if b == batches - 1:
                    out[:, l, columns] = x[:, l * part_w : (l + 1) * part_w]
                else:
                    layers_ref[l, :, columns] = x[:, l * part_w : (l + 1) * part_w]


def slow_shards(ensemble, diff_x, diff_z, cour_x, cour_z, obs_cell, obs_radius, obs_value, obs_var):
    members, depth, width = ensemble.shape
    batches, count = obs_cell.shape
    tiles, layers = lax.axis_size("tile"), lax.axis_size("layer")
    rows = batches * count * members // LANES
    plane_n, line_n = layers * 2, tiles // 4
    half = rows // batches // 2
    size = half // plane_n
    piece = size // line_n if size % (8 * line_n) == 0 else size
    vmem = pl.BlockSpec(memory_space=pltpu.VMEM)
    hbm = pl.BlockSpec(memory_space=pltpu.HBM)
    f32 = jnp.float32
    dma = pltpu.SemaphoreType.DMA
    state, prior = pl.pallas_call(
        functools.partial(gather_kernel, tiles, layers),
        out_shape=(jax.ShapeDtypeStruct((depth, members, width), f32), jax.ShapeDtypeStruct((rows, LANES), f32)),
        in_specs=[hbm] * 6,
        out_specs=(hbm, vmem),
        scratch_shapes=[
            pltpu.VMEM((depth, members, width), f32),
            dma,
            pltpu.VMEM((members, depth, width), f32),
            *[pltpu.VMEM((depth, width), f32)] * 4,
            pltpu.VMEM((batches, count), jnp.int32),
            dma((6,)),
            pltpu.VMEM((depth, members, width), f32),
            *[pltpu.VMEM((members, LANES), f32)] * 4,
            *[pltpu.VMEM((members, width), f32)] * 2,
            *[pltpu.VMEM((8, width), f32)] * 4,
            pltpu.VMEM((rows, LANES), f32),
            pltpu.VMEM((batches, half, LANES), f32),
            pltpu.VMEM((batches, plane_n - 1, size, LANES), f32),
            pltpu.VMEM((batches, line_n - 1, piece, LANES), f32),
            dma((6,)),
            dma((6,)),
            dma((batches, 4)),
            dma((batches, 2 * plane_n - 2)),
            dma((batches, 2 * plane_n - 2)),
            dma((batches, 2 * line_n - 2)),
            dma((batches, 2 * line_n - 2)),
        ],
        compiler_params=pltpu.CompilerParams(collective_id=0, has_side_effects=True, vmem_limit_bytes=63 * 2**20),
        name="gather_prior",
    )(ensemble, diff_x, diff_z, cour_x, cour_z, obs_cell)
    return pl.pallas_call(
        functools.partial(update_kernel, tiles * width, width),
        out_shape=jax.ShapeDtypeStruct((members, depth, width), f32),
        in_specs=[hbm] * 6,
        out_specs=vmem,
        scratch_shapes=[
            pltpu.VMEM((depth, members, width), f32),
            pltpu.VMEM((batches, members, count), f32),
            pltpu.VMEM((rows, LANES), f32),
            *[pltpu.VMEM((batches, count), jnp.int32)] * 2,
            *[pltpu.VMEM((batches, count), f32)] * 2,
            dma((6,)),
        ],
        compiler_params=pltpu.CompilerParams(vmem_limit_bytes=63 * 2**20),
        name="update",
    )(state, prior, obs_cell, obs_radius, obs_value, obs_var)


def shards(ensemble, diff_x, diff_z, cour_x, cour_z, obs_cell, obs_radius, obs_value, obs_var):
    members, depth, width = ensemble.shape
    batches, count = obs_cell.shape
    tiles, layers = lax.axis_size("tile"), lax.axis_size("layer")
    devices = tiles * layers
    plane_n, line_n = layers * 2, tiles // 4
    mean = batches * count / devices
    cap = -int(-(mean + 4.0 * mean**0.5) // 16) * 16
    piece = 16 if cap % 32 == 0 else 8
    chunks = cap // (2 * piece)
    cuts, bends = (2, 64) if width % (2 * LANES) == 0 else (1, LANES)
    vmem = pl.BlockSpec(memory_space=pltpu.VMEM)
    smem = pl.BlockSpec(memory_space=pltpu.SMEM)
    hbm = pl.BlockSpec(memory_space=pltpu.HBM)
    f32 = jnp.float32
    dma = pltpu.SemaphoreType.DMA
    state, flat, meta, taper_in, kinks, tapers, table, flag = pl.pallas_call(
        functools.partial(collect_kernel, tiles, layers, cap, cuts, bends),
        out_shape=(
            jax.ShapeDtypeStruct((depth, members, width), f32),
            jax.ShapeDtypeStruct((devices * cap + cap, LANES), f32),
            jax.ShapeDtypeStruct((4 * batches, count), f32),
            jax.ShapeDtypeStruct((cuts * 4 * batches, count), f32),
            jax.ShapeDtypeStruct((batches, cuts, bends, width // cuts), f32),
            jax.ShapeDtypeStruct((batches * (batches - 1) // 2, count, count), f32),
            jax.ShapeDtypeStruct((2 * devices, 3 * batches + 2), jnp.int32),
            jax.ShapeDtypeStruct((1,), jnp.int32),
        ),
        in_specs=[hbm] * 9,
        out_specs=(hbm, vmem, vmem, vmem, vmem, vmem, vmem, smem),
        scratch_shapes=[
            pltpu.VMEM((depth, members, width), f32),
            dma,
            pltpu.VMEM((members, depth, width), f32),
            *[pltpu.VMEM((depth, width), f32)] * 4,
            *[pltpu.VMEM((batches, count), jnp.int32)] * 2,
            *[pltpu.VMEM((batches, count), f32)] * 2,
            dma((9,)),
            pltpu.VMEM((depth, members, width), f32),
            *[pltpu.VMEM((8, LANES), f32)] * 4,
            *[pltpu.VMEM((piece, LANES), f32)] * 4,
            *[pltpu.VMEM((members, width), f32)] * 2,
            pltpu.VMEM((chunks, devices, piece, LANES), f32),
            dma((6,)),
            dma((6,)),
            *[dma((chunks, max(line_n - 1, 1)))] * 2,
            *[dma((chunks, plane_n - 1))] * 2,
            *[dma((chunks,))] * 2,
        ],
        compiler_params=pltpu.CompilerParams(collective_id=1, has_side_effects=True, vmem_limit_bytes=48 * 2**20),
        name="collect",
    )(ensemble, diff_x, diff_z, cour_x, cour_z, obs_cell, obs_radius, obs_value, obs_var)

    def fast():
        return pl.pallas_call(
            functools.partial(apply_kernel, cap),
            out_shape=jax.ShapeDtypeStruct((members, depth, width), f32),
            in_specs=[smem, hbm, vmem, vmem, vmem, vmem, vmem],
            out_specs=vmem,
            scratch_shapes=[
                pltpu.VMEM((depth, members, width), f32),
                pltpu.VMEM((batches, members, count), f32),
                pltpu.VMEM((batches, count + cap, LANES), f32),
                dma,
            ],
            compiler_params=pltpu.CompilerParams(vmem_limit_bytes=48 * 2**20),
            name="apply",
        )(table, state, flat, meta, taper_in, kinks, tapers)

    def slow():
        return slow_shards(ensemble, diff_x, diff_z, cour_x, cour_z, obs_cell, obs_radius, obs_value, obs_var)

    return lax.cond(flag[0] > 0, slow, fast)


def solution(mesh):
    in_specs = (
        P(None, "layer", "tile"),
        P("layer", "tile"),
        P("layer", "tile"),
        P("layer", "tile"),
        P("layer", "tile"),
        P(),
        P(),
        P(),
        P(),
    )
    out_specs = P(None, "layer", "tile")
    return jax.shard_map(shards, mesh=mesh, in_specs=in_specs, out_specs=out_specs, check_vma=False)
```

```python
import functools

import jax
import jax.numpy as jnp
from jax import lax
from jax.experimental import pallas as pl
from jax.experimental.pallas import tpu as pltpu
from jax.sharding import PartitionSpec as P

MESH = pl.DeviceIdType.MESH
LANES = 128


def split_cell(cells, total):
    if total & (total - 1) == 0:
        return cells >> (total.bit_length() - 1), cells & (total - 1)
    return cells // total, cells % total


def halves(value):
    high = value.astype(jnp.bfloat16)
    return high, (value - high.astype(jnp.float32)).astype(jnp.bfloat16)


def gather_kernel(
    tiles, layers, ens_in, dx_in, dz_in, cx_in, cz_in, cell_in, state_out, prior,
    state, state_sem, ens, diff_x, diff_z, cour_x, cour_z, obs_cell, load_sem,
    cells, edge_w, edge_e, halo_w, halo_e, halo_u, halo_d, coef_up, coef_down, coef_u, coef_d,
    part, in_core, in_plane, in_line, halo_send, halo_recv, core_sem, plane_send, plane_recv, line_send, line_recv,
):
    loads = []
    for i, (src, dst) in enumerate(
        ((ens_in, ens), (dz_in, diff_z), (cz_in, cour_z), (dx_in, diff_x), (cx_in, cour_x), (cell_in, obs_cell))
    ):
        copy = pltpu.make_async_copy(src, dst, load_sem.at[i])
        copy.start()
        loads.append(copy)
    members, depth, width = ens.shape
    batches, count = obs_cell.shape
    tile, layer = lax.axis_index("tile"), lax.axis_index("layer")
    core, row, line = tile % 2, (tile // 2) % 2, tile // 4
    plane_n, line_n = layers * 2, tiles // 4
    spot = layer * 2 + row
    pair = (tile + 1 - 2 * core, layer)

    def plane_at(index):
        return (line * 4 + (index % 2) * 2 + core, index // 2)

    def line_at(index):
        return (index * 4 + row * 2 + core, layer)

    greeted = [pair, ((tile + 1) % tiles, layer), ((tile + tiles - 1) % tiles, layer)]
    greeted += [(tile, (layer + 1) % layers), (tile, (layer + layers - 1) % layers)]
    greeted += [plane_at((spot + j) % plane_n) for j in range(1, plane_n)]
    greeted += [line_at((line + j) % line_n) for j in range(1, line_n)]
    barrier = pltpu.get_barrier_semaphore()
    for device in greeted:
        pl.semaphore_signal(barrier, inc=1, device_id=device, device_id_type=MESH)

    for copy in loads:
        copy.wait()
    lane = lax.broadcasted_iota(jnp.int32, (members, LANES), 1)
    west = jnp.zeros((members, LANES), jnp.float32)
    east = jnp.zeros((members, LANES), jnp.float32)
    for l in range(depth):
        x = ens[:, l, :]
        cells[l] = x
        west = jnp.where(lane == l, x[:, 0:1], west)
        east = jnp.where(lane == l, x[:, width - 1 : width], east)
    edge_w[...] = west
    edge_e[...] = east
    tall = coef_up.shape
    coef_up[...] = jnp.broadcast_to(diff_z[0:1, :] + 0.5 * cour_z[0:1, :], tall)
    coef_down[...] = jnp.broadcast_to(diff_z[depth - 1 : depth, :] - 0.5 * cour_z[depth - 1 : depth, :], tall)
    pl.semaphore_wait(barrier, len(greeted))

    def remote(src, dst, send, recv, device):
        return pltpu.make_async_remote_copy(
            src_ref=src, dst_ref=dst, send_sem=send, recv_sem=recv, device_id=device, device_id_type=MESH
        )

    up, down = layer > 0, layer < layers - 1
    before, after = tile > 0, tile < tiles - 1
    above, below = (tile, lax.rem(layer + layers - 1, layers)), (tile, lax.rem(layer + 1, layers))
    ahead, behind = (lax.rem(tile + 1, tiles), layer), (lax.rem(tile + tiles - 1, tiles), layer)

    def move(i, sends, receives, src, dst, device):
        return sends, receives, remote(src, dst, halo_send.at[i], halo_recv.at[i], device), dst

    small = (
        move(0, after, before, edge_e, halo_w, ahead),
        move(1, before, after, edge_w, halo_e, behind),
        move(2, down, up, coef_down, coef_u, below),
        move(3, up, down, coef_up, coef_d, above),
    )
    large = (
        move(4, down, up, cells.at[depth - 1], halo_u, below),
        move(5, up, down, cells.at[0], halo_d, above),
    )
    for sends, receives, copy, place in small:
        pl.when(sends)(copy.start)
    for sends, receives, copy, place in small + large:

        @pl.when(jnp.logical_not(receives))
        def _(place=place):
            place[...] = jnp.zeros_like(place)

    for sends, receives, copy, place in small:
        pl.when(receives)(copy.wait_recv)

    column = lax.broadcasted_iota(jnp.int32, (members, width), 1)
    levels = list(range(depth)) + [-1, depth]
    parts = []
    for l in range(depth):
        x = cells[l]
        left = jnp.where(column == 0, halo_w[:, l : l + 1], pltpu.roll(x, 1, 1))
        right = jnp.where(column == width - 1, halo_e[:, l : l + 1], pltpu.roll(x, width - 1, 1))
        dx, dz = diff_x[l : l + 1, :], diff_z[l : l + 1, :]
        cx, cz = 0.5 * cour_x[l : l + 1, :], 0.5 * cour_z[l : l + 1, :]
        new = x * (1.0 - 2.0 * dz - 2.0 * dx) + left * (dx + cx) + right * (dx - cx)
        if l > 0:
            new = new + cells[l - 1] * (dz + cz)
        if l < depth - 1:
            new = new + cells[l + 1] * (dz - cz)
        state[l] = new
        parts.extend(halves(new))
    parts.extend(halves(cells[0] * coef_u[0:1, :]))
    parts.extend(halves(cells[depth - 1] * coef_d[0:1, :]))
    stacked = jnp.concatenate(parts, axis=0)

    blocks = count // LANES
    extent = blocks * members
    half = extent // 2
    size = half // plane_n
    scatter = size % (8 * line_n) == 0
    piece = size // line_n if scatter else size
    place = lax.broadcasted_iota(jnp.int32, (width, count), 0)

    def start_of(b, *steps):
        total = b * extent
        for index, length in steps:
            total = total + index * length
        return pl.multiple_of(total, 8)

    every = range(batches)
    core_out, plane_out, line_out, line_back, plane_back, core_back = ([[] for _ in every] for _ in range(6))
    for b in every:
        rows, cols = split_cell(obs_cell[b : b + 1, :], tiles * width)
        rows, cols = rows - layer * depth, cols - tile * width
        hot = jnp.where(place == cols, 1.0, 0.0).astype(jnp.bfloat16)
        picked = jnp.dot(stacked, hot, preferred_element_type=jnp.float32)
        total = jnp.zeros((members, count), jnp.float32)
        for i, l in enumerate(levels):
            both = picked[2 * i * members : (2 * i + 1) * members] + picked[(2 * i + 1) * members : (2 * i + 2) * members]
            total = jnp.where(rows == l, both, total)
        for k in range(blocks):
            part[pl.ds((b * blocks + k) * members, members), :] = total[:, k * LANES : (k + 1) * LANES]
        copy = remote(part.at[pl.ds(start_of(b, (1 - core, half)), half)], in_core.at[b], core_sem.at[b, 0], core_sem.at[b, 1], pair)
        copy.start()
        core_out[b].append(copy)

    for b in every:
        core_out[b][0].wait_recv()
        part[pl.ds(start_of(b, (core, half)), half), :] += in_core[b]
        for j in range(1, plane_n):
            to = (spot + j) % plane_n
            copy = remote(
                part.at[pl.ds(start_of(b, (core, half), (to, size)), size)], in_plane.at[b, j - 1],
                plane_send.at[b, j - 1], plane_recv.at[b, j - 1], plane_at(to),
            )
            copy.start()
            plane_out[b].append(copy)
    for b in every:
        base = start_of(b, (core, half), (spot, size))
        total = part[pl.ds(base, size), :]
        for j in range(1, plane_n):
            plane_out[b][j - 1].wait_recv()
            total = total + in_plane[b, j - 1]
        part[pl.ds(base, size), :] = total
        for j in range(1, line_n):
            to = (line + j) % line_n
            start = start_of(b, (core, half), (spot, size), (to, piece)) if scatter else base
            copy = remote(part.at[pl.ds(start, piece)], in_line.at[b, j - 1], line_send.at[b, j - 1], line_recv.at[b, j - 1], line_at(to))
            copy.start()
            line_out[b].append(copy)
    for sends, receives, copy, _ in large:
        pl.when(sends)(copy.start)

    def spread_plane(b):
        view = prior.at[pl.ds(start_of(b, (core, half), (spot, size)), size)]
        for j in range(1, plane_n):
            k = plane_n - 1 + j - 1
            copy = remote(view, view, plane_send.at[b, k], plane_recv.at[b, k], plane_at((spot + j) % plane_n))
            copy.start()
            plane_back[b].append(copy)

    for b in every:
        own = start_of(b, (core, half), (spot, size), (line, piece)) if scatter else start_of(b, (core, half), (spot, size))
        total = part[pl.ds(own, piece), :]
        for j in range(1, line_n):
            line_out[b][j - 1].wait_recv()
            total = total + in_line[b, j - 1]
        prior[pl.ds(own, piece), :] = total
        if scatter:
            view = prior.at[pl.ds(own, piece)]
            for j in range(1, line_n):
                k = line_n - 1 + j - 1
                copy = remote(view, view, line_send.at[b, k], line_recv.at[b, k], line_at((line + j) % line_n))
                copy.start()
                line_back[b].append(copy)
        else:
            spread_plane(b)
    if scatter:
        for b in every:
            for copy in line_back[b]:
                copy.wait_recv()
            spread_plane(b)

    for sends, receives, copy, _ in large:
        pl.when(receives)(copy.wait_recv)
    state[0] += halo_u[...] * (diff_z[0:1, :] + 0.5 * cour_z[0:1, :])
    state[depth - 1] += halo_d[...] * (diff_z[depth - 1 : depth, :] - 0.5 * cour_z[depth - 1 : depth, :])
    keep = pltpu.make_async_copy(state, state_out, state_sem)
    keep.start()

    for b in every:
        for copy in plane_back[b]:
            copy.wait_recv()
        view = prior.at[pl.ds(start_of(b, (core, half)), half)]
        copy = remote(view, view, core_sem.at[b, 2], core_sem.at[b, 3], pair)
        copy.start()
        core_back[b].append(copy)
    for b in every:
        core_back[b][0].wait_recv()
    for group in (core_out, plane_out, line_out, line_back, plane_back, core_back):
        for copies in group:
            for copy in copies:
                copy.wait_send()
    for sends, receives, copy, _ in small + large:
        pl.when(sends)(copy.wait_send)
    keep.wait()


def update_kernel(
    total_cols, width, state_in, prior_in, cell_in, radius_in, value_in, var_in, out,
    layers_ref, later_ref, prior, obs_cell, obs_radius, obs_value, obs_var, load_sem,
):
    loads = []
    for i, (src, dst) in enumerate(
        (
            (cell_in, obs_cell), (radius_in, obs_radius), (value_in, obs_value), (var_in, obs_var),
            (prior_in, prior), (state_in, layers_ref),
        )
    ):
        copy = pltpu.make_async_copy(src, dst, load_sem.at[i])
        copy.start()
        loads.append(copy)
    depth, members, _ = layers_ref.shape
    batches, count = obs_cell.shape
    blocks = count // LANES
    first = lax.axis_index("tile") * width
    for copy in loads[:-1]:
        copy.wait()
    for b in range(batches):
        for k in range(blocks):
            later_ref[b, :, k * LANES : (k + 1) * LANES] = prior[pl.ds((b * blocks + k) * members, members), :]
    centre = split_cell(obs_cell[...], total_cols)[1].astype(jnp.float32)
    inverse = 1.0 / obs_radius[...].astype(jnp.float32)
    upright = jnp.concatenate([centre, inverse], axis=0).T
    grid = (first + lax.broadcasted_iota(jnp.int32, (1, width), 1)).astype(jnp.float32)

    for b in range(batches):
        y = later_ref[b]
        value, variance = obs_value[b : b + 1, :], obs_var[b : b + 1, :]
        ymean = jnp.sum(y, axis=0, keepdims=True) * (1.0 / members)
        anomaly = y - ymean
        spread = jnp.sum(anomaly * anomaly, axis=0, keepdims=True) / (members - 1) + 1e-06
        shrink = variance / (spread + variance)
        postmean = spread * shrink * (ymean / spread + value / variance)
        delta = (postmean - ymean) + (jnp.sqrt(shrink) - 1.0) * anomaly
        delta = delta * (1.0 / ((members - 1) * spread))
        d_high, d_low = halves(delta)
        d_both = jnp.concatenate([d_high, d_low], axis=0)
        y_high = anomaly.astype(jnp.bfloat16).astype(jnp.float32)
        y_low = anomaly - y_high
        lhs = jnp.concatenate([y_high, y_high, y_low, y_low], axis=0).T.astype(jnp.bfloat16)
        here, scale = upright[:, b : b + 1], upright[:, batches + b : batches + b + 1]

        def taper(positions):
            frac = jnp.maximum(1.0 - jnp.abs(positions - here) * scale, 0.0)
            return frac * frac

        def change(x, weight):
            x_high, x_low = halves(x - jnp.sum(x, axis=0, keepdims=True) * (1.0 / members))
            rhs = jnp.concatenate([x_high, x_low, x_high, x_low], axis=0)
            gain = jnp.dot(lhs, rhs, preferred_element_type=jnp.float32) * weight
            g_high, g_low = halves(gain)
            one = jnp.dot(d_both, g_high, preferred_element_type=jnp.float32)
            two = jnp.dot(d_high, g_low, preferred_element_type=jnp.float32)
            return one[:members] + one[members:] + two

        for c in range(b + 1, batches):
            later_ref[c] += change(later_ref[c], taper(centre[c : c + 1, :]))
        weight = taper(grid)
        if b == 0:
            loads[-1].wait()
        for l in range(depth):
            x = layers_ref[l]
            x = x + change(x, weight)
            if b == batches - 1:
                out[:, l, :] = x
            else:
                layers_ref[l] = x


def divide(values, size):
    return values >> (size.bit_length() - 1) if size & (size - 1) == 0 else values // size


def dot_rows(a, b):
    return lax.dot_general(a, b, (((1,), (1,)), ((), ())), preferred_element_type=jnp.float32)


def remote(src, dst, send, recv, device):
    return pltpu.make_async_remote_copy(
        src_ref=src, dst_ref=dst, send_sem=send, recv_sem=recv, device_id=device, device_id_type=MESH
    )


def collect_kernel(
    tiles, layers, cap, cuts, bends, ens_in, dx_in, dz_in, cx_in, cz_in, cell_in, radius_in, value_in, var_in,
    state_out, flat, meta, taper_in, kinks, tapers, table, flag,
    state, state_sem, ens, diff_x, diff_z, cour_x, cour_z, obs_cell, obs_radius, obs_value, obs_var, load_sem,
    cells, edge_w, edge_e, halo_w, halo_e, near_u, near_d, part_u, part_d, halo_u, halo_d,
    gathered, hop_send, hop_recv, line_send, line_recv, plane_send, plane_recv, core_send, core_recv,
):
    loads = []
    for i, (src, dst) in enumerate(
        (
            (cell_in, obs_cell), (ens_in, ens), (dz_in, diff_z), (cz_in, cour_z), (dx_in, diff_x), (cx_in, cour_x),
            (radius_in, obs_radius), (value_in, obs_value), (var_in, obs_var),
        )
    ):
        copy = pltpu.make_async_copy(src, dst, load_sem.at[i])
        copy.start()
        loads.append(copy)
    members, depth, width = ens.shape
    batches, count = obs_cell.shape
    chunks, devices, piece, _ = gathered.shape
    f32, bf16 = jnp.float32, jnp.bfloat16
    tile, layer = lax.axis_index("tile"), lax.axis_index("layer")
    core, row, line = tile % 2, (tile // 2) % 2, tile // 4
    plane_n, line_n = layers * 2, tiles // 4
    spot = layer * 2 + row
    pair = (tile + 1 - 2 * core, layer)

    def plane_at(index):
        return (line * 4 + (index % 2) * 2 + core, index // 2)

    def line_at(index):
        return (index * 4 + row * 2 + core, layer)

    above, below = (tile, lax.rem(layer + layers - 1, layers)), (tile, lax.rem(layer + 1, layers))
    ahead, behind = (lax.rem(tile + 1, tiles), layer), (lax.rem(tile + tiles - 1, tiles), layer)
    greeted = [pair, ahead, behind, below, above]
    greeted += [plane_at((spot + j) % plane_n) for j in range(1, plane_n)]
    greeted += [line_at((line + j) % line_n) for j in range(1, line_n)]
    barrier = pltpu.get_barrier_semaphore()
    for device in greeted:
        pl.semaphore_signal(barrier, inc=1, device_id=device, device_id_type=MESH)

    loads[0].wait()
    cell_row, cell_col = split_cell(obs_cell[...], tiles * width)
    cell_tile, cell_layer = divide(cell_col, width), divide(cell_row, depth)
    local_col, local_row = cell_col - cell_tile * width, cell_row - cell_layer * depth
    here = cell_tile == tile
    up_rim = jnp.logical_and(local_row == 0, cell_layer > 0)
    down_rim = jnp.logical_and(local_row == depth - 1, cell_layer < layers - 1)
    side_rim = jnp.logical_or(local_col == 0, local_col == width - 1)
    rim = jnp.where(jnp.logical_or(side_rim, jnp.logical_or(up_rim, down_rim)), 1.0, 0.0)
    groups = [
        jnp.where(jnp.logical_and(here, cell_layer == layer + step), share, 0.0)
        for step, share in ((0, 1.0 - rim), (0, rim), (-1, rim), (1, rim))
    ]
    masks = jnp.concatenate(groups, axis=0).astype(bf16)
    first = lax.broadcasted_iota(jnp.int32, (count, count), 0)
    second = lax.broadcasted_iota(jnp.int32, (count, count), 1)
    running = jnp.dot(masks, jnp.where(first <= second, 1.0, 0.0).astype(bf16), preferred_element_type=f32)
    code = (local_row * width + local_col + 1).astype(f32)
    late = 2 * piece
    ranks, sums = [], []
    for k in range(4):
        total = jnp.zeros((1, 1), f32)
        rows = []
        for b in range(batches):
            i = k * batches + b
            rows.append(running[i : i + 1, :] + (total - 1.0))
            total = total + running[i : i + 1, count - 1 : count]
        ranks.append(rows)
        sums.append(total)

    def locate(size, slots_of):
        slot = lax.broadcasted_iota(jnp.int32, (size, count), 0).astype(f32)
        lanes = lax.broadcasted_iota(jnp.int32, (size, width), 1)
        total = jnp.zeros((size, count), f32)
        for b in range(batches):
            total = total + jnp.where(slots_of(b) == slot, code[b : b + 1, :], 0.0)
        cell = jnp.sum(total, axis=1, keepdims=True).astype(jnp.int32) - 1
        at_row = divide(cell, width)
        at_col = jnp.where(cell >= 0, cell - at_row * width, -1)
        return at_row, at_col, jnp.where(lanes == at_col, 1.0, 0.0)

    def facing(k, edge):
        def slots_of(b):
            wanted = jnp.logical_and(groups[k][b : b + 1, :] > 0.5, local_row[b : b + 1, :] == edge)
            return jnp.where(wanted, ranks[k][b] + (late - sums[k]), -1.0)

        return locate(late, slots_of)[2]

    def own(b):
        rim_slot = jnp.where(groups[1][b : b + 1, :] > 0.5, ranks[1][b] + (cap - sums[1]), -1.0)
        return jnp.where(groups[0][b : b + 1, :] > 0.5, ranks[0][b], rim_slot)

    low = lax.broadcasted_iota(jnp.int32, (piece, LANES), 1) < members

    def packed(values):
        out = []
        for k in range(values.shape[0] // late):
            base = 2 * piece * k
            out.append(jnp.where(low, values[base : base + piece], values[base + piece : base + 2 * piece]))
        return out

    def doubled(values):
        return values + pltpu.roll(values, members, 1)

    for copy in loads[1:6]:
        copy.wait()
    lane = lax.broadcasted_iota(jnp.int32, (members, LANES), 1)
    west = jnp.zeros((members, LANES), f32)
    east = jnp.zeros((members, LANES), f32)
    for l in range(depth):
        x = ens[:, l, :]
        cells[l] = x
        west = jnp.where(lane == l, x[:, 0:1], west)
        east = jnp.where(lane == l, x[:, width - 1 : width], east)
    edge_w[...] = jnp.concatenate([west, west], axis=0).T[:8]
    edge_e[...] = jnp.concatenate([east, east], axis=0).T[:8]
    for ref, k, edge, l in ((part_u, 2, depth - 1, 0), (part_d, 3, 0, depth - 1)):
        raw = jnp.concatenate(halves(cells[l]), axis=0)
        ref[...] = packed(doubled(dot_rows(facing(k, edge).astype(bf16), raw)))[0]
    pl.semaphore_wait(barrier, len(greeted))

    up, down = layer > 0, layer < layers - 1
    before, after = tile > 0, tile < tiles - 1

    def move(i, sends, receives, src, dst, device):
        return sends, receives, remote(src, dst, hop_send.at[i], hop_recv.at[i], device), dst

    small = (
        move(0, down, up, part_d, near_u, below),
        move(1, up, down, part_u, near_d, above),
        move(2, after, before, edge_e, halo_w, ahead),
        move(3, before, after, edge_w, halo_e, behind),
    )
    large = (
        move(4, down, up, cells.at[depth - 1], halo_u, below),
        move(5, up, down, cells.at[0], halo_d, above),
    )
    for sends, receives, copy, place in small:
        pl.when(sends)(copy.start)
    for sends, receives, copy, _ in large:
        pl.when(sends)(copy.start)
    for sends, receives, copy, place in small + large:

        @pl.when(jnp.logical_not(receives))
        def _(place=place):
            place[...] = jnp.zeros_like(place)

    at_row, at_col, hot = locate(cap, own)
    column = lax.broadcasted_iota(jnp.int32, (members, width), 1)
    total = jnp.zeros((cap, LANES), f32)
    for l in range(depth):
        x = cells[l]
        left = jnp.where(column == 0, 0.0, pltpu.roll(x, 1, 1))
        right = jnp.where(column == width - 1, 0.0, pltpu.roll(x, width - 1, 1))
        dx, dz = diff_x[l : l + 1, :], diff_z[l : l + 1, :]
        cx, cz = 0.5 * cour_x[l : l + 1, :], 0.5 * cour_z[l : l + 1, :]
        new = x * (1.0 - 2.0 * dz - 2.0 * dx) + left * (dx + cx) + right * (dx - cx)
        if l > 0:
            new = new + cells[l - 1] * (dz + cz)
        if l < depth - 1:
            new = new + cells[l + 1] * (dz - cz)
        state[l] = new
        picked = dot_rows(hot.astype(bf16), jnp.concatenate(halves(new), axis=0))
        total = total + jnp.where(at_row == l, picked, 0.0)
    mine = packed(doubled(total))
    me = (core * plane_n + spot) * line_n + line
    line_out, plane_out, core_out = ([[] for _ in range(chunks)] for _ in range(3))

    def send_line(k, value):
        gathered[k, me] = value
        view = gathered.at[k, me]
        for j in range(1, line_n):
            copy = remote(view, view, line_send.at[k, j - 1], line_recv.at[k, j - 1], line_at((line + j) % line_n))
            copy.start()
            line_out[k].append(copy)

    for k in range(chunks - 1):
        send_line(k, mine[k])
    coef_u = diff_z[0:1, :] + 0.5 * cour_z[0:1, :]
    coef_d = diff_z[depth - 1 : depth, :] - 0.5 * cour_z[depth - 1 : depth, :]
    coef_w = diff_x[:, 0:1] + 0.5 * cour_x[:, 0:1]
    coef_e = diff_x[:, width - 1 : width] - 0.5 * cour_x[:, width - 1 : width]
    at_row, at_col, hot = at_row[cap - late :], at_col[cap - late :], hot[cap - late :]
    take_u = jnp.where(at_row == 0, jnp.sum(hot * coef_u, axis=1, keepdims=True), 0.0)
    take_d = jnp.where(at_row == depth - 1, jnp.sum(hot * coef_d, axis=1, keepdims=True), 0.0)

    def spread_out(take):
        return packed(jnp.broadcast_to(take, (late, LANES)))[0]

    takes = [spread_out(take_u), spread_out(take_d)]
    sides = []
    for at, coef in ((0, coef_w), (width - 1, coef_e)):
        for l in range(depth):
            sides.append(spread_out(jnp.where(jnp.logical_and(at_row == l, at_col == at), coef[l : l + 1, :], 0.0)))

    for sends, receives, copy, place in small:
        pl.when(receives)(copy.wait_recv)
    value = mine[chunks - 1] + takes[0] * near_u[...] + takes[1] * near_d[...]
    for l in range(depth):
        value = value + sides[l] * halo_w[l : l + 1, :] + sides[depth + l] * halo_e[l : l + 1, :]
    send_line(chunks - 1, value)

    for ref, coef, at in ((halo_w, coef_w, 0), (halo_e, coef_e, width - 1)):
        base = at // LANES * LANES
        block = lax.broadcasted_iota(jnp.int32, (members, LANES), 1)
        turned = jnp.concatenate([ref[...]] * (LANES // 8), axis=0).T[:members]
        for l in range(depth):
            term = turned[:, l : l + 1] * coef[l : l + 1, :]
            state[l, :, base : base + LANES] += jnp.where(block == at - base, term, 0.0)

    for copy in loads[6:]:
        copy.wait()
    core_of, row_of, line_of = cell_tile & 1, divide(cell_tile, 2) & 1, divide(cell_tile, 4)
    owner = (core_of * plane_n + cell_layer * 2 + row_of) * line_n + line_of
    owner = owner * 2 + rim.astype(jnp.int32)
    key = (owner * count + lax.broadcasted_iota(jnp.int32, (batches, count), 1)).astype(f32)
    upright = jnp.concatenate([key, jnp.zeros_like(key)], axis=0).T

    def pieces(values, n):
        out = []
        for _ in range(n):
            high = values.astype(bf16).astype(f32)
            out.append(high)
            values = values - high
        return out

    fields = (
        (cell_col.astype(f32), 2), (obs_radius[...].astype(f32), 2), (obs_value[...], 3), (obs_var[...], 3)
    )
    parts = []
    for values, n in fields:
        parts.extend(pieces(values, n))
    holders = 2 * devices
    devices_at = lax.broadcasted_iota(jnp.int32, (holders, count), 0)
    cuts_at = lax.broadcasted_iota(jnp.int32, (tiles * cuts, count), 0)
    ends = [divide(cell_col + obs_radius[...] * step, width // cuts) for step in (-1, 0, 1)]
    used = jnp.zeros((holders, 1), f32)
    begins, starts = [], []
    worst = jnp.zeros((tiles * cuts, 1), f32)
    longest = jnp.zeros((holders, 1), f32)
    if len(parts) * batches % 16:
        parts.append(jnp.zeros((16 - len(parts) * batches % 16, count), f32))
    parts = jnp.concatenate(parts, axis=0).astype(bf16)
    place = first.astype(f32)
    for b in range(batches):
        less = jnp.where(upright[:, b : b + 1] < key[b : b + 1, :], 1.0, 0.0)
        position = jnp.sum(less, axis=0, keepdims=True)
        order = jnp.where(place == position, 1.0, 0.0).astype(bf16)
        ordered = dot_rows(parts, order)
        i = 0
        for f, (_, n) in enumerate(fields):
            total = ordered[i * batches + b : i * batches + b + 1, :]
            for p in range(1, n):
                total = total + ordered[(i + p) * batches + b : (i + p) * batches + b + 1, :]
            meta[f * batches + b : f * batches + b + 1, :] = total
            i += n
        holder = owner[b : b + 1, :]
        length = jnp.sum(jnp.where(holder == devices_at, 1.0, 0.0), axis=1, keepdims=True)
        start = jnp.sum(jnp.where(holder < devices_at, 1.0, 0.0), axis=1, keepdims=True)
        starts.append(start)
        begins.append(used)
        used = used + length
        longest = jnp.maximum(longest, length)
        bent = jnp.zeros((tiles * cuts, count), f32)
        for end in ends:
            bent = bent + jnp.where(end[b : b + 1, :] == cuts_at, 1.0, 0.0)
        worst = jnp.maximum(worst, jnp.sum(bent, axis=1, keepdims=True))
    odd = lax.broadcasted_iota(jnp.int32, (holders, 1), 0) % 2
    end = jnp.where(odd == 1, cap - used, 0.0)
    entries = starts + [begin + end for begin in begins]
    for i in range(2):
        most = jnp.max(jnp.where(odd == i, longest, 0.0), axis=0, keepdims=True)
        entries.append(jnp.broadcast_to(most, (holders, 1)))
    entry_lane = lax.broadcasted_iota(jnp.int32, (holders, LANES), 1)
    listed = jnp.zeros((holders, LANES), f32)
    for i, entry in enumerate(entries):
        listed = jnp.where(entry_lane == i, entry, listed)
    if holders % LANES:
        listed = jnp.concatenate([listed, jnp.zeros((-holders % LANES, LANES), f32)], axis=0)
    table[...] = listed.T[: table.shape[0]].astype(jnp.int32)
    inner = jnp.broadcast_to(jnp.where(odd == 0, used, 0.0), (holders, LANES))
    pair_of = jnp.broadcast_to(used, (holders, LANES))
    room = jnp.where(odd == 1, pltpu.roll(inner, 1, 0) + pair_of, 0.0)
    rim_most = jnp.max(jnp.where(odd == 1, used, 0.0))
    over = jnp.logical_or(jnp.max(room) > cap, jnp.logical_or(rim_most > late, jnp.max(worst) > bends))
    flag[0] = over.astype(jnp.int32)

    def send_plane(k):
        for copy in line_out[k]:
            copy.wait_recv()
        view = gathered.at[k, pl.ds((core * plane_n + spot) * line_n, line_n)]
        for j in range(1, plane_n):
            copy = remote(view, view, plane_send.at[k, j - 1], plane_recv.at[k, j - 1], plane_at((spot + j) % plane_n))
            copy.start()
            plane_out[k].append(copy)

    for k in range(chunks - 1):
        send_plane(k)

    part_w = width // cuts
    middle = (part_w - 1) / 2
    centre, radius = meta[0:batches, :], meta[batches : 2 * batches, :]
    inverse = 1.0 / radius
    near, far = centre - radius, centre + radius
    bent = []
    for c in range(cuts):
        lowest = (tile * width + c * part_w).astype(f32)
        highest = lowest + (part_w - 1)
        right_of, left_of = centre <= lowest, centre >= highest
        smooth = jnp.logical_or(
            jnp.logical_and(right_of, far >= highest), jnp.logical_and(left_of, near <= lowest)
        )
        away = jnp.logical_or(jnp.logical_and(right_of, far <= lowest), jnp.logical_and(left_of, near >= highest))
        bent.append(jnp.where(jnp.logical_or(smooth, away), 0.0, 1.0))
        value = jnp.where(smooth, 1.0 - jnp.abs(lowest + middle - centre) * inverse, 0.0)
        slope = jnp.where(smooth, jnp.where(right_of, -middle, middle) * inverse, 0.0)
        for i, rows in enumerate((value * value, 2.0 * value * slope, slope * slope)):
            start = (c * 4 + i) * batches
            taper_in[start : start + batches, :] = rows
    padded = jnp.concatenate(bent + [jnp.zeros_like(centre)] * (-cuts % (16 // batches)), axis=0).astype(bf16)
    counted = jnp.dot(padded, jnp.where(first <= second, 1.0, 0.0).astype(bf16), preferred_element_type=f32)
    ranks = []
    for c in range(cuts):
        ranks.append(jnp.where(bent[c] > 0.5, counted[c * batches : (c + 1) * batches] - 1.0, -1.0))
        taper_in[(c * 4 + 3) * batches : (c * 4 + 4) * batches, :] = ranks[c]
    parts = pieces(centre, 2) + pieces(inverse, 3)
    parts = jnp.concatenate(parts + [jnp.zeros_like(centre)] * (-len(parts) % (16 // batches)), axis=0).astype(bf16)
    kink_row = lax.broadcasted_iota(jnp.int32, (bends, count), 0).astype(f32)
    grid = (tile * width + lax.broadcasted_iota(jnp.int32, (1, width), 1)).astype(f32)

    def bump(positions, here, scale):
        frac = jnp.maximum(1.0 - jnp.abs(positions - here) * scale, 0.0)
        return frac * frac

    for b in range(batches):
        choose = [jnp.where(kink_row == ranks[c][b : b + 1, :], 1.0, 0.0).astype(bf16) for c in range(cuts)]
        ordered = dot_rows(jnp.concatenate(choose, axis=0), parts)
        at = [ordered[:, p * batches + b : p * batches + b + 1] for p in range(5)]
        kink_c, kink_i = at[0] + at[1], at[2] + at[3] + at[4]
        for c in range(cuts):
            rows = slice(c * bends, (c + 1) * bends)
            kinks[b, c] = bump(grid[:, c * part_w : (c + 1) * part_w], kink_c[rows], kink_i[rows])
    upright = jnp.concatenate([centre, inverse], axis=0).T
    i = 0
    for b in range(batches):
        for c in range(b + 1, batches):
            tapers[i] = bump(centre[c : c + 1, :], upright[:, b : b + 1], upright[:, batches + b : batches + b + 1])
            i += 1

    send_plane(chunks - 1)
    for sends, receives, copy, _ in large:
        pl.when(receives)(copy.wait_recv)
    state[0] += halo_u[...] * coef_u
    state[depth - 1] += halo_d[...] * coef_d
    keep = pltpu.make_async_copy(state, state_out, state_sem)
    keep.start()

    def unpack(k, side):
        for i in range(devices // 2):
            g = side * (devices // 2) + i
            rows = gathered[k, g]
            at = pl.multiple_of(g * cap + 2 * piece * k, 8)
            flat[pl.ds(at, piece), :] = rows
            flat[pl.ds(at + piece, piece), :] = pltpu.roll(rows, members, 1)

    for k in range(chunks):
        for copy in plane_out[k]:
            copy.wait_recv()
        view = gathered.at[k, pl.ds(core * plane_n * line_n, plane_n * line_n)]
        copy = remote(view, view, core_send.at[k], core_recv.at[k], pair)
        copy.start()
        core_out[k].append(copy)
        unpack(k, core)
    for k in range(chunks):
        core_out[k][0].wait_recv()
        unpack(k, 1 - core)
    for group in (line_out, plane_out, core_out):
        for copies in group:
            for copy in copies:
                copy.wait_send()
    for sends, receives, copy, _ in small + large:
        pl.when(sends)(copy.wait_send)
    keep.wait()


def apply_kernel(
    cap, devices, table, state_in, flat, meta, taper_in, kinks, tapers, out, layers_ref, later_ref, ordered, load_sem,
):
    load = pltpu.make_async_copy(state_in, layers_ref, load_sem)
    load.start()
    depth, members, _ = layers_ref.shape
    batches, _, count = later_ref.shape
    mean = count / devices
    run = min(cap, -int(-(mean + 4.0 * mean**0.5) // 8) * 8)
    short = max(8, run // 16 * 8)

    def spread(sizes):
        def step(g, carry):
            for b in range(batches):
                for i in range(2):
                    dst, src = table[b, 2 * g + i], g * cap + table[batches + b, 2 * g + i]
                    for at in range(0, sizes[i], 8):
                        ordered[b, pl.ds(dst + at, 8), :] = flat[pl.ds(src + at, 8), :]
            return carry

        return step

    lax.fori_loop(0, devices, spread((run, short)), 0, unroll=4)

    @pl.when(jnp.logical_or(table[2 * batches, 0] > run, table[2 * batches + 1, 0] > short))
    def _():
        lax.fori_loop(0, devices, spread((cap, cap)), 0)

    for b in range(batches):
        later_ref[b] = ordered[b, :count, :].T[:members]
    _, cuts, bends, part_w = kinks.shape
    middle = (part_w - 1) / 2
    offset = lax.broadcasted_iota(jnp.int32, (1, part_w), 1).astype(jnp.float32)
    ratio = (offset - middle) * (1.0 / middle)
    ratio = jnp.concatenate([ratio] * depth, axis=1)
    third = 3 * members
    both_low = lax.broadcasted_iota(jnp.int32, (third, LANES), 1) < members
    low = lax.broadcasted_iota(jnp.int32, (2 * members, LANES), 1) < members
    top = lax.broadcasted_iota(jnp.int32, (2 * members, LANES), 0) < members
    kink_row = lax.broadcasted_iota(jnp.int32, (bends, count), 0).astype(jnp.float32)
    pair = 0

    for b in range(batches):
        y = later_ref[b]
        value, variance = meta[2 * batches + b : 2 * batches + b + 1, :], meta[3 * batches + b : 3 * batches + b + 1, :]
        ymean = jnp.sum(y, axis=0, keepdims=True) * (1.0 / members)
        anomaly = y - ymean
        spread = jnp.sum(anomaly * anomaly, axis=0, keepdims=True) / (members - 1) + 1e-06
        shrink = variance / (spread + variance)
        postmean = spread * shrink * (ymean / spread + value / variance)
        delta = (postmean - ymean) + (jnp.sqrt(shrink) - 1.0) * anomaly
        delta = delta * (1.0 / ((members - 1) * spread))
        d_high, d_low = halves(delta)
        d_both = jnp.concatenate([d_high, d_low], axis=0)
        y_high = anomaly.astype(jnp.bfloat16).astype(jnp.float32)
        y_low = anomaly - y_high
        y_both = jnp.concatenate([y_high, y_low], axis=0).astype(jnp.bfloat16)

        def stack(x):
            x_high, x_low = halves(x - jnp.sum(x, axis=0, keepdims=True) * (1.0 / members))
            return jnp.concatenate([x_high, x_high, x_low, x_low], axis=0)

        def twice(x):
            return jnp.concatenate([x, x], axis=1).astype(jnp.bfloat16)

        if b < batches - 1:
            lhs = twice(jnp.concatenate([y_high, y_low], axis=0).T)
        scaled = []
        for c in range(cuts):
            for i in range(3):
                row = (c * 4 + i) * batches + b
                scaled.append(delta * taper_in[row : row + 1, :])
        moments = dot_rows(jnp.concatenate(halves(jnp.concatenate(scaled, axis=0)), axis=0), y_both)
        choose = []
        for c in range(cuts):
            row = (c * 4 + 3) * batches + b
            choose.append(jnp.where(kink_row == taper_in[row : row + 1, :], 1.0, 0.0).astype(jnp.bfloat16))
        choose = jnp.concatenate(choose, axis=0)
        y_kink = dot_rows(choose, y_both)
        d_kink = dot_rows(d_both, choose)
        turned = pltpu.roll(d_kink, members, 1)
        lefts, rights = [], []
        if b == 0:
            load.wait()
        for c in range(cuts):
            moment = moments[c * third : (c + 1) * third] + moments[(cuts + c) * third : (cuts + c + 1) * third]
            m_high, m_low = halves(moment + pltpu.roll(moment, members, 1))
            moment = jnp.where(both_low, m_high.astype(jnp.float32), m_low.astype(jnp.float32))
            left = twice(jnp.concatenate([moment, y_kink[c * bends : (c + 1) * bends]], axis=0))
            if cuts == 1:
                right = jnp.concatenate([d_kink, jnp.where(top, d_kink, 0.0)], axis=1)
            elif c == 0:
                right = jnp.where(low, d_kink, jnp.where(top, turned, 0.0))
            else:
                right = jnp.where(low, turned, jnp.where(top, d_kink, 0.0))
            right = right.astype(jnp.bfloat16)
            lefts.append(left)
            rights.append(right)
        rest = range(b + 1, batches)
        crosses = [jnp.dot(lhs, stack(later_ref[c]), preferred_element_type=jnp.float32) for c in rest]
        splits = [halves(cross * tapers[pair + i]) for i, cross in enumerate(crosses)]
        pair += len(rest)
        ones = [jnp.dot(d_both, high, preferred_element_type=jnp.float32) for high, _ in splits]
        twos = [jnp.dot(d_high, lower, preferred_element_type=jnp.float32) for _, lower in splits]
        for i, c in enumerate(rest):
            later_ref[c] += ones[i][:members] + ones[i][members:] + twos[i]

        olds, firsts, gains, seconds = [], [], [], []
        for c in range(cuts):
            columns = slice(c * part_w, (c + 1) * part_w)
            olds.append(jnp.concatenate([layers_ref[l, :, columns] for l in range(depth)], axis=1))
            firsts.append(jnp.dot(lefts[c], stack(olds[c]), preferred_element_type=jnp.float32))
        for c in range(cuts):
            weight = jnp.concatenate([kinks[b, c]] * depth, axis=1)
            gains.append(jnp.concatenate(halves(firsts[c][third:] * weight), axis=0))
        for c in range(cuts):
            seconds.append(jnp.dot(rights[c], gains[c], preferred_element_type=jnp.float32))
        for c in range(cuts):
            both, more = firsts[c], seconds[c]
            x = olds[c] + (both[:members] + ratio * (both[members : 2 * members] + ratio * both[2 * members : third]))
            x = x + (more[:members] + more[members:])
            columns = slice(c * part_w, (c + 1) * part_w)
            for l in range(depth):
                if b == batches - 1:
                    out[:, l, columns] = x[:, l * part_w : (l + 1) * part_w]
                else:
                    layers_ref[l, :, columns] = x[:, l * part_w : (l + 1) * part_w]


def slow_shards(ensemble, diff_x, diff_z, cour_x, cour_z, obs_cell, obs_radius, obs_value, obs_var):
    members, depth, width = ensemble.shape
    batches, count = obs_cell.shape
    tiles, layers = lax.axis_size("tile"), lax.axis_size("layer")
    rows = batches * count * members // LANES
    plane_n, line_n = layers * 2, tiles // 4
    half = rows // batches // 2
    size = half // plane_n
    piece = size // line_n if size % (8 * line_n) == 0 else size
    vmem = pl.BlockSpec(memory_space=pltpu.VMEM)
    hbm = pl.BlockSpec(memory_space=pltpu.HBM)
    f32 = jnp.float32
    dma = pltpu.SemaphoreType.DMA
    state, prior = pl.pallas_call(
        functools.partial(gather_kernel, tiles, layers),
        out_shape=(jax.ShapeDtypeStruct((depth, members, width), f32), jax.ShapeDtypeStruct((rows, LANES), f32)),
        in_specs=[hbm] * 6,
        out_specs=(hbm, vmem),
        scratch_shapes=[
            pltpu.VMEM((depth, members, width), f32),
            dma,
            pltpu.VMEM((members, depth, width), f32),
            *[pltpu.VMEM((depth, width), f32)] * 4,
            pltpu.VMEM((batches, count), jnp.int32),
            dma((6,)),
            pltpu.VMEM((depth, members, width), f32),
            *[pltpu.VMEM((members, LANES), f32)] * 4,
            *[pltpu.VMEM((members, width), f32)] * 2,
            *[pltpu.VMEM((8, width), f32)] * 4,
            pltpu.VMEM((rows, LANES), f32),
            pltpu.VMEM((batches, half, LANES), f32),
            pltpu.VMEM((batches, plane_n - 1, size, LANES), f32),
            pltpu.VMEM((batches, line_n - 1, piece, LANES), f32),
            dma((6,)),
            dma((6,)),
            dma((batches, 4)),
            dma((batches, 2 * plane_n - 2)),
            dma((batches, 2 * plane_n - 2)),
            dma((batches, 2 * line_n - 2)),
            dma((batches, 2 * line_n - 2)),
        ],
        compiler_params=pltpu.CompilerParams(collective_id=0, has_side_effects=True, vmem_limit_bytes=63 * 2**20),
        name="gather_prior",
    )(ensemble, diff_x, diff_z, cour_x, cour_z, obs_cell)
    return pl.pallas_call(
        functools.partial(update_kernel, tiles * width, width),
        out_shape=jax.ShapeDtypeStruct((members, depth, width), f32),
        in_specs=[hbm] * 6,
        out_specs=vmem,
        scratch_shapes=[
            pltpu.VMEM((depth, members, width), f32),
            pltpu.VMEM((batches, members, count), f32),
            pltpu.VMEM((rows, LANES), f32),
            *[pltpu.VMEM((batches, count), jnp.int32)] * 2,
            *[pltpu.VMEM((batches, count), f32)] * 2,
            dma((6,)),
        ],
        compiler_params=pltpu.CompilerParams(vmem_limit_bytes=63 * 2**20),
        name="update",
    )(state, prior, obs_cell, obs_radius, obs_value, obs_var)


def shards(ensemble, diff_x, diff_z, cour_x, cour_z, obs_cell, obs_radius, obs_value, obs_var):
    members, depth, width = ensemble.shape
    batches, count = obs_cell.shape
    tiles, layers = lax.axis_size("tile"), lax.axis_size("layer")
    devices = tiles * layers
    plane_n, line_n = layers * 2, tiles // 4
    mean = batches * count / devices
    cap = -int(-(mean + 4.0 * mean**0.5) // 16) * 16
    piece = 16 if cap % 32 == 0 else 8
    chunks = cap // (2 * piece)
    cuts, bends = 1, LANES
    vmem = pl.BlockSpec(memory_space=pltpu.VMEM)
    smem = pl.BlockSpec(memory_space=pltpu.SMEM)
    hbm = pl.BlockSpec(memory_space=pltpu.HBM)
    f32 = jnp.float32
    dma = pltpu.SemaphoreType.DMA
    state, flat, meta, taper_in, kinks, tapers, table, flag = pl.pallas_call(
        functools.partial(collect_kernel, tiles, layers, cap, cuts, bends),
        out_shape=(
            jax.ShapeDtypeStruct((depth, members, width), f32),
            jax.ShapeDtypeStruct((devices * cap + cap, LANES), f32),
            jax.ShapeDtypeStruct((4 * batches, count), f32),
            jax.ShapeDtypeStruct((cuts * 4 * batches, count), f32),
            jax.ShapeDtypeStruct((batches, cuts, bends, width // cuts), f32),
            jax.ShapeDtypeStruct((batches * (batches - 1) // 2, count, count), f32),
            jax.ShapeDtypeStruct((-(-(2 * batches + 2) // 8) * 8, -(-2 * devices // LANES) * LANES), jnp.int32),
            jax.ShapeDtypeStruct((1,), jnp.int32),
        ),
        in_specs=[hbm] * 9,
        out_specs=(hbm, vmem, vmem, vmem, vmem, vmem, vmem, smem),
        scratch_shapes=[
            pltpu.VMEM((depth, members, width), f32),
            dma,
            pltpu.VMEM((members, depth, width), f32),
            *[pltpu.VMEM((depth, width), f32)] * 4,
            *[pltpu.VMEM((batches, count), jnp.int32)] * 2,
            *[pltpu.VMEM((batches, count), f32)] * 2,
            dma((9,)),
            pltpu.VMEM((depth, members, width), f32),
            *[pltpu.VMEM((8, LANES), f32)] * 4,
            *[pltpu.VMEM((piece, LANES), f32)] * 4,
            *[pltpu.VMEM((members, width), f32)] * 2,
            pltpu.VMEM((chunks, devices, piece, LANES), f32),
            dma((6,)),
            dma((6,)),
            *[dma((chunks, max(line_n - 1, 1)))] * 2,
            *[dma((chunks, plane_n - 1))] * 2,
            *[dma((chunks,))] * 2,
        ],
        compiler_params=pltpu.CompilerParams(collective_id=1, has_side_effects=True, vmem_limit_bytes=48 * 2**20),
        name="collect",
    )(ensemble, diff_x, diff_z, cour_x, cour_z, obs_cell, obs_radius, obs_value, obs_var)

    def fast():
        return pl.pallas_call(
            functools.partial(apply_kernel, cap, devices),
            out_shape=jax.ShapeDtypeStruct((members, depth, width), f32),
            in_specs=[smem, hbm, vmem, vmem, vmem, vmem, vmem],
            out_specs=vmem,
            scratch_shapes=[
                pltpu.VMEM((depth, members, width), f32),
                pltpu.VMEM((batches, members, count), f32),
                pltpu.VMEM((batches, count + cap, LANES), f32),
                dma,
            ],
            compiler_params=pltpu.CompilerParams(vmem_limit_bytes=48 * 2**20),
            name="apply",
        )(table, state, flat, meta, taper_in, kinks, tapers)

    def slow():
        return slow_shards(ensemble, diff_x, diff_z, cour_x, cour_z, obs_cell, obs_radius, obs_value, obs_var)

    return lax.cond(flag[0] > 0, slow, fast)


def solution(mesh):
    in_specs = (
        P(None, "layer", "tile"),
        P("layer", "tile"),
        P("layer", "tile"),
        P("layer", "tile"),
        P("layer", "tile"),
        P(),
        P(),
        P(),
        P(),
    )
    out_specs = P(None, "layer", "tile")
    return jax.shard_map(shards, mesh=mesh, in_specs=in_specs, out_specs=out_specs, check_vma=False)
```

```python
import functools

import jax
import jax.numpy as jnp
from jax import lax
from jax.experimental import pallas as pl
from jax.experimental.pallas import tpu as pltpu
from jax.sharding import PartitionSpec as P

MESH = pl.DeviceIdType.MESH
LANES = 128


def split_cell(cells, total):
    if total & (total - 1) == 0:
        return cells >> (total.bit_length() - 1), cells & (total - 1)
    return cells // total, cells % total


def halves(value):
    high = value.astype(jnp.bfloat16)
    return high, (value - high.astype(jnp.float32)).astype(jnp.bfloat16)


def gather_kernel(
    tiles, layers, ens_in, dx_in, dz_in, cx_in, cz_in, cell_in, state_out, prior,
    state, state_sem, ens, diff_x, diff_z, cour_x, cour_z, obs_cell, load_sem,
    cells, edge_w, edge_e, halo_w, halo_e, halo_u, halo_d, coef_up, coef_down, coef_u, coef_d,
    part, in_core, in_plane, in_line, halo_send, halo_recv, core_sem, plane_send, plane_recv, line_send, line_recv,
):
    loads = []
    for i, (src, dst) in enumerate(
        ((ens_in, ens), (dz_in, diff_z), (cz_in, cour_z), (dx_in, diff_x), (cx_in, cour_x), (cell_in, obs_cell))
    ):
        copy = pltpu.make_async_copy(src, dst, load_sem.at[i])
        copy.start()
        loads.append(copy)
    members, depth, width = ens.shape
    batches, count = obs_cell.shape
    tile, layer = lax.axis_index("tile"), lax.axis_index("layer")
    core, row, line = tile % 2, (tile // 2) % 2, tile // 4
    plane_n, line_n = layers * 2, tiles // 4
    spot = layer * 2 + row
    pair = (tile + 1 - 2 * core, layer)

    def plane_at(index):
        return (line * 4 + (index % 2) * 2 + core, index // 2)

    def line_at(index):
        return (index * 4 + row * 2 + core, layer)

    greeted = [pair, ((tile + 1) % tiles, layer), ((tile + tiles - 1) % tiles, layer)]
    greeted += [(tile, (layer + 1) % layers), (tile, (layer + layers - 1) % layers)]
    greeted += [plane_at((spot + j) % plane_n) for j in range(1, plane_n)]
    greeted += [line_at((line + j) % line_n) for j in range(1, line_n)]
    barrier = pltpu.get_barrier_semaphore()
    for device in greeted:
        pl.semaphore_signal(barrier, inc=1, device_id=device, device_id_type=MESH)

    for copy in loads:
        copy.wait()
    lane = lax.broadcasted_iota(jnp.int32, (members, LANES), 1)
    west = jnp.zeros((members, LANES), jnp.float32)
    east = jnp.zeros((members, LANES), jnp.float32)
    for l in range(depth):
        x = ens[:, l, :]
        cells[l] = x
        west = jnp.where(lane == l, x[:, 0:1], west)
        east = jnp.where(lane == l, x[:, width - 1 : width], east)
    edge_w[...] = west
    edge_e[...] = east
    tall = coef_up.shape
    coef_up[...] = jnp.broadcast_to(diff_z[0:1, :] + 0.5 * cour_z[0:1, :], tall)
    coef_down[...] = jnp.broadcast_to(diff_z[depth - 1 : depth, :] - 0.5 * cour_z[depth - 1 : depth, :], tall)
    pl.semaphore_wait(barrier, len(greeted))

    def remote(src, dst, send, recv, device):
        return pltpu.make_async_remote_copy(
            src_ref=src, dst_ref=dst, send_sem=send, recv_sem=recv, device_id=device, device_id_type=MESH
        )

    up, down = layer > 0, layer < layers - 1
    before, after = tile > 0, tile < tiles - 1
    above, below = (tile, lax.rem(layer + layers - 1, layers)), (tile, lax.rem(layer + 1, layers))
    ahead, behind = (lax.rem(tile + 1, tiles), layer), (lax.rem(tile + tiles - 1, tiles), layer)

    def move(i, sends, receives, src, dst, device):
        return sends, receives, remote(src, dst, halo_send.at[i], halo_recv.at[i], device), dst

    small = (
        move(0, after, before, edge_e, halo_w, ahead),
        move(1, before, after, edge_w, halo_e, behind),
        move(2, down, up, coef_down, coef_u, below),
        move(3, up, down, coef_up, coef_d, above),
    )
    large = (
        move(4, down, up, cells.at[depth - 1], halo_u, below),
        move(5, up, down, cells.at[0], halo_d, above),
    )
    for sends, receives, copy, place in small:
        pl.when(sends)(copy.start)
    for sends, receives, copy, place in small + large:

        @pl.when(jnp.logical_not(receives))
        def _(place=place):
            place[...] = jnp.zeros_like(place)

    for sends, receives, copy, place in small:
        pl.when(receives)(copy.wait_recv)

    column = lax.broadcasted_iota(jnp.int32, (members, width), 1)
    levels = list(range(depth)) + [-1, depth]
    parts = []
    for l in range(depth):
        x = cells[l]
        left = jnp.where(column == 0, halo_w[:, l : l + 1], pltpu.roll(x, 1, 1))
        right = jnp.where(column == width - 1, halo_e[:, l : l + 1], pltpu.roll(x, width - 1, 1))
        dx, dz = diff_x[l : l + 1, :], diff_z[l : l + 1, :]
        cx, cz = 0.5 * cour_x[l : l + 1, :], 0.5 * cour_z[l : l + 1, :]
        new = x * (1.0 - 2.0 * dz - 2.0 * dx) + left * (dx + cx) + right * (dx - cx)
        if l > 0:
            new = new + cells[l - 1] * (dz + cz)
        if l < depth - 1:
            new = new + cells[l + 1] * (dz - cz)
        state[l] = new
        parts.extend(halves(new))
    parts.extend(halves(cells[0] * coef_u[0:1, :]))
    parts.extend(halves(cells[depth - 1] * coef_d[0:1, :]))
    stacked = jnp.concatenate(parts, axis=0)

    blocks = count // LANES
    extent = blocks * members
    half = extent // 2
    size = half // plane_n
    scatter = size % (8 * line_n) == 0
    piece = size // line_n if scatter else size
    place = lax.broadcasted_iota(jnp.int32, (width, count), 0)

    def start_of(b, *steps):
        total = b * extent
        for index, length in steps:
            total = total + index * length
        return pl.multiple_of(total, 8)

    every = range(batches)
    core_out, plane_out, line_out, line_back, plane_back, core_back = ([[] for _ in every] for _ in range(6))
    for b in every:
        rows, cols = split_cell(obs_cell[b : b + 1, :], tiles * width)
        rows, cols = rows - layer * depth, cols - tile * width
        hot = jnp.where(place == cols, 1.0, 0.0).astype(jnp.bfloat16)
        picked = jnp.dot(stacked, hot, preferred_element_type=jnp.float32)
        total = jnp.zeros((members, count), jnp.float32)
        for i, l in enumerate(levels):
            both = picked[2 * i * members : (2 * i + 1) * members] + picked[(2 * i + 1) * members : (2 * i + 2) * members]
            total = jnp.where(rows == l, both, total)
        for k in range(blocks):
            part[pl.ds((b * blocks + k) * members, members), :] = total[:, k * LANES : (k + 1) * LANES]
        copy = remote(part.at[pl.ds(start_of(b, (1 - core, half)), half)], in_core.at[b], core_sem.at[b, 0], core_sem.at[b, 1], pair)
        copy.start()
        core_out[b].append(copy)

    for b in every:
        core_out[b][0].wait_recv()
        part[pl.ds(start_of(b, (core, half)), half), :] += in_core[b]
        for j in range(1, plane_n):
            to = (spot + j) % plane_n
            copy = remote(
                part.at[pl.ds(start_of(b, (core, half), (to, size)), size)], in_plane.at[b, j - 1],
                plane_send.at[b, j - 1], plane_recv.at[b, j - 1], plane_at(to),
            )
            copy.start()
            plane_out[b].append(copy)
    for b in every:
        base = start_of(b, (core, half), (spot, size))
        total = part[pl.ds(base, size), :]
        for j in range(1, plane_n):
            plane_out[b][j - 1].wait_recv()
            total = total + in_plane[b, j - 1]
        part[pl.ds(base, size), :] = total
        for j in range(1, line_n):
            to = (line + j) % line_n
            start = start_of(b, (core, half), (spot, size), (to, piece)) if scatter else base
            copy = remote(part.at[pl.ds(start, piece)], in_line.at[b, j - 1], line_send.at[b, j - 1], line_recv.at[b, j - 1], line_at(to))
            copy.start()
            line_out[b].append(copy)
    for sends, receives, copy, _ in large:
        pl.when(sends)(copy.start)

    def spread_plane(b):
        view = prior.at[pl.ds(start_of(b, (core, half), (spot, size)), size)]
        for j in range(1, plane_n):
            k = plane_n - 1 + j - 1
            copy = remote(view, view, plane_send.at[b, k], plane_recv.at[b, k], plane_at((spot + j) % plane_n))
            copy.start()
            plane_back[b].append(copy)

    for b in every:
        own = start_of(b, (core, half), (spot, size), (line, piece)) if scatter else start_of(b, (core, half), (spot, size))
        total = part[pl.ds(own, piece), :]
        for j in range(1, line_n):
            line_out[b][j - 1].wait_recv()
            total = total + in_line[b, j - 1]
        prior[pl.ds(own, piece), :] = total
        if scatter:
            view = prior.at[pl.ds(own, piece)]
            for j in range(1, line_n):
                k = line_n - 1 + j - 1
                copy = remote(view, view, line_send.at[b, k], line_recv.at[b, k], line_at((line + j) % line_n))
                copy.start()
                line_back[b].append(copy)
        else:
            spread_plane(b)
    if scatter:
        for b in every:
            for copy in line_back[b]:
                copy.wait_recv()
            spread_plane(b)

    for sends, receives, copy, _ in large:
        pl.when(receives)(copy.wait_recv)
    state[0] += halo_u[...] * (diff_z[0:1, :] + 0.5 * cour_z[0:1, :])
    state[depth - 1] += halo_d[...] * (diff_z[depth - 1 : depth, :] - 0.5 * cour_z[depth - 1 : depth, :])
    keep = pltpu.make_async_copy(state, state_out, state_sem)
    keep.start()

    for b in every:
        for copy in plane_back[b]:
            copy.wait_recv()
        view = prior.at[pl.ds(start_of(b, (core, half)), half)]
        copy = remote(view, view, core_sem.at[b, 2], core_sem.at[b, 3], pair)
        copy.start()
        core_back[b].append(copy)
    for b in every:
        core_back[b][0].wait_recv()
    for group in (core_out, plane_out, line_out, line_back, plane_back, core_back):
        for copies in group:
            for copy in copies:
                copy.wait_send()
    for sends, receives, copy, _ in small + large:
        pl.when(sends)(copy.wait_send)
    keep.wait()


def update_kernel(
    total_cols, width, state_in, prior_in, cell_in, radius_in, value_in, var_in, out,
    layers_ref, later_ref, prior, obs_cell, obs_radius, obs_value, obs_var, load_sem,
):
    loads = []
    for i, (src, dst) in enumerate(
        (
            (cell_in, obs_cell), (radius_in, obs_radius), (value_in, obs_value), (var_in, obs_var),
            (prior_in, prior), (state_in, layers_ref),
        )
    ):
        copy = pltpu.make_async_copy(src, dst, load_sem.at[i])
        copy.start()
        loads.append(copy)
    depth, members, _ = layers_ref.shape
    batches, count = obs_cell.shape
    blocks = count // LANES
    first = lax.axis_index("tile") * width
    for copy in loads[:-1]:
        copy.wait()
    for b in range(batches):
        for k in range(blocks):
            later_ref[b, :, k * LANES : (k + 1) * LANES] = prior[pl.ds((b * blocks + k) * members, members), :]
    centre = split_cell(obs_cell[...], total_cols)[1].astype(jnp.float32)
    inverse = 1.0 / obs_radius[...].astype(jnp.float32)
    upright = jnp.concatenate([centre, inverse], axis=0).T
    grid = (first + lax.broadcasted_iota(jnp.int32, (1, width), 1)).astype(jnp.float32)

    for b in range(batches):
        y = later_ref[b]
        value, variance = obs_value[b : b + 1, :], obs_var[b : b + 1, :]
        ymean = jnp.sum(y, axis=0, keepdims=True) * (1.0 / members)
        anomaly = y - ymean
        spread = jnp.sum(anomaly * anomaly, axis=0, keepdims=True) / (members - 1) + 1e-06
        shrink = variance / (spread + variance)
        postmean = spread * shrink * (ymean / spread + value / variance)
        delta = (postmean - ymean) + (jnp.sqrt(shrink) - 1.0) * anomaly
        delta = delta * (1.0 / ((members - 1) * spread))
        d_high, d_low = halves(delta)
        d_both = jnp.concatenate([d_high, d_low], axis=0)
        y_high = anomaly.astype(jnp.bfloat16).astype(jnp.float32)
        y_low = anomaly - y_high
        lhs = jnp.concatenate([y_high, y_high, y_low, y_low], axis=0).T.astype(jnp.bfloat16)
        here, scale = upright[:, b : b + 1], upright[:, batches + b : batches + b + 1]

        def taper(positions):
            frac = jnp.maximum(1.0 - jnp.abs(positions - here) * scale, 0.0)
            return frac * frac

        def change(x, weight):
            x_high, x_low = halves(x - jnp.sum(x, axis=0, keepdims=True) * (1.0 / members))
            rhs = jnp.concatenate([x_high, x_low, x_high, x_low], axis=0)
            gain = jnp.dot(lhs, rhs, preferred_element_type=jnp.float32) * weight
            g_high, g_low = halves(gain)
            one = jnp.dot(d_both, g_high, preferred_element_type=jnp.float32)
            two = jnp.dot(d_high, g_low, preferred_element_type=jnp.float32)
            return one[:members] + one[members:] + two

        for c in range(b + 1, batches):
            later_ref[c] += change(later_ref[c], taper(centre[c : c + 1, :]))
        weight = taper(grid)
        if b == 0:
            loads[-1].wait()
        for l in range(depth):
            x = layers_ref[l]
            x = x + change(x, weight)
            if b == batches - 1:
                out[:, l, :] = x
            else:
                layers_ref[l] = x


def divide(values, size):
    return values >> (size.bit_length() - 1) if size & (size - 1) == 0 else values // size


def dot_rows(a, b):
    return lax.dot_general(a, b, (((1,), (1,)), ((), ())), preferred_element_type=jnp.float32)


def remote(src, dst, send, recv, device):
    return pltpu.make_async_remote_copy(
        src_ref=src, dst_ref=dst, send_sem=send, recv_sem=recv, device_id=device, device_id_type=MESH
    )


def collect_kernel(
    tiles, layers, cap, cuts, bends, ens_in, dx_in, dz_in, cx_in, cz_in, cell_in, radius_in, value_in, var_in,
    state_out, flat, meta, taper_in, kinks, tapers, table, flag,
    state, state_sem, ens, diff_x, diff_z, cour_x, cour_z, obs_cell, obs_radius, obs_value, obs_var, load_sem,
    cells, edge_w, edge_e, halo_w, halo_e, near_u, near_d, part_u, part_d, halo_u, halo_d,
    gathered, hop_send, hop_recv, line_send, line_recv, plane_send, plane_recv, core_send, core_recv,
):
    loads = []
    for i, (src, dst) in enumerate(
        (
            (cell_in, obs_cell), (ens_in, ens), (dz_in, diff_z), (cz_in, cour_z), (dx_in, diff_x), (cx_in, cour_x),
            (radius_in, obs_radius), (value_in, obs_value), (var_in, obs_var),
        )
    ):
        copy = pltpu.make_async_copy(src, dst, load_sem.at[i])
        copy.start()
        loads.append(copy)
    members, depth, width = ens.shape
    batches, count = obs_cell.shape
    chunks, devices, piece, _ = gathered.shape
    f32, bf16 = jnp.float32, jnp.bfloat16
    tile, layer = lax.axis_index("tile"), lax.axis_index("layer")
    core, row, line = tile % 2, (tile // 2) % 2, tile // 4
    plane_n, line_n = layers * 2, tiles // 4
    spot = layer * 2 + row
    pair = (tile + 1 - 2 * core, layer)

    def plane_at(index):
        return (line * 4 + (index % 2) * 2 + core, index // 2)

    def line_at(index):
        return (index * 4 + row * 2 + core, layer)

    above, below = (tile, lax.rem(layer + layers - 1, layers)), (tile, lax.rem(layer + 1, layers))
    ahead, behind = (lax.rem(tile + 1, tiles), layer), (lax.rem(tile + tiles - 1, tiles), layer)
    greeted = [pair, ahead, behind, below, above]
    greeted += [plane_at((spot + j) % plane_n) for j in range(1, plane_n)]
    greeted += [line_at((line + j) % line_n) for j in range(1, line_n)]
    barrier = pltpu.get_barrier_semaphore()
    for device in greeted:
        pl.semaphore_signal(barrier, inc=1, device_id=device, device_id_type=MESH)

    loads[0].wait()
    cell_row, cell_col = split_cell(obs_cell[...], tiles * width)
    cell_tile, cell_layer = divide(cell_col, width), divide(cell_row, depth)
    local_col, local_row = cell_col - cell_tile * width, cell_row - cell_layer * depth
    here = cell_tile == tile
    up_rim = jnp.logical_and(local_row == 0, cell_layer > 0)
    down_rim = jnp.logical_and(local_row == depth - 1, cell_layer < layers - 1)
    side_rim = jnp.logical_or(local_col == 0, local_col == width - 1)
    rim = jnp.where(jnp.logical_or(side_rim, jnp.logical_or(up_rim, down_rim)), 1.0, 0.0)
    groups = [
        jnp.where(jnp.logical_and(here, cell_layer == layer + step), share, 0.0)
        for step, share in ((0, 1.0 - rim), (0, rim), (-1, rim), (1, rim))
    ]
    masks = jnp.concatenate(groups, axis=0).astype(bf16)
    first = lax.broadcasted_iota(jnp.int32, (count, count), 0)
    second = lax.broadcasted_iota(jnp.int32, (count, count), 1)
    running = jnp.dot(masks, jnp.where(first <= second, 1.0, 0.0).astype(bf16), preferred_element_type=f32)
    code = (local_row * width + local_col + 1).astype(f32)
    late = 2 * piece
    ranks, sums = [], []
    for k in range(4):
        total = jnp.zeros((1, 1), f32)
        rows = []
        for b in range(batches):
            i = k * batches + b
            rows.append(running[i : i + 1, :] + (total - 1.0))
            total = total + running[i : i + 1, count - 1 : count]
        ranks.append(rows)
        sums.append(total)

    def locate(size, slots_of):
        slot = lax.broadcasted_iota(jnp.int32, (size, count), 0).astype(f32)
        lanes = lax.broadcasted_iota(jnp.int32, (size, width), 1)
        total = jnp.zeros((size, count), f32)
        for b in range(batches):
            total = total + jnp.where(slots_of(b) == slot, code[b : b + 1, :], 0.0)
        cell = jnp.sum(total, axis=1, keepdims=True).astype(jnp.int32) - 1
        at_row = divide(cell, width)
        at_col = jnp.where(cell >= 0, cell - at_row * width, -1)
        return at_row, at_col, jnp.where(lanes == at_col, 1.0, 0.0)

    def facing(k, edge):
        def slots_of(b):
            wanted = jnp.logical_and(groups[k][b : b + 1, :] > 0.5, local_row[b : b + 1, :] == edge)
            return jnp.where(wanted, ranks[k][b] + (late - sums[k]), -1.0)

        return locate(late, slots_of)[2]

    def own(b):
        rim_slot = jnp.where(groups[1][b : b + 1, :] > 0.5, ranks[1][b] + (cap - sums[1]), -1.0)
        return jnp.where(groups[0][b : b + 1, :] > 0.5, ranks[0][b], rim_slot)

    low = lax.broadcasted_iota(jnp.int32, (piece, LANES), 1) < members

    def packed(values):
        out = []
        for k in range(values.shape[0] // late):
            base = 2 * piece * k
            out.append(jnp.where(low, values[base : base + piece], values[base + piece : base + 2 * piece]))
        return out

    def doubled(values):
        return values + pltpu.roll(values, members, 1)

    for copy in loads[1:6]:
        copy.wait()
    lane = lax.broadcasted_iota(jnp.int32, (members, LANES), 1)
    west = jnp.zeros((members, LANES), f32)
    east = jnp.zeros((members, LANES), f32)
    for l in range(depth):
        x = ens[:, l, :]
        cells[l] = x
        west = jnp.where(lane == l, x[:, 0:1], west)
        east = jnp.where(lane == l, x[:, width - 1 : width], east)
    edge_w[...] = jnp.concatenate([west, west], axis=0).T[:8]
    edge_e[...] = jnp.concatenate([east, east], axis=0).T[:8]
    for there, ref, k, edge, l in (
        (layer > 0, part_u, 2, depth - 1, 0), (layer < layers - 1, part_d, 3, 0, depth - 1)
    ):

        @pl.when(there)
        def _(ref=ref, k=k, edge=edge, l=l):
            raw = jnp.concatenate(halves(cells[l]), axis=0)
            ref[...] = packed(doubled(dot_rows(facing(k, edge).astype(bf16), raw)))[0]

    pl.semaphore_wait(barrier, len(greeted))

    up, down = layer > 0, layer < layers - 1
    before, after = tile > 0, tile < tiles - 1

    def move(i, sends, receives, src, dst, device):
        return sends, receives, remote(src, dst, hop_send.at[i], hop_recv.at[i], device), dst

    small = (
        move(0, down, up, part_d, near_u, below),
        move(1, up, down, part_u, near_d, above),
        move(2, after, before, edge_e, halo_w, ahead),
        move(3, before, after, edge_w, halo_e, behind),
    )
    large = (
        move(4, down, up, cells.at[depth - 1], halo_u, below),
        move(5, up, down, cells.at[0], halo_d, above),
    )
    for sends, receives, copy, place in small:
        pl.when(sends)(copy.start)
    for sends, receives, copy, _ in large:
        pl.when(sends)(copy.start)
    for sends, receives, copy, place in small + large:

        @pl.when(jnp.logical_not(receives))
        def _(place=place):
            place[...] = jnp.zeros_like(place)

    at_row, at_col, hot = locate(cap, own)
    column = lax.broadcasted_iota(jnp.int32, (members, width), 1)
    total = jnp.zeros((cap, LANES), f32)
    for l in range(depth):
        x = cells[l]
        left = jnp.where(column == 0, 0.0, pltpu.roll(x, 1, 1))
        right = jnp.where(column == width - 1, 0.0, pltpu.roll(x, width - 1, 1))
        dx, dz = diff_x[l : l + 1, :], diff_z[l : l + 1, :]
        cx, cz = 0.5 * cour_x[l : l + 1, :], 0.5 * cour_z[l : l + 1, :]
        new = x * (1.0 - 2.0 * dz - 2.0 * dx) + left * (dx + cx) + right * (dx - cx)
        if l > 0:
            new = new + cells[l - 1] * (dz + cz)
        if l < depth - 1:
            new = new + cells[l + 1] * (dz - cz)
        state[l] = new
        picked = dot_rows(hot.astype(bf16), jnp.concatenate(halves(new), axis=0))
        total = total + jnp.where(at_row == l, picked, 0.0)
    mine = packed(doubled(total))
    me = (core * plane_n + spot) * line_n + line
    line_out, plane_out, core_out = ([[] for _ in range(chunks)] for _ in range(3))

    def send_line(k, value):
        gathered[k, me] = value
        view = gathered.at[k, me]
        for j in range(1, line_n):
            copy = remote(view, view, line_send.at[k, j - 1], line_recv.at[k, j - 1], line_at((line + j) % line_n))
            copy.start()
            line_out[k].append(copy)

    for k in range(chunks - 1):
        send_line(k, mine[k])
    coef_u = diff_z[0:1, :] + 0.5 * cour_z[0:1, :]
    coef_d = diff_z[depth - 1 : depth, :] - 0.5 * cour_z[depth - 1 : depth, :]
    coef_w = diff_x[:, 0:1] + 0.5 * cour_x[:, 0:1]
    coef_e = diff_x[:, width - 1 : width] - 0.5 * cour_x[:, width - 1 : width]
    at_row, at_col, hot = at_row[cap - late :], at_col[cap - late :], hot[cap - late :]
    take_u = jnp.where(at_row == 0, jnp.sum(hot * coef_u, axis=1, keepdims=True), 0.0)
    take_d = jnp.where(at_row == depth - 1, jnp.sum(hot * coef_d, axis=1, keepdims=True), 0.0)

    def spread_out(take):
        return packed(jnp.broadcast_to(take, (late, LANES)))[0]

    takes = [spread_out(take_u), spread_out(take_d)]
    sides = []
    for at, coef in ((0, coef_w), (width - 1, coef_e)):
        for l in range(depth):
            sides.append(spread_out(jnp.where(jnp.logical_and(at_row == l, at_col == at), coef[l : l + 1, :], 0.0)))

    for sends, receives, copy, place in small:
        pl.when(receives)(copy.wait_recv)
    value = mine[chunks - 1] + takes[0] * near_u[...] + takes[1] * near_d[...]
    for l in range(depth):
        value = value + sides[l] * halo_w[l : l + 1, :] + sides[depth + l] * halo_e[l : l + 1, :]
    send_line(chunks - 1, value)

    for ref, coef, at in ((halo_w, coef_w, 0), (halo_e, coef_e, width - 1)):
        base = at // LANES * LANES
        block = lax.broadcasted_iota(jnp.int32, (members, LANES), 1)
        turned = jnp.concatenate([ref[...]] * (LANES // 8), axis=0).T[:members]
        for l in range(depth):
            term = turned[:, l : l + 1] * coef[l : l + 1, :]
            state[l, :, base : base + LANES] += jnp.where(block == at - base, term, 0.0)

    for copy in loads[6:]:
        copy.wait()
    core_of, row_of, line_of = cell_tile & 1, divide(cell_tile, 2) & 1, divide(cell_tile, 4)
    owner = (core_of * plane_n + cell_layer * 2 + row_of) * line_n + line_of
    owner = owner * 2 + rim.astype(jnp.int32)
    key = (owner * count + lax.broadcasted_iota(jnp.int32, (batches, count), 1)).astype(f32)
    upright = jnp.concatenate([key, jnp.zeros_like(key)], axis=0).T

    def pieces(values, n):
        out = []
        for _ in range(n):
            high = values.astype(bf16).astype(f32)
            out.append(high)
            values = values - high
        return out

    fields = (
        (cell_col.astype(f32), 2), (obs_radius[...].astype(f32), 2), (obs_value[...], 3), (obs_var[...], 3)
    )
    parts = []
    for values, n in fields:
        parts.extend(pieces(values, n))
    holders = 2 * devices
    devices_at = lax.broadcasted_iota(jnp.int32, (holders, count), 0)
    cuts_at = lax.broadcasted_iota(jnp.int32, (tiles * cuts, count), 0)
    ends = [divide(cell_col + obs_radius[...] * step, width // cuts) for step in (-1, 0, 1)]
    used = jnp.zeros((holders, 1), f32)
    begins, starts = [], []
    worst = jnp.zeros((tiles * cuts, 1), f32)
    longest = jnp.zeros((holders, 1), f32)
    if len(parts) * batches % 16:
        parts.append(jnp.zeros((16 - len(parts) * batches % 16, count), f32))
    parts = jnp.concatenate(parts, axis=0).astype(bf16)
    place = first.astype(f32)
    for b in range(batches):
        less = jnp.where(upright[:, b : b + 1] < key[b : b + 1, :], 1.0, 0.0)
        position = jnp.sum(less, axis=0, keepdims=True)
        order = jnp.where(place == position, 1.0, 0.0).astype(bf16)
        ordered = dot_rows(parts, order)
        i = 0
        for f, (_, n) in enumerate(fields):
            total = ordered[i * batches + b : i * batches + b + 1, :]
            for p in range(1, n):
                total = total + ordered[(i + p) * batches + b : (i + p) * batches + b + 1, :]
            meta[f * batches + b : f * batches + b + 1, :] = total
            i += n
        holder = owner[b : b + 1, :]
        length = jnp.sum(jnp.where(holder == devices_at, 1.0, 0.0), axis=1, keepdims=True)
        start = jnp.sum(jnp.where(holder < devices_at, 1.0, 0.0), axis=1, keepdims=True)
        starts.append(start)
        begins.append(used)
        used = used + length
        longest = jnp.maximum(longest, length)
        bent = jnp.zeros((tiles * cuts, count), f32)
        for end in ends:
            bent = bent + jnp.where(end[b : b + 1, :] == cuts_at, 1.0, 0.0)
        worst = jnp.maximum(worst, jnp.sum(bent, axis=1, keepdims=True))
    odd = lax.broadcasted_iota(jnp.int32, (holders, 1), 0) % 2
    end = jnp.where(odd == 1, cap - used, 0.0)
    entries = starts + [begin + end for begin in begins]
    for i in range(2):
        most = jnp.max(jnp.where(odd == i, longest, 0.0), axis=0, keepdims=True)
        entries.append(jnp.broadcast_to(most, (holders, 1)))
    entry_lane = lax.broadcasted_iota(jnp.int32, (holders, LANES), 1)
    listed = jnp.zeros((holders, LANES), f32)
    for i, entry in enumerate(entries):
        listed = jnp.where(entry_lane == i, entry, listed)
    if holders % LANES:
        listed = jnp.concatenate([listed, jnp.zeros((-holders % LANES, LANES), f32)], axis=0)
    table[...] = listed.T[: table.shape[0]].astype(jnp.int32)
    inner = jnp.broadcast_to(jnp.where(odd == 0, used, 0.0), (holders, LANES))
    pair_of = jnp.broadcast_to(used, (holders, LANES))
    room = jnp.where(odd == 1, pltpu.roll(inner, 1, 0) + pair_of, 0.0)
    rim_most = jnp.max(jnp.where(odd == 1, used, 0.0))
    over = jnp.logical_or(jnp.max(room) > cap, jnp.logical_or(rim_most > late, jnp.max(worst) > bends))
    flag[0] = over.astype(jnp.int32)

    def send_plane(k):
        for copy in line_out[k]:
            copy.wait_recv()
        view = gathered.at[k, pl.ds((core * plane_n + spot) * line_n, line_n)]
        for j in range(1, plane_n):
            copy = remote(view, view, plane_send.at[k, j - 1], plane_recv.at[k, j - 1], plane_at((spot + j) % plane_n))
            copy.start()
            plane_out[k].append(copy)

    for k in range(chunks - 1):
        send_plane(k)

    part_w = width // cuts
    middle = (part_w - 1) / 2
    centre, radius = meta[0:batches, :], meta[batches : 2 * batches, :]
    inverse = 1.0 / radius
    near, far = centre - radius, centre + radius
    bent = []
    for c in range(cuts):
        lowest = (tile * width + c * part_w).astype(f32)
        highest = lowest + (part_w - 1)
        right_of, left_of = centre <= lowest, centre >= highest
        smooth = jnp.logical_or(
            jnp.logical_and(right_of, far >= highest), jnp.logical_and(left_of, near <= lowest)
        )
        away = jnp.logical_or(jnp.logical_and(right_of, far <= lowest), jnp.logical_and(left_of, near >= highest))
        bent.append(jnp.where(jnp.logical_or(smooth, away), 0.0, 1.0))
        value = jnp.where(smooth, 1.0 - jnp.abs(lowest + middle - centre) * inverse, 0.0)
        slope = jnp.where(smooth, jnp.where(right_of, -middle, middle) * inverse, 0.0)
        for i, rows in enumerate((value * value, 2.0 * value * slope, slope * slope)):
            start = (c * 4 + i) * batches
            taper_in[start : start + batches, :] = rows
    padded = jnp.concatenate(bent + [jnp.zeros_like(centre)] * (-cuts % (16 // batches)), axis=0).astype(bf16)
    counted = jnp.dot(padded, jnp.where(first <= second, 1.0, 0.0).astype(bf16), preferred_element_type=f32)
    ranks = []
    for c in range(cuts):
        ranks.append(jnp.where(bent[c] > 0.5, counted[c * batches : (c + 1) * batches] - 1.0, -1.0))
        taper_in[(c * 4 + 3) * batches : (c * 4 + 4) * batches, :] = ranks[c]
    parts = pieces(centre, 2) + pieces(inverse, 3)
    parts = jnp.concatenate(parts + [jnp.zeros_like(centre)] * (-len(parts) % (16 // batches)), axis=0).astype(bf16)
    kink_row = lax.broadcasted_iota(jnp.int32, (bends, count), 0).astype(f32)
    grid = (tile * width + lax.broadcasted_iota(jnp.int32, (1, width), 1)).astype(f32)

    def bump(positions, here, scale):
        frac = jnp.maximum(1.0 - jnp.abs(positions - here) * scale, 0.0)
        return frac * frac

    for b in range(batches):
        choose = [jnp.where(kink_row == ranks[c][b : b + 1, :], 1.0, 0.0).astype(bf16) for c in range(cuts)]
        ordered = dot_rows(jnp.concatenate(choose, axis=0), parts)
        at = [ordered[:, p * batches + b : p * batches + b + 1] for p in range(5)]
        kink_c, kink_i = at[0] + at[1], at[2] + at[3] + at[4]
        for c in range(cuts):
            rows = slice(c * bends, (c + 1) * bends)
            kinks[b, c] = bump(grid[:, c * part_w : (c + 1) * part_w], kink_c[rows], kink_i[rows])
    upright = jnp.concatenate([centre, inverse], axis=0).T
    i = 0
    for b in range(batches):
        for c in range(b + 1, batches):
            tapers[i] = bump(centre[c : c + 1, :], upright[:, b : b + 1], upright[:, batches + b : batches + b + 1])
            i += 1

    send_plane(chunks - 1)
    for sends, receives, copy, _ in large:
        pl.when(receives)(copy.wait_recv)
    state[0] += halo_u[...] * coef_u
    state[depth - 1] += halo_d[...] * coef_d
    keep = pltpu.make_async_copy(state, state_out, state_sem)
    keep.start()

    def unpack(k, side):
        for i in range(devices // 2):
            g = side * (devices // 2) + i
            rows = gathered[k, g]
            at = pl.multiple_of(g * cap + 2 * piece * k, 8)
            flat[pl.ds(at, piece), :] = rows
            flat[pl.ds(at + piece, piece), :] = pltpu.roll(rows, members, 1)

    for k in range(chunks):
        for copy in plane_out[k]:
            copy.wait_recv()
        view = gathered.at[k, pl.ds(core * plane_n * line_n, plane_n * line_n)]
        copy = remote(view, view, core_send.at[k], core_recv.at[k], pair)
        copy.start()
        core_out[k].append(copy)
        unpack(k, core)
    for k in range(chunks):
        core_out[k][0].wait_recv()
        unpack(k, 1 - core)
    for group in (line_out, plane_out, core_out):
        for copies in group:
            for copy in copies:
                copy.wait_send()
    for sends, receives, copy, _ in small + large:
        pl.when(sends)(copy.wait_send)
    keep.wait()


def apply_kernel(
    cap, devices, table, state_in, flat, meta, taper_in, kinks, tapers, out, layers_ref, later_ref, ordered, load_sem,
):
    load = pltpu.make_async_copy(state_in, layers_ref, load_sem)
    load.start()
    depth, members, _ = layers_ref.shape
    batches, _, count = later_ref.shape
    mean = count / devices
    run = min(cap, -int(-(mean + 4.0 * mean**0.5) // 8) * 8)
    short = max(8, run // 16 * 8)

    def spread(sizes):
        def step(g, carry):
            for b in range(batches):
                for i in range(2):
                    dst, src = table[b, 2 * g + i], g * cap + table[batches + b, 2 * g + i]
                    for at in range(0, sizes[i], 8):
                        ordered[b, pl.ds(dst + at, 8), :] = flat[pl.ds(src + at, 8), :]
            return carry

        return step

    lax.fori_loop(0, devices, spread((run, short)), 0, unroll=4)

    @pl.when(jnp.logical_or(table[2 * batches, 0] > run, table[2 * batches + 1, 0] > short))
    def _():
        lax.fori_loop(0, devices, spread((cap, cap)), 0)

    for b in range(batches):
        later_ref[b] = ordered[b, :count, :].T[:members]
    _, cuts, bends, part_w = kinks.shape
    middle = (part_w - 1) / 2
    offset = lax.broadcasted_iota(jnp.int32, (1, part_w), 1).astype(jnp.float32)
    ratio = (offset - middle) * (1.0 / middle)
    ratio = jnp.concatenate([ratio] * depth, axis=1)
    third = 3 * members
    both_low = lax.broadcasted_iota(jnp.int32, (third, LANES), 1) < members
    low = lax.broadcasted_iota(jnp.int32, (2 * members, LANES), 1) < members
    top = lax.broadcasted_iota(jnp.int32, (2 * members, LANES), 0) < members
    kink_row = lax.broadcasted_iota(jnp.int32, (bends, count), 0).astype(jnp.float32)
    pair = 0

    for b in range(batches):
        y = later_ref[b]
        value, variance = meta[2 * batches + b : 2 * batches + b + 1, :], meta[3 * batches + b : 3 * batches + b + 1, :]
        ymean = jnp.sum(y, axis=0, keepdims=True) * (1.0 / members)
        anomaly = y - ymean
        spread = jnp.sum(anomaly * anomaly, axis=0, keepdims=True) / (members - 1) + 1e-06
        shrink = variance / (spread + variance)
        postmean = spread * shrink * (ymean / spread + value / variance)
        delta = (postmean - ymean) + (jnp.sqrt(shrink) - 1.0) * anomaly
        delta = delta * (1.0 / ((members - 1) * spread))
        d_high, d_low = halves(delta)
        d_both = jnp.concatenate([d_high, d_low], axis=0)
        y_high = anomaly.astype(jnp.bfloat16).astype(jnp.float32)
        y_low = anomaly - y_high
        y_both = jnp.concatenate([y_high, y_low], axis=0).astype(jnp.bfloat16)

        def stack(x):
            x_high, x_low = halves(x - jnp.sum(x, axis=0, keepdims=True) * (1.0 / members))
            return jnp.concatenate([x_high, x_high, x_low, x_low], axis=0)

        def twice(x):
            return jnp.concatenate([x, x], axis=1).astype(jnp.bfloat16)

        if b < batches - 1:
            lhs = twice(jnp.concatenate([y_high, y_low], axis=0).T)
        scaled = []
        for c in range(cuts):
            for i in range(3):
                row = (c * 4 + i) * batches + b
                scaled.append(delta * taper_in[row : row + 1, :])
        moments = dot_rows(jnp.concatenate(halves(jnp.concatenate(scaled, axis=0)), axis=0), y_both)
        choose = []
        for c in range(cuts):
            row = (c * 4 + 3) * batches + b
            choose.append(jnp.where(kink_row == taper_in[row : row + 1, :], 1.0, 0.0).astype(jnp.bfloat16))
        choose = jnp.concatenate(choose, axis=0)
        y_kink = dot_rows(choose, y_both)
        d_kink = dot_rows(d_both, choose)
        turned = pltpu.roll(d_kink, members, 1)
        lefts, rights = [], []
        if b == 0:
            load.wait()
        for c in range(cuts):
            moment = moments[c * third : (c + 1) * third] + moments[(cuts + c) * third : (cuts + c + 1) * third]
            m_high, m_low = halves(moment + pltpu.roll(moment, members, 1))
            moment = jnp.where(both_low, m_high.astype(jnp.float32), m_low.astype(jnp.float32))
            left = twice(jnp.concatenate([moment, y_kink[c * bends : (c + 1) * bends]], axis=0))
            if cuts == 1:
                right = jnp.concatenate([d_kink, jnp.where(top, d_kink, 0.0)], axis=1)
            elif c == 0:
                right = jnp.where(low, d_kink, jnp.where(top, turned, 0.0))
            else:
                right = jnp.where(low, turned, jnp.where(top, d_kink, 0.0))
            right = right.astype(jnp.bfloat16)
            lefts.append(left)
            rights.append(right)
        rest = range(b + 1, batches)
        crosses = [jnp.dot(lhs, stack(later_ref[c]), preferred_element_type=jnp.float32) for c in rest]
        splits = [halves(cross * tapers[pair + i]) for i, cross in enumerate(crosses)]
        pair += len(rest)
        ones = [jnp.dot(d_both, high, preferred_element_type=jnp.float32) for high, _ in splits]
        twos = [jnp.dot(d_high, lower, preferred_element_type=jnp.float32) for _, lower in splits]
        for i, c in enumerate(rest):
            later_ref[c] += ones[i][:members] + ones[i][members:] + twos[i]

        olds, firsts, gains, seconds = [], [], [], []
        for c in range(cuts):
            columns = slice(c * part_w, (c + 1) * part_w)
            olds.append(jnp.concatenate([layers_ref[l, :, columns] for l in range(depth)], axis=1))
            firsts.append(jnp.dot(lefts[c], stack(olds[c]), preferred_element_type=jnp.float32))
        for c in range(cuts):
            weight = jnp.concatenate([kinks[b, c]] * depth, axis=1)
            gains.append(jnp.concatenate(halves(firsts[c][third:] * weight), axis=0))
        for c in range(cuts):
            seconds.append(jnp.dot(rights[c], gains[c], preferred_element_type=jnp.float32))
        for c in range(cuts):
            both, more = firsts[c], seconds[c]
            x = olds[c] + (both[:members] + ratio * (both[members : 2 * members] + ratio * both[2 * members : third]))
            x = x + (more[:members] + more[members:])
            columns = slice(c * part_w, (c + 1) * part_w)
            for l in range(depth):
                if b == batches - 1:
                    out[:, l, columns] = x[:, l * part_w : (l + 1) * part_w]
                else:
                    layers_ref[l, :, columns] = x[:, l * part_w : (l + 1) * part_w]


def slow_shards(ensemble, diff_x, diff_z, cour_x, cour_z, obs_cell, obs_radius, obs_value, obs_var):
    members, depth, width = ensemble.shape
    batches, count = obs_cell.shape
    tiles, layers = lax.axis_size("tile"), lax.axis_size("layer")
    rows = batches * count * members // LANES
    plane_n, line_n = layers * 2, tiles // 4
    half = rows // batches // 2
    size = half // plane_n
    piece = size // line_n if size % (8 * line_n) == 0 else size
    vmem = pl.BlockSpec(memory_space=pltpu.VMEM)
    hbm = pl.BlockSpec(memory_space=pltpu.HBM)
    f32 = jnp.float32
    dma = pltpu.SemaphoreType.DMA
    state, prior = pl.pallas_call(
        functools.partial(gather_kernel, tiles, layers),
        out_shape=(jax.ShapeDtypeStruct((depth, members, width), f32), jax.ShapeDtypeStruct((rows, LANES), f32)),
        in_specs=[hbm] * 6,
        out_specs=(hbm, vmem),
        scratch_shapes=[
            pltpu.VMEM((depth, members, width), f32),
            dma,
            pltpu.VMEM((members, depth, width), f32),
            *[pltpu.VMEM((depth, width), f32)] * 4,
            pltpu.VMEM((batches, count), jnp.int32),
            dma((6,)),
            pltpu.VMEM((depth, members, width), f32),
            *[pltpu.VMEM((members, LANES), f32)] * 4,
            *[pltpu.VMEM((members, width), f32)] * 2,
            *[pltpu.VMEM((8, width), f32)] * 4,
            pltpu.VMEM((rows, LANES), f32),
            pltpu.VMEM((batches, half, LANES), f32),
            pltpu.VMEM((batches, plane_n - 1, size, LANES), f32),
            pltpu.VMEM((batches, line_n - 1, piece, LANES), f32),
            dma((6,)),
            dma((6,)),
            dma((batches, 4)),
            dma((batches, 2 * plane_n - 2)),
            dma((batches, 2 * plane_n - 2)),
            dma((batches, 2 * line_n - 2)),
            dma((batches, 2 * line_n - 2)),
        ],
        compiler_params=pltpu.CompilerParams(collective_id=0, has_side_effects=True, vmem_limit_bytes=63 * 2**20),
        name="gather_prior",
    )(ensemble, diff_x, diff_z, cour_x, cour_z, obs_cell)
    return pl.pallas_call(
        functools.partial(update_kernel, tiles * width, width),
        out_shape=jax.ShapeDtypeStruct((members, depth, width), f32),
        in_specs=[hbm] * 6,
        out_specs=vmem,
        scratch_shapes=[
            pltpu.VMEM((depth, members, width), f32),
            pltpu.VMEM((batches, members, count), f32),
            pltpu.VMEM((rows, LANES), f32),
            *[pltpu.VMEM((batches, count), jnp.int32)] * 2,
            *[pltpu.VMEM((batches, count), f32)] * 2,
            dma((6,)),
        ],
        compiler_params=pltpu.CompilerParams(vmem_limit_bytes=63 * 2**20),
        name="update",
    )(state, prior, obs_cell, obs_radius, obs_value, obs_var)


def shards(ensemble, diff_x, diff_z, cour_x, cour_z, obs_cell, obs_radius, obs_value, obs_var):
    members, depth, width = ensemble.shape
    batches, count = obs_cell.shape
    tiles, layers = lax.axis_size("tile"), lax.axis_size("layer")
    devices = tiles * layers
    plane_n, line_n = layers * 2, tiles // 4
    mean = batches * count / devices
    cap = -int(-(mean + 4.0 * mean**0.5) // 16) * 16
    piece = 16 if cap % 32 == 0 else 8
    chunks = cap // (2 * piece)
    cuts, bends = 1, LANES
    vmem = pl.BlockSpec(memory_space=pltpu.VMEM)
    smem = pl.BlockSpec(memory_space=pltpu.SMEM)
    hbm = pl.BlockSpec(memory_space=pltpu.HBM)
    f32 = jnp.float32
    dma = pltpu.SemaphoreType.DMA
    state, flat, meta, taper_in, kinks, tapers, table, flag = pl.pallas_call(
        functools.partial(collect_kernel, tiles, layers, cap, cuts, bends),
        out_shape=(
            jax.ShapeDtypeStruct((depth, members, width), f32),
            jax.ShapeDtypeStruct((devices * cap + cap, LANES), f32),
            jax.ShapeDtypeStruct((4 * batches, count), f32),
            jax.ShapeDtypeStruct((cuts * 4 * batches, count), f32),
            jax.ShapeDtypeStruct((batches, cuts, bends, width // cuts), f32),
            jax.ShapeDtypeStruct((batches * (batches - 1) // 2, count, count), f32),
            jax.ShapeDtypeStruct((-(-(2 * batches + 2) // 8) * 8, -(-2 * devices // LANES) * LANES), jnp.int32),
            jax.ShapeDtypeStruct((1,), jnp.int32),
        ),
        in_specs=[hbm] * 9,
        out_specs=(hbm, vmem, vmem, vmem, vmem, vmem, vmem, smem),
        scratch_shapes=[
            pltpu.VMEM((depth, members, width), f32),
            dma,
            pltpu.VMEM((members, depth, width), f32),
            *[pltpu.VMEM((depth, width), f32)] * 4,
            *[pltpu.VMEM((batches, count), jnp.int32)] * 2,
            *[pltpu.VMEM((batches, count), f32)] * 2,
            dma((9,)),
            pltpu.VMEM((depth, members, width), f32),
            *[pltpu.VMEM((8, LANES), f32)] * 4,
            *[pltpu.VMEM((piece, LANES), f32)] * 4,
            *[pltpu.VMEM((members, width), f32)] * 2,
            pltpu.VMEM((chunks, devices, piece, LANES), f32),
            dma((6,)),
            dma((6,)),
            *[dma((chunks, max(line_n - 1, 1)))] * 2,
            *[dma((chunks, plane_n - 1))] * 2,
            *[dma((chunks,))] * 2,
        ],
        compiler_params=pltpu.CompilerParams(collective_id=1, has_side_effects=True, vmem_limit_bytes=48 * 2**20),
        name="collect",
    )(ensemble, diff_x, diff_z, cour_x, cour_z, obs_cell, obs_radius, obs_value, obs_var)

    def fast():
        return pl.pallas_call(
            functools.partial(apply_kernel, cap, devices),
            out_shape=jax.ShapeDtypeStruct((members, depth, width), f32),
            in_specs=[smem, hbm, vmem, vmem, vmem, vmem, vmem],
            out_specs=vmem,
            scratch_shapes=[
                pltpu.VMEM((depth, members, width), f32),
                pltpu.VMEM((batches, members, count), f32),
                pltpu.VMEM((batches, count + cap, LANES), f32),
                dma,
            ],
            compiler_params=pltpu.CompilerParams(vmem_limit_bytes=48 * 2**20),
            name="apply",
        )(table, state, flat, meta, taper_in, kinks, tapers)

    def slow():
        return slow_shards(ensemble, diff_x, diff_z, cour_x, cour_z, obs_cell, obs_radius, obs_value, obs_var)

    return lax.cond(flag[0] > 0, slow, fast)


def solution(mesh):
    in_specs = (
        P(None, "layer", "tile"),
        P("layer", "tile"),
        P("layer", "tile"),
        P("layer", "tile"),
        P("layer", "tile"),
        P(),
        P(),
        P(),
        P(),
    )
    out_specs = P(None, "layer", "tile")
    return jax.shard_map(shards, mesh=mesh, in_specs=in_specs, out_specs=out_specs, check_vma=False)
```
